32 devices in a mesh: wide: 16 (over z, y, core), narrow: 2 (over x).
Axes of the slice: x: 2, y: 2, z: 4, core: 2. Of those that a mesh axis runs over, the one named last changes fastest.
Arguments:
- signal_samples: float32 [512, 512], P(('wide', 'narrow')), may hold values from -9 to 9
- present_mask: int32 [512, 512], P(('wide', 'narrow')), may hold values 0 or 1
- embedder_inner_matrix: bfloat16 [32, 1536], replicated, may hold values from -1 to 1
- embedder_inner_offset: float32 [1536], replicated, may hold values from -3 to 3
- embedder_final_matrix: bfloat16 [1536, 384], replicated, may hold values from -0.15625 to 0.15625
- embedder_shortcut_matrix: bfloat16 [32, 384], replicated, may hold values from -1 to 1
- embedder_final_offset: float32 [384], replicated, may hold values from -3 to 3
- mixer_prescale_factor: float32 [384], replicated, may hold values from 0.1 to 1.9
- probe_matrix: bfloat16 [384, 512], replicated, may hold values from -0.3125 to 0.3125
- address_matrix: bfloat16 [384, 512], replicated, may hold values from -0.3125 to 0.3125
- content_matrix: bfloat16 [384, 512], replicated, may hold values from -0.3125 to 0.3125
- mixer_merge_matrix: bfloat16 [512, 384], replicated, may hold values from -0.75 to 0.75
- perceptron_prescale_factor: float32 [384], replicated, may hold values from 0.1 to 1.9
- expand_matrix: bfloat16 [384, 1536], replicated, may hold values from -0.3125 to 0.3125
- contract_matrix: bfloat16 [1536, 384], replicated, may hold values from -0.15625 to 0.15625
- readout_inner_matrix: bfloat16 [384, 1536], replicated, may hold values from -0.3125 to 0.3125
- readout_inner_offset: float32 [1536], replicated, may hold values from -3 to 3
- readout_horizon_matrix: bfloat16 [1536, 576], P(None, 'narrow'), may hold values from -0.15625 to 0.15625
- readout_shortcut_matrix: bfloat16 [384, 576], P(None, 'narrow'), may hold values from -0.3125 to 0.3125
- readout_offset: bfloat16 [576], P('narrow'), may hold values from -3 to 3
- prediction_cotangent: float32 [16384, 576], P('wide', 'narrow'), may hold values from -6 to 6
Outputs:
- prediction_native: float32 [16384, 576], P('wide', 'narrow')
- series_grad: float32 [512, 512], P(('wide', 'narrow'))
- grad_tok_in_w: float32 [32, 1536], replicated
- grad_tok_in_b: float32 [1536], replicated
- grad_tok_out_w: float32 [1536, 384], replicated
- grad_tok_skip_w: float32 [32, 384], replicated
- grad_tok_out_b: float32 [384], replicated
- grad_norm1_gain: float32 [384], replicated
- grad_w_query: float32 [384, 512], replicated
- grad_w_key: float32 [384, 512], replicated
- grad_w_value: float32 [384, 512], replicated
- grad_w_out: float32 [512, 384], replicated
- grad_norm2_gain: float32 [384], replicated
- grad_w_up: float32 [384, 1536], replicated
- grad_w_down: float32 [1536, 384], replicated
- grad_head_in_w: float32 [384, 1536], replicated
- grad_head_in_b: float32 [1536], replicated
- grad_head_out_w: float32 [1536, 576], P(None, 'narrow')
- grad_head_skip_w: float32 [384, 576], P(None, 'narrow')
- grad_head_out_b: float32 [576], P('narrow')
The draws below stay inside these ranges and needn't reach their ends.
All inputs are finite; a program needn't handle non-finite values. No bound on the sum of `present_mask` on one device may be relied on, other than what follows from the above.
Results may differ from the reference program's by a relative error of at most 0.017.
Values may be sent and summed in bfloat16 or wider, within the bound.
No kernel may reach another device: no remote copies, remote signals or barrier semaphores. Data moves between devices by JAX's collectives and lax.ppermute only.
A program may use at most 192 MiB of HBM per device.

```python
import jax
import jax.numpy as jnp
from jax import lax

EMBED_DIMENSION = 384
INNER_WIDTH = 1536
HEADS = 8
HEAD_DIM = 64
PATCH = 16
SAMPLE_LENGTH = 512
SER_DEV = 16
SEGMENT_COUNT = 32
HORIZON_ENTRIES = 576
SERIES = 512
ELEMENT_COUNT = 16384
N_WIDE = 16
N_NARROW = 2


def plant(values, key, low, top_value):
    dims = values.shape
    index_at = [jax.random.randint(jax.random.fold_in(key, axis), (), 0, dims[axis]) for axis in range(len(dims))]
    values = values.at[tuple(index_at)].set(low)
    longest = dims.index(max(dims))
    index_at[longest] = (index_at[longest] + 1) % dims[longest]
    return values.at[tuple(index_at)].set(top_value)


def block_scale(rng, shape, split, low, high):
    factor_of, own = 1.0, jax.random.fold_in(rng, 6)
    for position, parts in split:
        draws = jnp.exp(jax.random.uniform(jax.random.fold_in(own, position), (parts,), jnp.float32, low / len(split), high / len(split)))
        factor_of = factor_of * jnp.repeat(draws, shape[position] // parts).reshape([-1 if axis == position else 1 for axis in range(len(shape))])
    return factor_of


def centred(own_key, extent, scale, reach, shards=(), dtype=jnp.bfloat16):
    values = scale * jax.random.normal(own_key, extent, jnp.float32)
    if shards:
        values = values * block_scale(own_key, extent, shards, -0.22, 0.18)
    return jnp.clip(values, -reach, reach).astype(dtype)


def setup_inputs(seed: int = 0) -> dict:
    seeds = jax.random.split(jax.random.key(seed), 22)
    return {
        "signal_samples": centred(seeds[0], (SERIES, SAMPLE_LENGTH), 1.5, 9.0, ((0, 32),), jnp.float32),
        "present_mask": plant((jax.random.randint(seeds[1], (SERIES, SAMPLE_LENGTH), 0, 8) < 7).astype(jnp.int32), jax.random.fold_in(seeds[1], 1), 0, 1),
        "embedder_inner_matrix": centred(seeds[2], (2 * PATCH, INNER_WIDTH), (2 * PATCH) ** -0.5, 1.0),
        "embedder_inner_offset": centred(seeds[3], (INNER_WIDTH,), 0.5, 3.0, (), jnp.float32),
        "embedder_final_matrix": centred(seeds[4], (INNER_WIDTH, EMBED_DIMENSION), INNER_WIDTH ** -0.5, 0.15625),
        "embedder_shortcut_matrix": centred(seeds[5], (2 * PATCH, EMBED_DIMENSION), (2 * PATCH) ** -0.5, 1.0),
        "embedder_final_offset": centred(seeds[6], (EMBED_DIMENSION,), 0.5, 3.0, (), jnp.float32),
        "mixer_prescale_factor": jnp.clip(1.0 + 0.18 * jax.random.normal(seeds[7], (EMBED_DIMENSION,), jnp.float32), 0.1, 1.9),
        "probe_matrix": centred(seeds[8], (EMBED_DIMENSION, HEADS * HEAD_DIM), EMBED_DIMENSION ** -0.5, 0.3125),
        "address_matrix": centred(seeds[9], (EMBED_DIMENSION, HEADS * HEAD_DIM), EMBED_DIMENSION ** -0.5, 0.3125),
        "content_matrix": centred(seeds[10], (EMBED_DIMENSION, HEADS * HEAD_DIM), EMBED_DIMENSION ** -0.5, 0.3125),
        "mixer_merge_matrix": centred(seeds[11], (HEADS * HEAD_DIM, EMBED_DIMENSION), (HEADS * HEAD_DIM // 8) ** -0.5, 0.75),
        "perceptron_prescale_factor": jnp.clip(1.0 + 0.18 * jax.random.normal(seeds[12], (EMBED_DIMENSION,), jnp.float32), 0.1, 1.9),
        "expand_matrix": centred(seeds[13], (EMBED_DIMENSION, INNER_WIDTH), EMBED_DIMENSION ** -0.5, 0.3125),
        "contract_matrix": centred(seeds[14], (INNER_WIDTH, EMBED_DIMENSION), INNER_WIDTH ** -0.5, 0.15625),
        "readout_inner_matrix": centred(seeds[15], (EMBED_DIMENSION, INNER_WIDTH), EMBED_DIMENSION ** -0.5, 0.3125),
        "readout_inner_offset": centred(seeds[16], (INNER_WIDTH,), 0.5, 3.0, (), jnp.float32),
        "readout_horizon_matrix": centred(seeds[17], (INNER_WIDTH, HORIZON_ENTRIES), INNER_WIDTH ** -0.5, 0.15625, ((1, 2),)),
        "readout_shortcut_matrix": centred(seeds[18], (EMBED_DIMENSION, HORIZON_ENTRIES), EMBED_DIMENSION ** -0.5, 0.3125, ((1, 2),)),
        "readout_offset": centred(seeds[19], (HORIZON_ENTRIES,), 0.5, 3.0, ((0, 2),)),
        "prediction_cotangent": centred(seeds[20], (ELEMENT_COUNT, HORIZON_ENTRIES), 1.0, 6.0, ((0, 16), (1, 2)), jnp.float32),
    }


@jax.custom_vjp
def low(v):
    return lax.optimization_barrier(v.astype(jnp.bfloat16)).astype(jnp.float32)

@jax.custom_vjp
def low_back(v):
    return v

def low_keep(v):
    return (low(v), None)

def low_pass(kept, grad):
    return (grad,)

def back_keep(v):
    return (v, None)

def back_low(kept, grad):
    return (low(grad),)
low.defvjp(low_keep, low_pass)
low_back.defvjp(back_keep, back_low)
epsilon = 1e-06
highest = lax.Precision.HIGHEST

def matmul_result(left, right):
    return jnp.dot(left, right, precision=highest, preferred_element_type=jnp.float32)

def rms_scale(value, gain):
    return value * lax.rsqrt(lax.optimization_barrier(jnp.mean(value * value, axis=-1, keepdims=True)) + epsilon) * gain

def group_forward(signal_samples, observed_float, learnable_tensors):
    embedder_inner_matrix, embedder_inner_offset, embedder_final_matrix, embedder_shortcut_matrix, embedder_final_offset, mixer_prescale_factor, probe_matrix, address_matrix, content_matrix, mixer_merge_matrix, perceptron_prescale_factor, expand_matrix, contract_matrix, readout_inner_matrix, readout_inner_offset, readout_horizon_matrix, readout_shortcut_matrix, readout_offset = learnable_tensors
    first_mask = observed_float[:, :PATCH]
    first = signal_samples[:, :PATCH]
    count = jnp.maximum(lax.optimization_barrier(jnp.sum(first_mask, axis=1, keepdims=True)), 1.0)
    center = lax.optimization_barrier(jnp.sum(first_mask * first, axis=1, keepdims=True)) / count
    spread = lax.optimization_barrier(jnp.sum(first_mask * (first - center) ** 2, axis=1, keepdims=True)) / count
    sigma = jnp.sqrt(jnp.maximum(spread, 1.0))
    scaled = observed_float * (signal_samples - center) / sigma
    row_count = signal_samples.shape[0] * SEGMENT_COUNT
    patches = low(jnp.concatenate([scaled.reshape(row_count, PATCH), observed_float.reshape(row_count, PATCH)], axis=1))
    pre_one = low_back(matmul_result(patches, embedder_inner_matrix) + embedder_inner_offset)
    embed = low_back(matmul_result(low(jax.nn.silu(pre_one)), embedder_final_matrix) + matmul_result(patches, embedder_shortcut_matrix) + embedder_final_offset)
    normed = low(rms_scale(embed, mixer_prescale_factor))
    shape = (signal_samples.shape[0], SEGMENT_COUNT, HEADS, HEAD_DIM)
    query = low(low_back(matmul_result(normed, probe_matrix))).reshape(shape)
    keys = low(low_back(matmul_result(normed, address_matrix))).reshape(shape)
    values = low(low_back(matmul_result(normed, content_matrix))).reshape(shape)
    scores = low_back(jnp.einsum('snhd,smhd->shnm', query, keys, precision=highest) * HEAD_DIM ** (-0.5))
    attention = jax.nn.softmax(scores, axis=-1)
    mixed = jnp.einsum('shnm,smhd->snhd', low(attention), values, precision=highest)
    mixed = low(low_back(mixed)).reshape(row_count, HEADS * HEAD_DIM)
    middle = low_back(embed + matmul_result(mixed, mixer_merge_matrix))
    pre_two = low_back(matmul_result(low(rms_scale(middle, perceptron_prescale_factor)), expand_matrix))
    final = low_back(middle + matmul_result(low(jax.nn.silu(pre_two)), contract_matrix))
    layer_activations = low(final)
    before_readout = matmul_result(layer_activations, readout_inner_matrix) + readout_inner_offset
    scale_rows = jnp.repeat(sigma, SEGMENT_COUNT, axis=0)
    center_rows = jnp.repeat(center, SEGMENT_COUNT, axis=0)
    breadth_extent = HORIZON_ENTRIES // N_NARROW
    pieces = []
    for block in range(N_NARROW):
        reduced_precision = block * breadth_extent
        inner_activation = low(jax.nn.silu(low_back(before_readout)))
        restored_entries = matmul_result(inner_activation, readout_horizon_matrix[:, reduced_precision:reduced_precision + breadth_extent]) + matmul_result(layer_activations, readout_shortcut_matrix[:, reduced_precision:reduced_precision + breadth_extent])
        restored_entries = low_back(restored_entries + readout_offset[reduced_precision:reduced_precision + breadth_extent])
        pieces.append(restored_entries * scale_rows + center_rows)
    return jnp.concatenate(pieces, axis=1)

def reference(signal_samples, present_mask, embedder_inner_matrix, embedder_inner_offset, embedder_final_matrix, embedder_shortcut_matrix, embedder_final_offset, mixer_prescale_factor, probe_matrix, address_matrix, content_matrix, mixer_merge_matrix, perceptron_prescale_factor, expand_matrix, contract_matrix, readout_inner_matrix, readout_inner_offset, readout_horizon_matrix, readout_shortcut_matrix, readout_offset, prediction_cotangent):
    learnable_tensors = tuple((element_index.astype(jnp.float32) for element_index in (embedder_inner_matrix, embedder_inner_offset, embedder_final_matrix, embedder_shortcut_matrix, embedder_final_offset, mixer_prescale_factor, probe_matrix, address_matrix, content_matrix, mixer_merge_matrix, perceptron_prescale_factor, expand_matrix, contract_matrix, readout_inner_matrix, readout_inner_offset, readout_horizon_matrix, readout_shortcut_matrix, readout_offset)))
    observed_float = present_mask.astype(jnp.float32)
    signal_batch = SER_DEV * N_NARROW
    series_groups = signal_samples.reshape(N_WIDE, signal_batch, SAMPLE_LENGTH)
    mask_groups = observed_float.reshape(N_WIDE, signal_batch, SAMPLE_LENGTH)
    batch_cotangents = prediction_cotangent.reshape(N_WIDE, signal_batch * SEGMENT_COUNT, HORIZON_ENTRIES)

    def advance(accumulated_sum, item):
        values, mask_values, cotangent = item
        result, pull = jax.vjp(lambda inputs, weights: group_forward(inputs, mask_values, weights), values, learnable_tensors)
        incoming_cotangents, grad_weights = pull(cotangent)
        return (jax.tree.map(jnp.add, accumulated_sum, grad_weights), (result, incoming_cotangents))
    zero = jax.tree.map(jnp.zeros_like, learnable_tensors)
    accumulated_sum, (outcome_list, incoming_cotangents) = lax.scan(advance, zero, (series_groups, mask_groups, batch_cotangents))
    return (outcome_list.reshape(-1, HORIZON_ENTRIES), incoming_cotangents.reshape(-1, SAMPLE_LENGTH), accumulated_sum[0], accumulated_sum[1], accumulated_sum[2], accumulated_sum[3], accumulated_sum[4], accumulated_sum[5], accumulated_sum[6], accumulated_sum[7], accumulated_sum[8], accumulated_sum[9], accumulated_sum[10], accumulated_sum[11], accumulated_sum[12], accumulated_sum[13], accumulated_sum[14], accumulated_sum[15], accumulated_sum[16], accumulated_sum[17])
```

```python
import functools

import jax
import jax.numpy as jnp
from jax import lax
from jax.experimental import pallas as pl
from jax.experimental.pallas import tpu as pltpu
from jax.sharding import PartitionSpec as P

HEADS = 8
HEAD_DIM = 64
EPS = 1e-06
SCALE = HEAD_DIM ** (-0.5)
bf = jnp.bfloat16
f32 = jnp.float32
TILE = 384
AXES = ("wide", "narrow")
MIB = 1 << 20


def dot(a, b):
    return lax.dot_general(a, b, (((1,), (0,)), ((), ())), preferred_element_type=f32)


def dot_nt(a, b):
    return lax.dot_general(a, b, (((1,), (1,)), ((), ())), preferred_element_type=f32)


def dot_tn(a, b):
    return lax.dot_general(a, b, (((0,), (0,)), ((), ())), preferred_element_type=f32)


def call(kernel, outs, args, scratch=(), limit=16):
    vmem = pl.BlockSpec(memory_space=pltpu.VMEM)
    return list(pl.pallas_call(
        kernel,
        out_shape=[jax.ShapeDtypeStruct(s, d) for s, d in outs],
        in_specs=[vmem] * len(args),
        out_specs=[vmem] * len(outs),
        scratch_shapes=list(scratch),
        compiler_params=pltpu.CompilerParams(vmem_limit_bytes=limit * MIB),
    )(*args))


def silu_parts(v):
    s = 0.5 * jnp.tanh(0.5 * v) + 0.5
    h = v * s
    return h, s + h * (1.0 - s)


def iota(shape, dim):
    return lax.broadcasted_iota(jnp.int32, shape, dim)


def series_stats(samples, observed, patch):
    first = jnp.where(iota(samples.shape, 1) < patch, observed, 0.0)
    count = jnp.maximum(jnp.sum(first, axis=1, keepdims=True), 1.0)
    center = jnp.sum(first * samples, axis=1, keepdims=True) / count
    offset = samples - center
    spread = jnp.sum(first * offset * offset, axis=1, keepdims=True) / count
    sigma = jnp.sqrt(jnp.maximum(spread, 1.0))
    return first, count, center, offset, spread, sigma


def rms(v):
    return lax.rsqrt(jnp.mean(v * v, axis=-1, keepdims=True) + EPS)


def norm_back(g, v, gain):
    r = rms(v)
    u = v * r
    w = g * gain
    grad_gain = jnp.sum(g * u, axis=0, keepdims=True)
    return r * (w - u * jnp.mean(w * u, axis=-1, keepdims=True)), grad_gain


def per_token(v, tokens):
    n = v.shape[0]
    return jnp.broadcast_to(v[:, None, :], (n, tokens, v.shape[1])).reshape(n * tokens, v.shape[1])


def tokens_kernel(patch, samples, mask, wi, bi, wfin, wskip, bfin, gain, wq, wk, wv,
                  patches, hid, dhid, embed, normed, qkv, sigma_tok, center_tok):
    series, points = samples.shape
    tokens = points // patch
    rows = series * tokens
    observed = mask[...].astype(f32)
    x = samples[...]
    _, _, center, offset, _, sigma = series_stats(x, observed, patch)
    sigma_tok[...] = per_token(sigma, tokens)
    center_tok[...] = per_token(center, tokens)
    scaled = (observed * offset / sigma).astype(bf)
    spread_rows = (iota((rows, series), 0) // tokens == iota((rows, series), 1)).astype(f32).astype(bf)
    own = (iota((rows, points), 1) // patch == iota((rows, points), 0) % tokens).astype(f32)
    col = iota((points, 2 * patch), 0) % patch
    lane = iota((points, 2 * patch), 1)
    fold_s = (col == lane).astype(f32).astype(bf)
    fold_o = (col + patch == lane).astype(f32).astype(bf)
    es = (dot(spread_rows, scaled) * own).astype(bf)
    eo = (dot(spread_rows, observed.astype(bf)) * own).astype(bf)
    p = (dot(es, fold_s) + dot(eo, fold_o)).astype(bf)
    patches[...] = p
    acc = dot(p, wskip[...]) + bfin[...]
    width = wi.shape[1]
    for j in range(0, width, TILE):
        t = slice(j, j + TILE)
        h, d = silu_parts(dot(p, wi[:, t]) + bi[:, t])
        h = h.astype(bf)
        hid[:, t] = h
        dhid[:, t] = d.astype(bf)
        acc = acc + dot(h, wfin[t, :])
    embed[...] = acc
    n = (acc * rms(acc) * gain[...]).astype(bf)
    normed[...] = n
    inner = wq.shape[1]
    for i, w in enumerate((wq, wk, wv)):
        qkv[:, i * inner:(i + 1) * inner] = dot(n, w[...]).astype(bf)


def block_mask():
    return (iota((128, 256), 0) // 32 == iota((128, 256), 1) // 64).astype(f32).astype(bf)


def spread_heads(v, keep):
    return jnp.concatenate([v] * 4, axis=0) * keep


def pick_heads(v):
    head = iota((32, 256), 1) // 64
    out = v[0:32]
    for h in range(1, 4):
        out = jnp.where(head == h, v[32 * h:32 * h + 32], out)
    return out


def attend_kernel(qkv, probs, mixed):
    keep = block_mask()
    inner = HEADS * HEAD_DIM

    def one(s, carry):
        rows = pl.ds(pl.multiple_of(s * 32, 32), 32)
        for half in range(2):
            c = 256 * half
            q = spread_heads(qkv[rows, c:c + 256], keep)
            k = qkv[rows, inner + c:inner + c + 256]
            v = qkv[rows, 2 * inner + c:2 * inner + c + 256]
            scores = dot_nt(k, q) * SCALE
            e = jnp.exp(scores - jnp.max(scores, axis=0, keepdims=True))
            p = e / jnp.sum(e, axis=0, keepdims=True)
            probs[2 * s + half] = p
            mixed[rows, c:c + 256] = pick_heads(dot_tn(p.astype(bf), v)).astype(bf)
        return carry

    lax.fori_loop(0, qkv.shape[0] // 32, one, 0, unroll=4)


def ffn_kernel(embed, mixed, wm, gain, we, wc, middle, normed, hid, dhid, states):
    mid = embed[...] + dot(mixed[...], wm[...])
    middle[...] = mid
    n = (mid * rms(mid) * gain[...]).astype(bf)
    normed[...] = n
    acc = mid
    for j in range(0, we.shape[1], TILE):
        t = slice(j, j + TILE)
        h, d = silu_parts(dot(n, we[:, t]))
        h = h.astype(bf)
        hid[:, t] = h
        dhid[:, t] = d.astype(bf)
        acc = acc + dot(h, wc[t, :])
    states[...] = acc.astype(bf)


def me_of(masks, count):
    index = lax.axis_index("wide") * count + lax.axis_index("narrow")
    out = jnp.int32(0)
    for m in masks:
        out = out * 2 + (index // m) % 2
    return out


def head_kernel(count, masks, *refs):
    states, wri, bri, sigma = refs[:4]
    cots = refs[4:4 + count]
    whz = refs[4 + count:4 + 2 * count]
    refs = refs[4 + 2 * count:]
    hid, gpre = refs[:2]
    gs = refs[2:2 + count]
    keep, send, scr, tmp = refs[2 + count:]
    me = me_of(masks, count)
    st = states[...]
    sg = sigma[...]
    width = wri.shape[1]
    grads = [(c[...].astype(f32) * sg).astype(bf) for c in cots]
    for g_ref, g in zip(gs, grads):
        g_ref[...] = g
    sums = []
    for j in range(0, width, TILE):
        t = slice(j, j + TILE)
        h, d = silu_parts(dot(st, wri[:, t]) + bri[:, t])
        hid[:, t] = h.astype(bf)
        acc = dot_nt(grads[0], whz[0][t, :])
        for r in range(1, count):
            acc = acc + dot_nt(grads[r], whz[r][t, :])
        gp = (acc * d).astype(bf)
        gpre[:, t] = gp
        sums.append(jnp.sum(gp.astype(f32), axis=0, keepdims=True))
    nb = scr.shape[1]
    cols = grads[0].shape[1]
    for r in range(count):
        gt = grads[r].T
        for j in range(0, width, TILE):
            v = dot(gt, hid[:, j:j + TILE]).astype(bf)
            for i in range(TILE // 128):
                scr[r, (j // 128 + i) ^ me] = v[:, 128 * i:128 * i + 128]
        v = dot(gt, st).astype(bf)
        for i in range(v.shape[1] // 128):
            scr[r, (width // 128 + i) ^ me] = v[:, 128 * i:128 * i + 128]
        tmp[...] = jnp.zeros_like(tmp)
        bias = jnp.sum(grads[r].astype(f32), axis=0, keepdims=True)
        row = 0
        for j in range(0, cols, 128):
            n = min(128, cols - j)
            tmp[row:row + 1, 0:n] = bias[:, j:j + n]
            row += 1
        for s in sums:
            for i in range(TILE // 128):
                tmp[row:row + 1, :] = s[:, 128 * i:128 * i + 128]
                row += 1
        scr[r, (nb - 1) ^ me] = tmp[...].astype(bf)
    half = nb // 2
    for r in range(count):
        keep[r] = scr[r, :half]
        send[r] = scr[r, half:]


def put_matrix(scr, me, tile, value, offset, rows):
    v = value.astype(bf)
    for i in range(8):
        scr[(8 * tile + i) ^ me, offset:offset + rows, :] = v[rows * i:rows * i + rows]


def ship(scr, keep, send):
    half = scr.shape[0] // 2
    keep[...] = scr[:half]
    send[...] = scr[half:]


def head_back_kernel(count, masks, *refs):
    states, gpre, wri = refs[:3]
    gs = refs[3:3 + count]
    wsk = refs[3 + count:3 + 2 * count]
    gstates, keep, send, scr = refs[3 + 2 * count:]
    me = me_of(masks, count)
    acc = dot_nt(gpre[...], wri[...])
    for r in range(count):
        acc = acc + dot_nt(gs[r][...], wsk[r][...])
    gstates[...] = acc.astype(bf)
    st = states[...].T
    for j in range(4):
        put_matrix(scr, me, j, dot(st, gpre[:, TILE * j:TILE * j + TILE]), 0, 48)
    ship(scr, keep, send)


def ffn_back_kernel(count, masks, gstates, hid, dhid, normed, middle, wc, we, gain,
                    gmiddle, ggain, keep, send, scr):
    me = me_of(masks, count)
    g = gstates[...]
    nt = normed[...].T
    acc = None
    for j in range(4):
        t = slice(TILE * j, TILE * j + TILE)
        gp = (dot_nt(g, wc[t, :]) * dhid[:, t].astype(f32)).astype(bf)
        part = dot_nt(gp, we[:, t])
        acc = part if acc is None else acc + part
        put_matrix(scr, me, j, dot(nt, gp), 0, 48)
        put_matrix(scr, me, j, dot_tn(hid[:, t], g), 48, 48)
    back, gg = norm_back(acc, middle[...], gain[...])
    ggain[...] = gg
    gmiddle[...] = (g.astype(f32) + back).astype(bf)
    ship(scr, keep, send)


def attend_back_kernel(gmiddle, wm, qkv, probs, gqkv, gmix):
    keep = block_mask()
    inner = HEADS * HEAD_DIM
    gmix[...] = dot_nt(gmiddle[...], wm[...]).astype(bf)

    def one(s, carry):
        rows = pl.ds(pl.multiple_of(s * 32, 32), 32)
        for half in range(2):
            c = 256 * half
            q = spread_heads(qkv[rows, c:c + 256], keep)
            k = qkv[rows, inner + c:inner + c + 256]
            v = qkv[rows, 2 * inner + c:2 * inner + c + 256]
            g = spread_heads(gmix[rows, c:c + 256], keep)
            p = probs[2 * s + half]
            gp = dot_nt(v, g)
            gqkv[rows, 2 * inner + c:2 * inner + c + 256] = dot(p.astype(bf), g).astype(bf)
            ds = (p * (gp - jnp.sum(gp * p, axis=0, keepdims=True))).astype(bf)
            gqkv[rows, c:c + 256] = (pick_heads(dot_tn(ds, k)) * SCALE).astype(bf)
            gqkv[rows, inner + c:inner + c + 256] = (dot(ds, q) * SCALE).astype(bf)
        return carry

    lax.fori_loop(0, qkv.shape[0] // 32, one, 0, unroll=4)


def project_back_kernel(count, masks, gqkv, gmiddle, mixed, normed, embed, wq, wk, wv, gain,
                        gembed, ggain, keep, send, scr):
    me = me_of(masks, count)
    inner = wq.shape[1]
    acc = dot_nt(gqkv[:, :inner], wq[...])
    acc = acc + dot_nt(gqkv[:, inner:2 * inner], wk[...])
    acc = acc + dot_nt(gqkv[:, 2 * inner:], wv[...])
    back, gg = norm_back(acc, embed[...], gain[...])
    ggain[...] = gg
    gm = gmiddle[...]
    gembed[...] = (gm.astype(f32) + back).astype(bf)
    nt = normed[...].T
    for j in range(4):
        put_matrix(scr, me, j, dot(nt, gqkv[:, TILE * j:TILE * j + TILE]), 0, 48)
    v = dot_tn(mixed[...], gm).astype(bf)
    for i in range(32):
        scr[i ^ me, 48:64, :] = v[16 * i:16 * i + 16]
    ship(scr, keep, send)


def rows_of(tmp, row, v):
    for j in range(0, v.shape[1], 128):
        tmp[row:row + 1, :] = v[:, j:j + 128]
        row += 1
    return row


def tokens_back_kernel(count, masks, patch, gembed, hid, dhid, patches, wfin, wskip, wi, gain_one, gain_two,
                       gscaled, keep, send, scr, tmp):
    me = me_of(masks, count)
    g = gembed[...]
    p = patches[...]
    pt = p.T
    tmp[...] = jnp.zeros_like(tmp)
    gpat = dot_nt(g, wskip[...])
    row = 480
    for j in range(4):
        t = slice(TILE * j, TILE * j + TILE)
        gp = (dot_nt(g, wfin[t, :]) * dhid[:, t].astype(f32)).astype(bf)
        gpat = gpat + dot_nt(gp, wi[:, t])
        v = dot(pt, gp)
        for i in range(3):
            c = 3 * j + i
            tmp[32 * c:32 * c + 32, :] = v[:, 128 * i:128 * i + 128]
        row = rows_of(tmp, row, jnp.sum(gp.astype(f32), axis=0, keepdims=True))
        v = dot_tn(hid[:, t], g).astype(bf)
        for i in range(8):
            for k in range(3):
                scr[(8 * j + i) ^ me, 48 * k:48 * k + 48, :] = v[48 * i:48 * i + 48, 128 * k:128 * k + 128]
    v = dot(pt, g)
    for i in range(3):
        tmp[384 + 32 * i:416 + 32 * i, :] = v[:, 128 * i:128 * i + 128]
    row = rows_of(tmp, row, jnp.sum(g.astype(f32), axis=0, keepdims=True))
    row = rows_of(tmp, row, gain_one[...])
    row = rows_of(tmp, row, gain_two[...])
    for b in range(32):
        scr[b ^ me, 144:160, :] = tmp[16 * b:16 * b + 16].astype(bf)
    ship(scr, keep, send)
    series, points = gscaled.shape
    tokens = points // patch
    rows = series * tokens
    lane = iota((2 * patch, points), 1) % patch
    fold = (iota((2 * patch, points), 0) == lane).astype(f32).astype(bf)
    own = (iota((rows, points), 1) // patch == iota((rows, points), 0) % tokens).astype(f32)
    high = gpat.astype(bf)
    low = (gpat - high.astype(f32)).astype(bf)
    full = (dot(high, fold) + dot(low, fold)) * own
    gscaled[...] = jnp.sum(full.reshape(series, tokens, points), axis=1)


def forecast_kernel(count, patch, *refs):
    samples, mask, gscaled, hid, states, sigma_tok, center_tok = refs[:7]
    whz = refs[7:7 + count]
    wsk = refs[7 + count:7 + 2 * count]
    bias = refs[7 + 2 * count:7 + 3 * count]
    cots = refs[7 + 3 * count:7 + 4 * count]
    refs = refs[7 + 4 * count:]
    preds, series_grad = refs[:count], refs[count]
    sg = sigma_tok[...]
    ct = center_tok[...]
    row_c, row_s = None, None
    for r in range(count):
        raw = dot(hid[...], whz[r][...]) + dot(states[...], wsk[r][...]) + bias[r][...].astype(f32)
        preds[r][...] = (raw * sg + ct).astype(preds[r].dtype)
        c = cots[r][...].astype(f32)
        a = jnp.sum(c, axis=1, keepdims=True)
        b = jnp.sum(c * raw, axis=1, keepdims=True)
        row_c = a if row_c is None else row_c + a
        row_s = b if row_s is None else row_s + b
    observed = mask[...].astype(f32)
    x = samples[...]
    series, points = x.shape
    tokens = points // patch
    first, cnt, center, offset, spread, sigma = series_stats(x, observed, patch)
    out_c = jnp.sum(row_c.reshape(series, tokens, 1), axis=1)
    out_s = jnp.sum(row_s.reshape(series, tokens, 1), axis=1)
    og = observed * gscaled[...]
    g_center = out_c - jnp.sum(og, axis=1, keepdims=True) / sigma
    g_sigma = out_s - jnp.sum(og * offset, axis=1, keepdims=True) / (sigma * sigma)
    g_spread = jnp.where(spread > 1.0, g_sigma * 0.5 / sigma, 0.0)
    g_center = g_center - g_spread * 2.0 * jnp.sum(first * offset, axis=1, keepdims=True) / cnt
    series_grad[...] = og / sigma + g_spread * 2.0 * first * offset / cnt + g_center * first / cnt


def sum_split_kernel(n, *refs):
    ins, outs = refs[:n], refs[n:]
    step = ins[0].shape[0] // len(outs)
    for i, o in enumerate(outs):
        for k in range(step):
            v = ins[0][i * step + k].astype(f32)
            for a in ins[1:]:
                v = v + a[i * step + k].astype(f32)
            o[k] = v.astype(o.dtype)


def sum_split(arrays, parts):
    shape = arrays[0].shape
    out = (shape[0] // parts,) + shape[1:]
    return call(functools.partial(sum_split_kernel, len(arrays)), [(out, bf)] * parts, arrays, limit=4)


def xor_send(v, mask, total):
    return lax.ppermute(v, AXES, [(i, i ^ mask) for i in range(total)])


def combos(bits):
    out = [0]
    for b in bits:
        out = [o + s for o in out for s in (0, b)]
    return out


def reduce_blocks(pieces, steps, rest, total):
    for k, bits in enumerate(steps):
        masks = combos(bits)
        received = [xor_send(p, m, total) for p, m in zip(pieces[1:], masks[1:])]
        parts = 1 if k + 1 == len(steps) else 1 << len(steps[k + 1])
        pieces = sum_split([pieces[0]] + received, parts)
    own = pieces[0]
    for m in rest:
        own = sum_split([own, xor_send(own, m, total)], 1)[0]
    return own


def gather_blocks(own, steps, total):
    have = [own]
    for k in reversed(range(len(steps))):
        masks = combos(steps[k])
        if k == 0:
            return have + [xor_send(h, m, total) for m in masks[1:] for h in have]
        whole = have[0] if len(have) == 1 else jnp.concatenate(have, axis=0)
        have = [whole] + [xor_send(whole, m, total) for m in masks[1:]]


def unpack(kernel, arrays, outs, extra=()):
    n = sum(a.shape[0] for a in arrays)
    block = arrays[0].shape[1:]
    return call(kernel, outs, arrays, scratch=[pltpu.VMEM((n,) + block, bf)] + list(extra), limit=24)


def assemble(refs, scr):
    k = 0
    for a in refs:
        scr[k:k + a.shape[0]] = a[...]
        k += a.shape[0]


def unpack_head(count, masks, n, *refs):
    arrays, (w, skip, bias, bin_, scr, tmp) = refs[:n], refs[n:]
    me = me_of(masks, count)
    assemble(arrays, scr)
    width, cols = w.shape
    for b in range(width // 128):
        w[128 * b:128 * b + 128, :] = scr[b ^ me].astype(f32).T
    for i in range(skip.shape[0] // 128):
        skip[128 * i:128 * i + 128, :] = scr[(width // 128 + i) ^ me].astype(f32).T
    tmp[...] = scr[(scr.shape[0] - 1) ^ me].astype(f32)
    row = 0
    for j in range(0, cols, 128):
        n = min(128, cols - j)
        bias[:, j:j + n] = tmp[row:row + 1, 0:n]
        row += 1
    for j in range(0, bin_.shape[1], 128):
        bin_[:, j:j + 128] = tmp[row:row + 1, :]
        row += 1


def unpack_wide(w, scr, me, offset):
    for b in range(32):
        j, i = b // 8, b % 8
        w[48 * i:48 * i + 48, TILE * j:TILE * j + TILE] = scr[b ^ me, offset:offset + 48, :].astype(f32)


def unpack_tall(w, scr, me, offset):
    for b in range(32):
        w[48 * b:48 * b + 48, :] = scr[b ^ me, offset:offset + 48, :].astype(f32)


def unpack_in(count, masks, n, *refs):
    arrays, (w, scr) = refs[:n], refs[n:]
    assemble(arrays, scr)
    unpack_wide(w, scr, me_of(masks, count), 0)


def unpack_ffn(count, masks, n, *refs):
    arrays, (up, down, scr) = refs[:n], refs[n:]
    me = me_of(masks, count)
    assemble(arrays, scr)
    unpack_wide(up, scr, me, 0)
    unpack_tall(down, scr, me, 48)


def unpack_attention(count, masks, n, *refs):
    arrays, (gq, gk, gv, wo, scr) = refs[:n], refs[n:]
    me = me_of(masks, count)
    assemble(arrays, scr)
    for b in range(32):
        j, i = b // 8, b % 8
        v = scr[b ^ me, 0:48, :].astype(f32)
        for k in range(3):
            c = TILE * j + 128 * k
            o = (gq, gk, gv)[c // 512]
            o[48 * i:48 * i + 48, c % 512:c % 512 + 128] = v[:, 128 * k:128 * k + 128]
        wo[16 * b:16 * b + 16, :] = scr[b ^ me, 48:64, :].astype(f32)


def unpack_tokens(count, masks, n, *refs):
    arrays, (out, tin, skip, bin_, bout, g1, g2, scr, tmp) = refs[:n], refs[n:]
    me = me_of(masks, count)
    assemble(arrays, scr)
    for b in range(32):
        for k in range(3):
            out[48 * b:48 * b + 48, 128 * k:128 * k + 128] = scr[b ^ me, 48 * k:48 * k + 48, :].astype(f32)
        tmp[16 * b:16 * b + 16, :] = scr[b ^ me, 144:160, :].astype(f32)
    for c in range(12):
        tin[:, 128 * c:128 * c + 128] = tmp[32 * c:32 * c + 32, :]
    for i in range(3):
        skip[:, 128 * i:128 * i + 128] = tmp[384 + 32 * i:416 + 32 * i, :]
    row = 480
    for o in (bin_, bout, g1, g2):
        for j in range(0, o.shape[1], 128):
            o[:, j:j + 128] = tmp[row:row + 1, :]
            row += 1


def per_device(wide, count, signal_samples, present_mask, wi, bi, wfin, wskip, bfin, gain_one, wq, wk, wv, wm,
               gain_two, we, wc, wri, bri, whz, wrs, bro, cotangent):
    series, points = signal_samples.shape
    patch = wi.shape[0] // 2
    tokens = points // patch
    rows = series * tokens
    dim, width = wri.shape
    cols = whz.shape[1]
    inner = wq.shape[1]
    total = wide * count
    X, CORE, Y, Z0, Z1 = 1, count, 2 * count, 4 * count, 8 * count
    narrow_rest = [1 << i for i in range(1, count.bit_length() - 1)]
    wide_rest = [count << i for i in range(4, wide.bit_length() - 1)]
    row = lambda v: v.reshape(1, -1)

    narrow = lax.axis_index("narrow")
    cot = [
        lax.dynamic_slice_in_dim(cotangent, (narrow ^ r) * rows, rows, 0) for r in range(count)
    ]
    cots = [cot[0]] + [xor_send(cot[r].astype(bf), r, total) for r in range(1, count)]
    whzs = [whz] + [xor_send(whz, r, total) for r in range(1, count)]
    wrss = [wrs] + [xor_send(wrs, r, total) for r in range(1, count)]
    bros = [row(bro)] + [xor_send(row(bro), r, total) for r in range(1, count)]

    patches, hid1, d1, embed, normed1, qkv, sigma, center = call(
        functools.partial(tokens_kernel, patch),
        [((rows, 2 * patch), bf), ((rows, width), bf), ((rows, width), bf), ((rows, dim), f32), ((rows, dim), bf),
         ((rows, 3 * inner), bf), ((rows, 1), f32), ((rows, 1), f32)],
        [signal_samples, present_mask, wi, row(bi), wfin, wskip, row(bfin), row(gain_one), wq, wk, wv],
    )
    probs, mixed = call(attend_kernel, [((2 * series, 32, 128), f32), ((rows, inner), bf)], [qkv])
    middle, normed2, hid2, d2, states = call(
        ffn_kernel,
        [((rows, dim), f32), ((rows, dim), bf), ((rows, width), bf), ((rows, width), bf), ((rows, dim), bf)],
        [embed, mixed, wm, row(gain_two), we, wc],
    )

    steps = [[CORE], [Y, X], [Z1, Z0]]
    rest = narrow_rest + wide_rest
    masks = [b for s in steps for b in s]
    head_steps = [[CORE], [Y], [Z1, Z0]]
    head_masks = [b for s in head_steps for b in s]

    out = call(
        functools.partial(head_kernel, count, head_masks),
        [((rows, width), bf), ((rows, width), bf)] + [((rows, cols), bf)] * count
        + [((count, 8, cols, 128), bf)] * 2,
        [states, wri, row(bri), sigma] + cots + whzs,
        scratch=[pltpu.VMEM((count, 16, cols, 128), bf), pltpu.VMEM((cols, 128), f32)],
    )
    hidh, gpre = out[:2]
    gs = out[2:2 + count]
    keep, send = out[2 + count:]
    got = xor_send(send, CORE, total)
    flat = lambda v: v.reshape(2 * count, 4, cols, 128)
    pieces = sum_split([flat(keep), flat(got)], 2 * count)
    got = [
        xor_send(pieces[2 * r + y].reshape(4, cols, 128), r + y * Y, total)
        for r in range(count) for y in range(2) if r or y
    ]
    pieces = sum_split([pieces[0].reshape(4, cols, 128)] + got, 4)
    head_own = reduce_blocks(pieces, [[Z1, Z0]], wide_rest, total)
    head_arrays = gather_blocks(head_own, head_steps, total)
    n = len(head_arrays)
    g_hw, g_hs, g_hb, g_hib = unpack(
        functools.partial(unpack_head, count, head_masks, n), head_arrays,
        [((width, cols), f32), ((dim, cols), f32), ((1, cols), f32), ((1, width), f32)],
        extra=[pltpu.VMEM((cols, 128), f32)],
    )

    def group(kernel, args, outs, block):
        res = call(functools.partial(kernel, count, masks), outs + [((16,) + block, bf)] * 2, args,
                   scratch=[pltpu.VMEM((32,) + block, bf)])
        return res[:-2], res[-2:]

    def exchange(pair, kernel, outs, extra=()):
        own = reduce_blocks(list(pair), steps, rest, total)
        arrays = gather_blocks(own, steps, total)
        return unpack(functools.partial(kernel, count, masks, len(arrays)), arrays, outs, extra)

    (gstates,), pair = group(head_back_kernel, [states, gpre, wri] + gs + wrss, [((rows, dim), bf)], (48, TILE))
    (g_hiw,) = exchange(pair, unpack_in, [((dim, width), f32)])

    (gmiddle, gg2), pair = group(
        ffn_back_kernel, [gstates, hid2, d2, normed2, middle, wc, we, row(gain_two)],
        [((rows, dim), bf), ((1, dim), f32)], (96, TILE))
    g_up, g_down = exchange(pair, unpack_ffn, [((dim, width), f32), ((width, dim), f32)])

    (gqkv,) = call(attend_back_kernel, [((rows, 3 * inner), bf)], [gmiddle, wm, qkv, probs],
                   scratch=[pltpu.VMEM((rows, inner), bf)])
    (gembed, gg1), pair = group(
        project_back_kernel, [gqkv, gmiddle, mixed, normed1, embed, wq, wk, wv, row(gain_one)],
        [((rows, dim), bf), ((1, dim), f32)], (64, TILE))
    g_q, g_k, g_v, g_wo = exchange(pair, unpack_attention, [((dim, inner), f32)] * 3 + [((inner, dim), f32)])

    gscaled, keep, send = call(
        functools.partial(tokens_back_kernel, count, masks, patch),
        [((series, points), f32)] + [((16, 160, 128), bf)] * 2,
        [gembed, hid1, d1, patches, wfin, wskip, wi, gg1, gg2],
        scratch=[pltpu.VMEM((32, 160, 128), bf), pltpu.VMEM((512, 128), f32)])
    g_to, g_ti, g_ts, g_tib, g_tob, g_g1, g_g2 = exchange(
        [keep, send], unpack_tokens,
        [((width, dim), f32), ((2 * patch, width), f32), ((2 * patch, dim), f32), ((1, width), f32), ((1, dim), f32),
         ((1, dim), f32), ((1, dim), f32)],
        extra=[pltpu.VMEM((512, 128), f32)])

    out = call(
        functools.partial(forecast_kernel, count, patch),
        [((rows, cols), f32)] + [((rows, cols), bf)] * (count - 1) + [((series, points), f32)],
        [signal_samples, present_mask, gscaled, hidh, states, sigma, center] + whzs + wrss + bros + cots,
    )
    preds, g_series = out[:count], out[count]
    preds = [preds[0]] + [xor_send(preds[r], r, total).astype(f32) for r in range(1, count)]
    prediction = jnp.concatenate(
        [functools.reduce(lambda a, r: jnp.where((narrow ^ r) == s, preds[r], a), range(1, count), preds[0])
         for s in range(count)], axis=0)

    vec = lambda v: v.reshape(-1)
    return (prediction, g_series, g_ti, vec(g_tib), g_to, g_ts, vec(g_tob), vec(g_g1), g_q, g_k, g_v, g_wo,
            vec(g_g2), g_up, g_down, g_hiw, vec(g_hib), g_hw, g_hs, vec(g_hb))


def solution(mesh):
    wide, count = mesh.shape["wide"], mesh.shape["narrow"]
    both = P(("wide", "narrow"), None)
    return jax.shard_map(
        functools.partial(per_device, wide, count),
        mesh=mesh,
        in_specs=(both, both) + (P(),) * 15 + (P(None, "narrow"), P(None, "narrow"), P("narrow"), P("wide", "narrow")),
        out_specs=(P("wide", "narrow"), both) + (P(),) * 15
        + (P(None, "narrow"), P(None, "narrow"), P("narrow")),
        check_vma=False,
    )
```

```python
import functools

import jax
import jax.numpy as jnp
from jax import lax
from jax.experimental import pallas as pl
from jax.experimental.pallas import tpu as pltpu
from jax.sharding import PartitionSpec as P

HEADS = 8
HEAD_DIM = 64
EPS = 1e-06
SCALE = HEAD_DIM ** (-0.5)
bf = jnp.bfloat16
f32 = jnp.float32
TILE = 384
AXES = ("wide", "narrow")
MIB = 1 << 20


def dot(a, b):
    return lax.dot_general(a, b, (((1,), (0,)), ((), ())), preferred_element_type=f32)


def dot_nt(a, b):
    return lax.dot_general(a, b, (((1,), (1,)), ((), ())), preferred_element_type=f32)


def dot_tn(a, b):
    return lax.dot_general(a, b, (((0,), (0,)), ((), ())), preferred_element_type=f32)


class Chain:
    def __init__(self):
        self.last = None

    def __call__(self, kernel, outs, args, scratch=(), limit=16, raw=()):
        vmem = pl.BlockSpec(memory_space=pltpu.VMEM)
        hbm = pl.BlockSpec(memory_space=pl.ANY)
        args, raw = list(args), [pltpu.with_memory_space_constraint(v, pltpu.HBM) for v in raw]
        deps = [] if self.last is None or any(a is self.last for a in args) else [self.last]
        n, d = len(args) + len(raw), len(deps)

        def body(*refs):
            kernel(*refs[:n], *refs[n + d:])

        name = getattr(kernel, "__name__", None) or kernel.func.__name__
        res = list(pl.pallas_call(
            body,
            name=name,
            out_shape=[jax.ShapeDtypeStruct(s, d) for s, d in outs],
            in_specs=[vmem] * len(args) + [pl.BlockSpec(memory_space=pltpu.HBM)] * len(raw) + [hbm] * d,
            out_specs=[vmem] * len(outs),
            scratch_shapes=list(scratch),
            cost_estimate=pl.CostEstimate(flops=1000, bytes_accessed=1000, transcendentals=0),
            compiler_params=pltpu.CompilerParams(vmem_limit_bytes=limit * MIB),
        )(*args, *raw, *deps))
        self.last = min(res, key=lambda r: r.size)
        return res


def silu_parts(v):
    s = 0.5 * jnp.tanh(0.5 * v) + 0.5
    h = v * s
    return h, s + h * (1.0 - s)


def iota(shape, dim):
    return lax.broadcasted_iota(jnp.int32, shape, dim)


def series_stats(samples, observed, patch):
    first = jnp.where(iota(samples.shape, 1) < patch, observed, 0.0)
    count = jnp.maximum(jnp.sum(first, axis=1, keepdims=True), 1.0)
    center = jnp.sum(first * samples, axis=1, keepdims=True) / count
    offset = samples - center
    spread = jnp.sum(first * offset * offset, axis=1, keepdims=True) / count
    sigma = jnp.sqrt(jnp.maximum(spread, 1.0))
    return first, count, center, offset, spread, sigma


def rms(v):
    return lax.rsqrt(jnp.mean(v * v, axis=-1, keepdims=True) + EPS)


def norm_back(g, v, gain):
    r = rms(v)
    u = v * r
    w = g * gain
    grad_gain = jnp.sum(g * u, axis=0, keepdims=True)
    return r * (w - u * jnp.mean(w * u, axis=-1, keepdims=True)), grad_gain


def token_row(v, rows):
    series = v.shape[0]
    own = iota((series, rows), 1) // (rows // series) == iota((series, rows), 0)
    return jnp.sum(jnp.where(own, v, 0.0), axis=0, keepdims=True)


def series_column(v, series):
    rows = v.shape[1]
    own = iota((series, rows), 1) // (rows // series) == iota((series, rows), 0)
    return jnp.sum(jnp.where(own, v, 0.0), axis=1, keepdims=True)


def me_of(masks, count):
    index = lax.axis_index("wide") * count + lax.axis_index("narrow")
    out = jnp.int32(0)
    for m in masks:
        out = out * 2 + (index // m) % 2
    return out


def prepare_kernel(count, rows, bias, cot, whz, wrs, *refs):
    cots, (own, mine, short) = refs[:count - 1], refs[count - 1:count + 2]
    wide_cots, half, shortcut, sems = refs[count + 2:]
    narrow = lax.axis_index("narrow")
    core = lax.axis_index("wide") % 2
    width, dim = half.shape[1], shortcut.shape[1]

    def tokens(r):
        return cot.at[:, pl.ds(pl.multiple_of((narrow ^ r) * rows, 128), rows)]

    copies = [
        pltpu.make_async_copy(whz.at[:, pl.ds(pl.multiple_of(core * width, 128), width)], half, sems.at[0]),
        pltpu.make_async_copy(wrs, shortcut, sems.at[1]),
        pltpu.make_async_copy(tokens(0), own, sems.at[2]),
    ] + [pltpu.make_async_copy(tokens(r), wide_cots.at[r - 1], sems.at[2 + r]) for r in range(1, count)]
    for c in copies:
        c.start()
    for c in copies[:2]:
        c.wait()
    short[:, :dim] = shortcut[...]
    short[:, dim:] = dot_tn(bias[...].astype(f32)[None, :].astype(bf), jnp.ones((1, 128), bf)).astype(bf)
    mine[:, :width] = half[...]
    part = (dim + 128) // 2
    mine[:, width:] = short[:, pl.ds(pl.multiple_of(core * part, 128), part)]
    for c in copies[2:]:
        c.wait()
    for r in range(1, count):
        cots[r - 1][...] = wide_cots[r - 1].astype(bf)


def gate_kernel(v, out):
    out[...] = v[...]


def tokens_kernel(patch, *refs):
    samples, mask, bi, bfin, gain = refs[:5]
    hbm = refs[5:16]
    patches, hid, dhid, embed, normed, qkv, sigma_row, center_row = refs[16:24]
    vmem, sems = refs[24:35], refs[35]
    copies = [pltpu.make_async_copy(h, v, sems.at[i]) for i, (h, v) in enumerate(zip(hbm, vmem))]
    for c in copies:
        c.start()
    wi, wfin, wskip, wq, wk, wv = vmem[:6]
    series, points = samples.shape
    tokens = points // patch
    rows = series * tokens
    observed = mask[...].astype(f32)
    _, _, center, offset, _, sigma = series_stats(samples[...], observed, patch)
    sigma_row[...] = token_row(sigma, rows)
    center_row[...] = token_row(center, rows)
    scaled = (observed * offset / sigma).astype(bf)
    spread_rows = (iota((rows, series), 0) // tokens == iota((rows, series), 1)).astype(f32).astype(bf)
    own = (iota((rows, points), 1) // patch == iota((rows, points), 0) % tokens).astype(f32)
    col = iota((points, 2 * patch), 0) % patch
    lane = iota((points, 2 * patch), 1)
    fold_s = (col == lane).astype(f32).astype(bf)
    fold_o = (col + patch == lane).astype(f32).astype(bf)
    es = (dot(spread_rows, scaled) * own).astype(bf)
    eo = (dot(spread_rows, observed.astype(bf)) * own).astype(bf)
    p = (dot(es, fold_s) + dot(eo, fold_o)).astype(bf)
    patches[...] = p
    for c in copies[:3]:
        c.wait()
    acc = dot(p, wskip[...]) + bfin[...][None, :]
    for j in range(0, wi.shape[1], TILE):
        t = slice(j, j + TILE)
        h, d = silu_parts(dot(p, wi[:, t]) + bi[t][None, :])
        h = h.astype(bf)
        hid[:, t] = h
        dhid[:, t] = d.astype(bf)
        acc = acc + dot(h, wfin[t, :])
    embed[...] = acc
    n = (acc * rms(acc) * gain[...][None, :]).astype(bf)
    normed[...] = n
    inner = wq.shape[1]
    for i, w in enumerate((wq, wk, wv)):
        copies[3 + i].wait()
        qkv[:, i * inner:(i + 1) * inner] = dot(n, w[...]).astype(bf)
    for c in copies[6:]:
        c.wait()


def block_mask():
    return (iota((128, 256), 0) // 32 == iota((128, 256), 1) // 64).astype(f32).astype(bf)


def spread_heads(v, keep):
    return jnp.concatenate([v] * 4, axis=0) * keep


def pick_heads(v):
    head = iota((32, 256), 1) // 64
    out = v[0:32]
    for h in range(1, 4):
        out = jnp.where(head == h, v[32 * h:32 * h + 32], out)
    return out


def pairs(rows):
    for i in range(rows // 16):
        yield i, slice(32 * (i // 2), 32 * (i // 2) + 32), 256 * (i % 2)


def attend_kernel(qkv, probs, mixed):
    keep = block_mask()
    inner = HEADS * HEAD_DIM
    rows = qkv.shape[0]
    for i, s, c in pairs(rows):
        q = spread_heads(qkv[s, c:c + 256], keep)
        probs[i] = dot_nt(qkv[s, inner + c:inner + c + 256], q)
    for i in range(0, rows // 16, 4):
        v = probs[i:i + 4] * SCALE
        e = jnp.exp(v - jnp.max(v, axis=1, keepdims=True))
        probs[i:i + 4] = e / jnp.sum(e, axis=1, keepdims=True)
    for i, s, c in pairs(rows):
        v = qkv[s, 2 * inner + c:2 * inner + c + 256]
        mixed[s, c:c + 256] = pick_heads(dot_tn(probs[i].astype(bf), v)).astype(bf)


def ffn_kernel(embed, mixed, wm, gain, we, wc, wri, bri, middle, normed, hid, dhid, states, hidh, dh):
    mid = embed[...] + dot(mixed[...], wm[...])
    middle[...] = mid
    n = (mid * rms(mid) * gain[...][None, :]).astype(bf)
    normed[...] = n
    acc = mid
    for j in range(0, we.shape[1], TILE):
        t = slice(j, j + TILE)
        h, d = silu_parts(dot(n, we[:, t]))
        h = h.astype(bf)
        hid[:, t] = h
        dhid[:, t] = d.astype(bf)
        acc = acc + dot(h, wc[t, :])
    st = acc.astype(bf)
    states[...] = st
    for j in range(0, wri.shape[1], TILE):
        t = slice(j, j + TILE)
        h, d = silu_parts(dot(st, wri[:, t]) + bri[t][None, :])
        hidh[:, t] = h.astype(bf)
        dh[:, t] = d.astype(bf)


def put_slabs(scr, me, tile, value, offset, slabs):
    for i in range(8):
        for n, k in enumerate(slabs):
            scr[(8 * tile + i) ^ me, offset + 48 * n:offset + 48 * n + 48, :] = (
                value[48 * i:48 * i + 48, 128 * k:128 * k + 128])


def ship(parts, keep, send):
    at = 0
    for p in parts:
        n, rows = p.shape[0] // 2, p.shape[1]
        keep[:, at:at + rows] = p[:n]
        send[:, at:at + rows] = p[n:]
        at += rows


def first_rows(cols):
    return 16 * ((cols + 31) // 32)


def rows_of(tmp, row, v):
    for j in range(0, v.shape[1], 128):
        tmp[row:row + 1, :] = v[:, j:j + 128]
        row += 1
    return row


def columns_kernel(count, masks, *refs):
    states, hidh, sigma = refs[:3]
    cots, refs = refs[3:3 + count], refs[3 + count:]
    groups = max(count // 2, 1)
    outs, (tmp, *scrs) = refs[:2 * groups], refs[2 * groups:]
    me = me_of(masks, count)
    st = states[...]
    width = hidh.shape[1]
    cols = tmp.shape[0]
    cut = first_rows(cols)
    for r in range(count):
        turned = (cots[r][...].astype(f32) * sigma[...]).astype(bf)
        scr_a, scr_b = scrs[2 * (r // 2):2 * (r // 2) + 2]

        def put(c, v):
            rel = c ^ me
            core, y, z = rel // 8, (rel // 4) % 2, rel % 4
            scr_a[core * 16 + (r % 2) * 8 + y * 4 + z] = v[:cut]
            scr_b[core * 16 + y * 8 + (r % 2) * 4 + z] = v[cut:]

        for j in range(0, width, TILE):
            v = dot(turned, hidh[:, j:j + TILE]).astype(bf)
            for i in range(TILE // 128):
                put(j // 128 + i, v[:, 128 * i:128 * i + 128])
        v = dot(turned, st).astype(bf)
        for i in range(st.shape[1] // 128):
            put(width // 128 + i, v[:, 128 * i:128 * i + 128])
        tmp[...] = jnp.zeros_like(tmp)
        bias = dot_nt(jnp.ones((8, turned.shape[1]), bf), turned)
        for row, j in enumerate(range(0, cols, 128)):
            n = min(128, cols - j)
            tmp[row:row + 1, 0:n] = bias[0:1, j:j + n]
        put(15, tmp[...].astype(bf))
    for i in range(groups):
        ship(scrs[2 * i:2 * i + 2], *outs[2 * i:2 * i + 2])


def head_kernel(count, *refs):
    dh, sigma, wri = refs[:3]
    refs = refs[3:]
    cots, refs = refs[:count], refs[count:]
    whz, refs = refs[0], refs[1:]
    far, refs = refs[:2 * (count - 1)], refs[2 * (count - 1):]
    short, refs = refs[0], refs[1:]
    gstates, gpre, sums = refs[:3]
    mats, shorts = refs[3:2 + count], refs[2 + count:1 + 2 * count]
    width = wri.shape[1]
    dim = wri.shape[0]
    half, part = width // 2, (dim + 128) // 2
    core = lax.axis_index("wide") % 2
    for r in range(count - 1):
        for k, c in enumerate((core, 1 - core)):
            mats[r][:, pl.ds(pl.multiple_of(c * half, 128), half)] = far[2 * r + k][:, :half]
            shorts[r][:, pl.ds(pl.multiple_of(c * part, 128), part)] = far[2 * r + k][:, half:]
    mats = [whz] + list(mats)
    shorts = [short] + list(shorts)
    grads = [(c[...].astype(f32) * sigma[...]).astype(bf).T for c in cots]
    for j in range(0, width, TILE):
        t = slice(j, j + TILE)
        acc = dot(grads[0], mats[0][:, t])
        for r in range(1, count):
            acc = acc + dot(grads[r], mats[r][:, t])
        gp = (acc * dh[:, t].astype(f32)).astype(bf)
        gpre[:, t] = gp
        sums[:, t] = jnp.sum(gp.astype(f32), axis=0, keepdims=True)
    acc = dot_nt(gpre[...], wri[...])
    for r in range(count):
        acc = acc + dot(grads[r], shorts[r][:, :dim])
    gstates[...] = acc.astype(bf)


def ffn_back_kernel(count, masks, gstates, states, gpre, sums, hid, dhid, normed, middle, wc, we, gain,
                    gmiddle, keep, send, scr_a, scr_b, tmp):
    me_a, me_b = (me_of(m, count) for m in masks)
    g = gstates[...]
    nt = normed[...].T
    acc = None
    for j in range(4):
        t = slice(TILE * j, TILE * j + TILE)
        gp = (dot_nt(g, wc[t, :]) * dhid[:, t].astype(f32)).astype(bf)
        part = dot_nt(gp, we[:, t])
        acc = part if acc is None else acc + part
        up = dot(nt, gp).astype(bf)
        put_slabs(scr_a, me_a, j, up, 160, (0,))
        put_slabs(scr_b, me_b, j, up, 0, (1, 2))
        put_slabs(scr_b, me_b, j, dot_tn(hid[:, t], g).astype(bf), 96, (0, 1, 2))
    back, gg = norm_back(acc, middle[...], gain[...][None, :])
    gmiddle[...] = (g.astype(f32) + back).astype(bf)
    st = states[...].T
    for j in range(4):
        put_slabs(scr_a, me_a, j, dot(st, gpre[:, TILE * j:TILE * j + TILE]).astype(bf), 0, (0, 1, 2))
    scr_a[:, 144:160, :] = jnp.zeros((32, 16, 128), bf)
    tmp[...] = jnp.zeros_like(tmp)
    row = rows_of(tmp, 0, sums[...])
    rows_of(tmp, row, gg)
    scr_a[me_a, 144:160, :] = tmp[...].astype(bf)
    ship((scr_a, scr_b), keep, send)


def attend_back_kernel(gmiddle, wm, qkv, probs, gqkv, gmix, gprobs, low):
    keep = block_mask()
    inner = HEADS * HEAD_DIM
    rows = qkv.shape[0]
    gmix[...] = dot_nt(gmiddle[...], wm[...]).astype(bf)
    for i, s, c in pairs(rows):
        g = spread_heads(gmix[s, c:c + 256], keep)
        gprobs[i] = dot_nt(qkv[s, 2 * inner + c:2 * inner + c + 256], g)
        gqkv[s, 2 * inner + c:2 * inner + c + 256] = dot(probs[i].astype(bf), g).astype(bf)
    for i in range(0, rows // 16, 4):
        p, g = probs[i:i + 4], gprobs[i:i + 4]
        low[i:i + 4] = (p * (g - jnp.sum(g * p, axis=1, keepdims=True))).astype(bf)
    for i, s, c in pairs(rows):
        ds = low[i]
        q = spread_heads(qkv[s, c:c + 256], keep)
        k = qkv[s, inner + c:inner + c + 256]
        gqkv[s, c:c + 256] = (pick_heads(dot_tn(ds, k)) * SCALE).astype(bf)
        gqkv[s, inner + c:inner + c + 256] = (dot(ds, q) * SCALE).astype(bf)


def project_back_kernel(count, masks, gqkv, gmiddle, mixed, normed, embed, wq, wk, wv, gain, gembed, ggain, part_a, part_b):
    me_a, me_b = (me_of(m, count) for m in masks)
    inner = wq.shape[1]
    acc = dot_nt(gqkv[:, :inner], wq[...])
    acc = acc + dot_nt(gqkv[:, inner:2 * inner], wk[...])
    acc = acc + dot_nt(gqkv[:, 2 * inner:], wv[...])
    back, gg = norm_back(acc, embed[...], gain[...][None, :])
    ggain[...] = gg
    gm = gmiddle[...]
    gembed[...] = (gm.astype(f32) + back).astype(bf)
    nt = normed[...].T
    for j in range(4):
        put_slabs(part_a, me_a, j, dot(nt, gqkv[:, TILE * j:TILE * j + TILE]).astype(bf), 0, (0, 1, 2))
    v = dot_tn(mixed[...], gm).astype(bf)
    for i in range(32):
        for k in range(3):
            part_b[i ^ me_b, 16 * k:16 * k + 16, :] = v[16 * i:16 * i + 16, 128 * k:128 * k + 128]


def tokens_back_kernel(count, masks, patch, gembed, hid, dhid, patches, wfin, wskip, wi, gain_one, part_a, part_b,
                       gscaled, keep, send, scr_a, scr_b, tmp):
    me_a, me_b = (me_of(m, count) for m in masks)
    g = gembed[...]
    p = patches[...]
    pt = p.T
    tmp[...] = jnp.zeros_like(tmp)
    gpat = dot_nt(g, wskip[...])
    row = 480
    for j in range(4):
        t = slice(TILE * j, TILE * j + TILE)
        gp = (dot_nt(g, wfin[t, :]) * dhid[:, t].astype(f32)).astype(bf)
        gpat = gpat + dot_nt(gp, wi[:, t])
        v = dot(pt, gp)
        for i in range(3):
            c = 3 * j + i
            tmp[32 * c:32 * c + 32, :] = v[:, 128 * i:128 * i + 128]
        row = rows_of(tmp, row, jnp.sum(gp.astype(f32), axis=0, keepdims=True))
        put_slabs(scr_b, me_b, j, dot_tn(hid[:, t], g).astype(bf), 0, (0, 1, 2))
    v = dot(pt, g)
    for i in range(3):
        tmp[384 + 32 * i:416 + 32 * i, :] = v[:, 128 * i:128 * i + 128]
    row = rows_of(tmp, row, jnp.sum(g.astype(f32), axis=0, keepdims=True))
    rows_of(tmp, row, gain_one[...])
    for b in range(32):
        scr_a[b ^ me_a] = tmp[16 * b:16 * b + 16].astype(bf)
    ship((part_a, scr_a, scr_b, part_b), keep, send)
    series, points = gscaled.shape
    tokens = points // patch
    rows = series * tokens
    lane = iota((2 * patch, points), 1) % patch
    fold = (iota((2 * patch, points), 0) == lane).astype(f32).astype(bf)
    own = (iota((rows, points), 1) // patch == iota((rows, points), 0) % tokens).astype(f32)
    high = gpat.astype(bf)
    low = (gpat - high.astype(f32)).astype(bf)
    full = (dot(high, fold) + dot(low, fold)) * own
    gscaled[...] = jnp.sum(full.reshape(series, tokens, points), axis=1)


def forecast_kernel(count, patch, *refs):
    samples, mask, gscaled, hid, states, sigma_row, center_row = refs[:7]
    refs = refs[7:]
    mats, refs = refs[:count], refs[count:]
    short, refs = refs[:count], refs[count:]
    cots, refs = refs[:count], refs[count:]
    preds, series_grad = refs[:count], refs[count]
    sg = sigma_row[...]
    ct = center_row[...]
    st = states[...]
    dim = st.shape[1]
    row_c, row_s = 0.0, 0.0
    for r in range(count):
        raw = dot_nt(mats[r][...], hid[...]) + dot_nt(short[r][:, :dim], st) + short[r][:, dim:dim + 1].astype(f32)
        preds[r][...] = (raw * sg + ct).astype(preds[r].dtype)
        c = cots[r][...].astype(f32)
        row_c = row_c + jnp.sum(c, axis=0, keepdims=True)
        row_s = row_s + jnp.sum(c * raw, axis=0, keepdims=True)
    observed = mask[...].astype(f32)
    series = samples.shape[0]
    first, cnt, center, offset, spread, sigma = series_stats(samples[...], observed, patch)
    out_c = series_column(row_c, series)
    out_s = series_column(row_s, series)
    og = observed * gscaled[...]
    g_center = out_c - jnp.sum(og, axis=1, keepdims=True) / sigma
    g_sigma = out_s - jnp.sum(og * offset, axis=1, keepdims=True) / (sigma * sigma)
    g_spread = jnp.where(spread > 1.0, g_sigma * 0.5 / sigma, 0.0)
    g_center = g_center - g_spread * 2.0 * jnp.sum(first * offset, axis=1, keepdims=True) / cnt
    series_grad[...] = og / sigma + g_spread * 2.0 * first * offset / cnt + g_center * first / cnt


def place_kernel(count, *refs):
    preds, out = refs[:count], refs[count]
    rows = preds[0].shape[1]
    narrow = lax.axis_index("narrow")
    for r in range(count):
        out[:, pl.ds(pl.multiple_of((narrow ^ r) * rows, 128), rows)] = preds[r][...].astype(f32)


def added(a, b):
    return (a.astype(f32) + b.astype(f32)).astype(bf)


def add_core_kernel(keep, got, a0, a1, b0, b1):
    cut = a0.shape[1]
    n = keep.shape[0] // 2
    for k in range(2 * n):
        v = added(keep[k], got[k])
        (a0, a1)[k // n][k % n] = v[:cut]
        (b0, b1)[k // n][k % n] = v[cut:]


def add_pair_kernel(a, a_got, b, b_got, a0, a1, b0, b1):
    n = a.shape[0] // 2
    for k in range(2 * n):
        (a0, a1)[k // n][k % n] = added(a[k], a_got[k])
        (b0, b1)[k // n][k % n] = added(b[k], b_got[k])


def add_merge_kernel(a, a_got, b, b_got, *outs):
    n, cut = outs[0].shape[0], a.shape[1]
    for i, o in enumerate(outs):
        for k in range(n):
            o[k, :cut] = added(a[i * n + k], a_got[i * n + k])
            o[k, cut:] = added(b[i * n + k], b_got[i * n + k])


def add_split_kernel(v, got, *outs):
    n = outs[0].shape[0]
    for i, o in enumerate(outs):
        o[...] = added(v[i * n:i * n + n], got[i * n:i * n + n])


def join_split_kernel(cut, here, got, a, b):
    n = here.shape[0]
    for k, v in enumerate((here, got)):
        a[k * n:k * n + n] = v[:, :cut]
        b[k * n:k * n + n] = v[:, cut:]


def join_kernel(*refs):
    ins, out = refs[:-1], refs[-1]
    n = ins[0].shape[0]
    for k, v in enumerate(ins):
        out[k * n:k * n + n] = v[...]


def join_pair_kernel(a, a_got, b, b_got, a_out, b_out):
    n = a.shape[0]
    for k, (v, w) in enumerate(((a, b), (a_got, b_got))):
        a_out[k * n:k * n + n] = v[...]
        b_out[k * n:k * n + n] = w[...]


def join_merge_kernel(a, a_got, b, b_got, out):
    n, cut = a.shape[0], a.shape[1]
    for k, (v, w) in enumerate(((a, b), (a_got, b_got))):
        out[k * n:k * n + n, :cut] = v[...]
        out[k * n:k * n + n, cut:] = w[...]


def xor_send(v, mask, total):
    return lax.ppermute(v, AXES, [(i, i ^ mask) for i in range(total)])


class Flow:
    def __init__(self, chain, count, total, bits, rest, cut, keep, send, name, head=False):
        self.chain, self.count, self.total, self.rest, self.cut, self.head = chain, count, total, rest, cut, head
        self.core, self.x, self.y, self.z1, self.z0 = bits
        self.rows = keep.shape[1]
        self.name = name
        self.held = [keep, self.to(send, self.core)]

    def to(self, v, mask):
        with jax.named_scope(self.name + str(mask)):
            return xor_send(v, mask, self.total)

    def shapes(self, n):
        return [((n, self.cut, 128), bf), ((n, self.rows - self.cut, 128), bf)]

    def run(self, kernel, outs, args):
        return self.chain(kernel, outs, args, limit=4)

    def add_core(self):
        a, b = self.shapes(8)
        a0, a1, b0, b1 = self.run(add_core_kernel, [a, a, b, b], self.held)
        self.held = [a0, self.to(a1, self.x), b0, self.to(b1, self.y)]

    def add_first(self):
        a, b = self.shapes(4)
        a0, a1, b0, b1 = self.run(add_pair_kernel, [a, a, b, b], self.held)
        self.held = [a0, self.to(a1, self.y), b0, self.to(b1, self.x)]

    def add_second(self):
        parts = self.run(add_merge_kernel, [((2, self.rows, 128), bf)] * 2, self.held)
        self.held = [parts[0], self.to(parts[1], self.z0)]

    def add_z(self):
        parts = self.run(add_split_kernel, [((1, self.rows, 128), bf)] * 2, self.held)
        self.held = [parts[0], self.to(parts[1], self.z1)]

    def add_last(self):
        (own,) = self.run(add_split_kernel, [((1, self.rows, 128), bf)], self.held)
        for m in self.rest:
            own = own + self.to(own, m)
        self.held = [own, self.to(own, self.z1)]

    def join_last(self):
        (v,) = self.run(join_kernel, [((2, self.rows, 128), bf)], self.held)
        self.held = [v, self.to(v, self.z0)]

    def join_z(self):
        if self.head:
            (v,) = self.run(join_kernel, [((4, self.rows, 128), bf)], self.held)
            self.held = [v, self.to(v, self.y)]
        else:
            a, b = self.run(functools.partial(join_split_kernel, self.cut), self.shapes(4), self.held)
            self.held = [a, self.to(a, self.y), b, self.to(b, self.x)]

    def join_first(self):
        if self.head:
            (v,) = self.run(join_kernel, [((8, self.rows, 128), bf)], self.held)
            self.held = [v, self.to(v, self.core)]
        else:
            a, b = self.run(join_pair_kernel, self.shapes(8), self.held)
            self.held = [a, self.to(a, self.x), b, self.to(b, self.y)]

    def join_second(self):
        (v,) = self.run(join_merge_kernel, [((16, self.rows, 128), bf)], self.held)
        self.held = [v, self.to(v, self.core)]


def assemble(refs, scr):
    k = 0
    for a in refs:
        scr[k:k + a.shape[0]] = a[...]
        k += a.shape[0]


def slab(scr, index, at):
    return scr[index, at:at + 48, :].astype(f32)


def vectors(tmp, row, outs):
    for o in outs:
        n = o.shape[0]
        for j in range(0, n, 128):
            o[pl.ds(j, 128)] = tmp[row]
            row += 1


def unpack_columns(count, masks, here, there, w, skip, bias, scr, tmp):
    me = me_of(masks, count)
    assemble((here, there), scr)
    cols, width = w.shape
    for b in range(width // 128):
        w[:, 128 * b:128 * b + 128] = scr[b ^ me].astype(f32)
    for i in range(skip.shape[1] // 128):
        skip[:, 128 * i:128 * i + 128] = scr[(width // 128 + i) ^ me].astype(f32)
    tmp[...] = scr[15 ^ me].astype(f32)
    bias[...] = jnp.concatenate([tmp[i:i + 1, :] for i in range(-(-cols // 128))], axis=1)[0, :cols]


def unpack_ffn(count, masks, here, there, inner, up, down, bias, gain, scr, tmp):
    me_a, me_b = (me_of(m, count) for m in masks)
    assemble((here, there), scr)
    for b in range(32):
        a_at, b_at = b ^ me_a, b ^ me_b
        j, i = b // 8, b % 8
        rows = slice(48 * i, 48 * i + 48)
        for k in range(3):
            cols = slice(TILE * j + 128 * k, TILE * j + 128 * k + 128)
            inner[rows, cols] = slab(scr, a_at, 48 * k)
            up[rows, cols] = slab(scr, a_at, 160) if k == 0 else slab(scr, b_at, 208 + 48 * (k - 1))
            down[48 * b:48 * b + 48, 128 * k:128 * k + 128] = slab(scr, b_at, 304 + 48 * k)
    tmp[...] = scr[me_a, 144:160, :].astype(f32)
    vectors(tmp, 0, (bias, gain))


def unpack_tokens(count, masks, here, there, gq, gk, gv, wo, out, tin, skip, bin_, bout, gain, scr, tmp):
    me_a, me_b = (me_of(m, count) for m in masks)
    assemble((here, there), scr)
    for b in range(32):
        a_at, b_at = b ^ me_a, b ^ me_b
        j, i = b // 8, b % 8
        tmp[16 * b:16 * b + 16, :] = scr[a_at, 144:160, :].astype(f32)
        for k in range(3):
            c = TILE * j + 128 * k
            (gq, gk, gv)[c // 512][48 * i:48 * i + 48, c % 512:c % 512 + 128] = slab(scr, a_at, 48 * k)
            out[48 * b:48 * b + 48, 128 * k:128 * k + 128] = slab(scr, b_at, 160 + 48 * k)
            wo[16 * b:16 * b + 16, 128 * k:128 * k + 128] = scr[b_at, 304 + 16 * k:320 + 16 * k, :].astype(f32)
    for c in range(12):
        tin[:, 128 * c:128 * c + 128] = tmp[32 * c:32 * c + 32, :]
    for i in range(3):
        skip[:, 128 * i:128 * i + 128] = tmp[384 + 32 * i:416 + 32 * i, :]
    vectors(tmp, 480, (bin_, bout, gain))


def per_device(wide, count, signal_samples, present_mask, wi, bi, wfin, wskip, bfin, gain_one, wq, wk, wv, wm,
               gain_two, we, wc, wri, bri, whz, wrs, bro, cotangent):
    series, points = signal_samples.shape
    patch = wi.shape[0] // 2
    rows = series * (points // patch)
    dim, width = wri.shape
    cols = whz.shape[1]
    inner = wq.shape[1]
    total = wide * count
    X, CORE, Y, Z0, Z1 = 1, count, 2 * count, 4 * count, 8 * count
    bits = (CORE, X, Y, Z1, Z0)
    narrow_rest = [1 << i for i in range(1, count.bit_length() - 1)]
    wide_rest = [count << i for i in range(4, wide.bit_length() - 1)]
    masks = [[CORE, X, Y, Z0, Z1], [CORE, Y, X, Z0, Z1]]
    column_masks = [CORE, Y, Z0, Z1]
    chain = Chain()
    vmem = pltpu.VMEM

    whz_t, wrs_t, cot_t = whz.T, wrs.T, cotangent.T
    packed = (width + dim + 128) // 2
    prepared = chain(
        functools.partial(prepare_kernel, count, rows),
        [((cols, rows), bf)] * (count - 1) + [((cols, rows), f32), ((cols, packed), bf), ((cols, dim + 128), bf)],
        [bro], raw=[cot_t, whz_t, wrs_t],
        scratch=[vmem((max(count - 1, 1), cols, rows), f32), vmem((cols, width // 2), bf), vmem((cols, dim), bf),
                 pltpu.SemaphoreType.DMA((count + 2,))], limit=24)
    own_cot, mine, short = prepared[count - 1:]
    cots = [own_cot] + [xor_send(prepared[r - 1], r, total) for r in range(1, count)]
    far = [xor_send(mine, r, total) for r in range(1, count)]

    weights = [wi, wfin, wskip, wq, wk, wv, wm, we, wc, wri, whz_t]
    out = chain(
        functools.partial(tokens_kernel, patch),
        [((rows, 2 * patch), bf), ((rows, width), bf), ((rows, width), bf), ((rows, dim), f32), ((rows, dim), bf),
         ((rows, 3 * inner), bf), ((1, rows), f32), ((1, rows), f32)] + [(w.shape, bf) for w in weights],
        [signal_samples, present_mask, bi, bfin, gain_one], raw=weights,
        scratch=[pltpu.SemaphoreType.DMA((len(weights),))])
    patches, hid1, d1, embed, normed1, qkv, sigma, center = out[:8]
    wi, wfin, wskip, wq, wk, wv, wm, we, wc, wri, whz_t = out[8:]

    probs, mixed = chain(attend_kernel, [((2 * series, 32, 128), f32), ((rows, inner), bf)], [qkv])
    middle, normed2, hid2, d2, states, hidh, dh = chain(
        ffn_kernel,
        [((rows, dim), f32), ((rows, dim), bf), ((rows, width), bf), ((rows, width), bf), ((rows, dim), bf),
         ((rows, width), bf), ((rows, width), bf)],
        [embed, mixed, wm, gain_two, we, wc, wri, bri])

    cut = first_rows(cols)
    groups = max(count // 2, 1)

    def columns():
        out = chain(
            functools.partial(columns_kernel, count, column_masks), [((16, cols, 128), bf)] * (2 * groups),
            [states, hidh, sigma] + cots,
            scratch=[vmem((cols, 128), f32)] + [vmem((32, n, 128), bf) for n in (cut, cols - cut)] * groups, limit=24)
        first = list(out[:2])
        for i in range(1, groups):
            for k in range(2):
                first[k] = first[k] + xor_send(out[2 * i + k], 2 * i, total)
        return Flow(chain, count, total, bits, wide_rest, cut, *first, "columns", head=True)

    def gate():
        out = []
        for v in far:
            (v,) = chain(gate_kernel, [(v.shape, bf)], [v], limit=4)
            out += [v, xor_send(v, CORE, total)]
        return out

    def head():
        out = chain(
            functools.partial(head_kernel, count),
            [((rows, dim), bf), ((rows, width), bf), ((1, width), f32)] + [((cols, width), bf)] * (count - 1)
            + [((cols, dim + 128), bf)] * (count - 1),
            [dh, sigma, wri] + cots + [whz_t] + far_both + [short])
        return out[0], out[1], out[2], [whz_t] + out[3:2 + count], [short] + out[2 + count:]

    def ffn_back():
        gmiddle, keep, send = chain(
            functools.partial(ffn_back_kernel, count, masks), [((rows, dim), bf)] + [((16, 448, 128), bf)] * 2,
            [gstates, states, gpre, sums, hid2, d2, normed2, middle, wc, we, gain_two],
            scratch=[vmem((32, 208, 128), bf), vmem((32, 240, 128), bf), vmem((16, 128), f32)])
        return gmiddle, Flow(chain, count, total, bits, narrow_rest + wide_rest, 208, keep, send, "ffn")

    def attend_back():
        return chain(attend_back_kernel, [((rows, 3 * inner), bf)], [gmiddle, wm, qkv, probs],
                     scratch=[vmem((rows, inner), bf), vmem(probs.shape, f32), vmem(probs.shape, bf)])[0]

    def project_back():
        return chain(
            functools.partial(project_back_kernel, count, masks),
            [((rows, dim), bf), ((1, dim), f32), ((32, 144, 128), bf), ((32, 48, 128), bf)],
            [gqkv, gmiddle, mixed, normed1, embed, wq, wk, wv, gain_one])

    def tokens_back():
        gscaled, keep, send = chain(
            functools.partial(tokens_back_kernel, count, masks, patch),
            [((series, points), f32)] + [((16, 352, 128), bf)] * 2,
            [gembed, hid1, d1, patches, wfin, wskip, wi, gg1, part_a, part_b],
            scratch=[vmem((32, 16, 128), bf), vmem((32, 144, 128), bf), vmem((512, 128), f32)])
        return gscaled, Flow(chain, count, total, bits, narrow_rest + wide_rest, 160, keep, send, "tokens")

    def forecast():
        out = chain(
            functools.partial(forecast_kernel, count, patch),
            [((cols, rows), f32)] + [((cols, rows), bf)] * (count - 1) + [((series, points), f32)],
            [signal_samples, present_mask, gscaled, hidh, states, sigma, center] + mats + shorts + cots)
        return [out[0]] + [xor_send(out[r], r, total) for r in range(1, count)], out[count]

    def place():
        return chain(functools.partial(place_kernel, count), [((cols, count * rows), f32)], preds)[0]

    def finish_columns():
        return chain(functools.partial(unpack_columns, count, column_masks),
                     [((cols, width), f32), ((cols, dim), f32), ((cols,), f32)],
                     one.held, scratch=[vmem((16, cols, 128), bf), vmem((cols, 128), f32)], limit=24)

    def finish_ffn():
        return chain(functools.partial(unpack_ffn, count, masks),
                     [((dim, width), f32)] * 2 + [((width, dim), f32), ((width,), f32), ((dim,), f32)], two.held,
                     scratch=[vmem((32, 448, 128), bf), vmem((16, 128), f32)], limit=24)

    def finish_tokens():
        return chain(
            functools.partial(unpack_tokens, count, masks),
            [((dim, inner), f32)] * 3 + [((inner, dim), f32), ((width, dim), f32), ((2 * patch, width), f32),
                                         ((2 * patch, dim), f32), ((width,), f32), ((dim,), f32), ((dim,), f32)],
            three.held, scratch=[vmem((32, 352, 128), bf), vmem((512, 128), f32)], limit=24)

    one = columns()
    far_both = gate()
    gstates, gpre, sums, mats, shorts = head()
    one.add_core()
    gmiddle, two = ffn_back()
    gqkv = attend_back()
    one.add_first()
    two.add_core()
    gembed, gg1, part_a, part_b = project_back()
    gscaled, three = tokens_back()
    one.add_second()
    preds, g_series = forecast()
    three.add_core()
    two.add_first()
    one.add_z()
    three.add_first()
    two.add_second()
    one.add_last()
    three.add_second()
    one.join_last()
    two.add_z()
    one.join_z()
    three.add_z()
    two.add_last()
    three.add_last()
    one.join_first()
    prediction = place()
    two.join_last()
    three.join_last()
    columns_out = finish_columns()
    two.join_z()
    three.join_z()
    two.join_first()
    three.join_first()
    two.join_second()
    three.join_second()
    ffn_out = finish_ffn()
    tokens_out = finish_tokens()
    g_hw, g_hs, g_hb = columns_out
    g_hiw, g_up, g_down, g_hib, g_g2 = ffn_out
    g_q, g_k, g_v, g_wo, g_to, g_ti, g_ts, g_tib, g_tob, g_g1 = tokens_out
    return (prediction.T, g_series, g_ti, g_tib, g_to, g_ts, g_tob, g_g1, g_q, g_k, g_v, g_wo, g_g2, g_up, g_down,
            g_hiw, g_hib, g_hw.T, g_hs.T, g_hb)


def solution(mesh):
    wide, count = mesh.shape["wide"], mesh.shape["narrow"]
    both = P(("wide", "narrow"), None)
    return jax.shard_map(
        functools.partial(per_device, wide, count),
        mesh=mesh,
        in_specs=(both, both) + (P(),) * 15 + (P(None, "narrow"), P(None, "narrow"), P("narrow"), P("wide", "narrow")),
        out_specs=(P("wide", "narrow"), both) + (P(),) * 15
        + (P(None, "narrow"), P(None, "narrow"), P("narrow")),
        check_vma=False,
    )
```

```python
import functools

import jax
import jax.numpy as jnp
from jax import lax
from jax.experimental import pallas as pl
from jax.experimental.pallas import tpu as pltpu
from jax.sharding import PartitionSpec as P

HEADS = 8
HEAD_DIM = 64
EPS = 1e-06
SCALE = HEAD_DIM ** (-0.5)
bf = jnp.bfloat16
f32 = jnp.float32
TILE = 384
AXES = ("wide", "narrow")
MIB = 1 << 20
COSTS = {25: 10000000000, 31: 20000000000, 20: 6000000000, 12: 30000000000, 19: 30000000000, 35: 30000000000, 27: 30000000000, 5: 10000000000, 16: 3000000000, 21: 6000000000, 28: 3000000000, 23: 30000000000, 29: 15000000000}


def dot(a, b):
    return lax.dot_general(a, b, (((1,), (0,)), ((), ())), preferred_element_type=f32)


def dot_nt(a, b):
    return lax.dot_general(a, b, (((1,), (1,)), ((), ())), preferred_element_type=f32)


def dot_tn(a, b):
    return lax.dot_general(a, b, (((0,), (0,)), ((), ())), preferred_element_type=f32)


class Chain:
    def __init__(self):
        self.last = None
        self.calls = 0

    def __call__(self, kernel, outs, args, scratch=(), limit=16, raw=()):
        vmem = pl.BlockSpec(memory_space=pltpu.VMEM)
        hbm = pl.BlockSpec(memory_space=pl.ANY)
        args, raw = list(args), [pltpu.with_memory_space_constraint(v, pltpu.HBM) for v in raw]
        deps = [] if self.last is None or any(a is self.last for a in args) else [self.last]
        n, d = len(args) + len(raw), len(deps)
        cost = COSTS.get(self.calls, 1000)
        self.calls += 1

        def body(*refs):
            kernel(*refs[:n], *refs[n + d:])

        name = getattr(kernel, "__name__", None) or kernel.func.__name__
        res = list(pl.pallas_call(
            body,
            name=name,
            out_shape=[jax.ShapeDtypeStruct(s, d) for s, d in outs],
            in_specs=[vmem] * len(args) + [pl.BlockSpec(memory_space=pltpu.HBM)] * len(raw) + [hbm] * d,
            out_specs=[vmem] * len(outs),
            scratch_shapes=list(scratch),
            cost_estimate=pl.CostEstimate(flops=cost, bytes_accessed=1000, transcendentals=0),
            compiler_params=pltpu.CompilerParams(vmem_limit_bytes=limit * MIB),
        )(*args, *raw, *deps))
        self.last = min(res, key=lambda r: r.size)
        return res


def silu_parts(v):
    s = 0.5 * jnp.tanh(0.5 * v) + 0.5
    h = v * s
    return h, s + h * (1.0 - s)


def iota(shape, dim):
    return lax.broadcasted_iota(jnp.int32, shape, dim)


def series_stats(samples, observed, patch):
    first = jnp.where(iota(samples.shape, 1) < patch, observed, 0.0)
    count = jnp.maximum(jnp.sum(first, axis=1, keepdims=True), 1.0)
    center = jnp.sum(first * samples, axis=1, keepdims=True) / count
    offset = samples - center
    spread = jnp.sum(first * offset * offset, axis=1, keepdims=True) / count
    sigma = jnp.sqrt(jnp.maximum(spread, 1.0))
    return first, count, center, offset, spread, sigma


def rms(v):
    return lax.rsqrt(jnp.mean(v * v, axis=-1, keepdims=True) + EPS)


def norm_back(g, v, gain):
    r = rms(v)
    u = v * r
    w = g * gain
    grad_gain = jnp.sum(g * u, axis=0, keepdims=True)
    return r * (w - u * jnp.mean(w * u, axis=-1, keepdims=True)), grad_gain


def token_row(v, rows):
    series = v.shape[0]
    own = iota((series, rows), 1) // (rows // series) == iota((series, rows), 0)
    return jnp.sum(jnp.where(own, v, 0.0), axis=0, keepdims=True)


def series_column(v, series):
    rows = v.shape[1]
    own = iota((series, rows), 1) // (rows // series) == iota((series, rows), 0)
    return jnp.sum(jnp.where(own, v, 0.0), axis=1, keepdims=True)


def me_of(masks, count):
    index = lax.axis_index("wide") * count + lax.axis_index("narrow")
    out = jnp.int32(0)
    for m in masks:
        out = out * 2 + (index // m) % 2
    return out


def prepare_kernel(count, rows, bias, cot, whz, wrs, *refs):
    cots, (own, mine, short) = refs[:count - 1], refs[count - 1:count + 2]
    wide_cots, half, shortcut, sems = refs[count + 2:]
    narrow = lax.axis_index("narrow")
    core = lax.axis_index("wide") % 2
    width, dim = half.shape[1], shortcut.shape[1]

    def tokens(r):
        return cot.at[:, pl.ds(pl.multiple_of((narrow ^ r) * rows, 128), rows)]

    copies = [
        pltpu.make_async_copy(whz.at[:, pl.ds(pl.multiple_of(core * width, 128), width)], half, sems.at[0]),
        pltpu.make_async_copy(wrs, shortcut, sems.at[1]),
        pltpu.make_async_copy(tokens(0), own, sems.at[2]),
    ] + [pltpu.make_async_copy(tokens(r), wide_cots.at[r - 1], sems.at[2 + r]) for r in range(1, count)]
    for c in copies:
        c.start()
    for c in copies[:2]:
        c.wait()
    short[:, :dim] = shortcut[...]
    short[:, dim:] = dot_tn(bias[...].astype(f32)[None, :].astype(bf), jnp.ones((1, 128), bf)).astype(bf)
    mine[:, :width] = half[...]
    part = (dim + 128) // 2
    mine[:, width:] = short[:, pl.ds(pl.multiple_of(core * part, 128), part)]
    for c in copies[2:]:
        c.wait()
    for r in range(1, count):
        cots[r - 1][...] = wide_cots[r - 1].astype(bf)


def gate_kernel(v, out):
    out[...] = v[...]


def tokens_kernel(patch, *refs):
    samples, mask, bi, bfin, gain = refs[:5]
    hbm = refs[5:16]
    patches, hid, dhid, embed, normed, qkv, sigma_row, center_row = refs[16:24]
    vmem, sems = refs[24:35], refs[35]
    copies = [pltpu.make_async_copy(h, v, sems.at[i]) for i, (h, v) in enumerate(zip(hbm, vmem))]
    for c in copies:
        c.start()
    wi, wfin, wskip, wq, wk, wv = vmem[:6]
    series, points = samples.shape
    tokens = points // patch
    rows = series * tokens
    observed = mask[...].astype(f32)
    _, _, center, offset, _, sigma = series_stats(samples[...], observed, patch)
    sigma_row[...] = token_row(sigma, rows)
    center_row[...] = token_row(center, rows)
    scaled = (observed * offset / sigma).astype(bf)
    spread_rows = (iota((rows, series), 0) // tokens == iota((rows, series), 1)).astype(f32).astype(bf)
    own = (iota((rows, points), 1) // patch == iota((rows, points), 0) % tokens).astype(f32)
    col = iota((points, 2 * patch), 0) % patch
    lane = iota((points, 2 * patch), 1)
    fold_s = (col == lane).astype(f32).astype(bf)
    fold_o = (col + patch == lane).astype(f32).astype(bf)
    es = (dot(spread_rows, scaled) * own).astype(bf)
    eo = (dot(spread_rows, observed.astype(bf)) * own).astype(bf)
    p = (dot(es, fold_s) + dot(eo, fold_o)).astype(bf)
    patches[...] = p
    for c in copies[:3]:
        c.wait()
    acc = dot(p, wskip[...]) + bfin[...][None, :]
    for j in range(0, wi.shape[1], TILE):
        t = slice(j, j + TILE)
        h, d = silu_parts(dot(p, wi[:, t]) + bi[t][None, :])
        h = h.astype(bf)
        hid[:, t] = h
        dhid[:, t] = d.astype(bf)
        acc = acc + dot(h, wfin[t, :])
    embed[...] = acc
    n = (acc * rms(acc) * gain[...][None, :]).astype(bf)
    normed[...] = n
    inner = wq.shape[1]
    for i, w in enumerate((wq, wk, wv)):
        copies[3 + i].wait()
        qkv[:, i * inner:(i + 1) * inner] = dot(n, w[...]).astype(bf)
    for c in copies[6:]:
        c.wait()


def block_mask():
    return (iota((128, 256), 0) // 32 == iota((128, 256), 1) // 64).astype(f32).astype(bf)


def spread_heads(v, keep):
    return jnp.concatenate([v] * 4, axis=0) * keep


def pick_heads(v):
    head = iota((32, 256), 1) // 64
    out = v[0:32]
    for h in range(1, 4):
        out = jnp.where(head == h, v[32 * h:32 * h + 32], out)
    return out


def pairs(rows):
    for i in range(rows // 16):
        yield i, slice(32 * (i // 2), 32 * (i // 2) + 32), 256 * (i % 2)


def attend_kernel(qkv, probs, mixed):
    keep = block_mask()
    inner = HEADS * HEAD_DIM
    rows = qkv.shape[0]
    for i, s, c in pairs(rows):
        q = spread_heads(qkv[s, c:c + 256], keep)
        probs[i] = dot_nt(qkv[s, inner + c:inner + c + 256], q)
    for i in range(0, rows // 16, 4):
        v = probs[i:i + 4] * SCALE
        e = jnp.exp(v - jnp.max(v, axis=1, keepdims=True))
        probs[i:i + 4] = e / jnp.sum(e, axis=1, keepdims=True)
    for i, s, c in pairs(rows):
        v = qkv[s, 2 * inner + c:2 * inner + c + 256]
        mixed[s, c:c + 256] = pick_heads(dot_tn(probs[i].astype(bf), v)).astype(bf)


def ffn_kernel(embed, mixed, wm, gain, we, wc, wri, bri, middle, normed, hid, dhid, states, hidh, dh):
    mid = embed[...] + dot(mixed[...], wm[...])
    middle[...] = mid
    n = (mid * rms(mid) * gain[...][None, :]).astype(bf)
    normed[...] = n
    acc = mid
    for j in range(0, we.shape[1], TILE):
        t = slice(j, j + TILE)
        h, d = silu_parts(dot(n, we[:, t]))
        h = h.astype(bf)
        hid[:, t] = h
        dhid[:, t] = d.astype(bf)
        acc = acc + dot(h, wc[t, :])
    st = acc.astype(bf)
    states[...] = st
    for j in range(0, wri.shape[1], TILE):
        t = slice(j, j + TILE)
        h, d = silu_parts(dot(st, wri[:, t]) + bri[t][None, :])
        hidh[:, t] = h.astype(bf)
        dh[:, t] = d.astype(bf)


HEAD_ORDER = "pqxy"
FFN_PARTS = [
    ("xypq", [("down", 0), ("down", 1), ("down", 2), ("up", 0), ("up", 1)]),
    ("yqxp", [("inner", 0), ("inner", 1), ("inner", 2), ("up", 2), ("vector", 0)]),
]
TOKEN_PARTS = [
    ("xypq", [("final", 0), ("final", 1), ("final", 2), ("small", 0)]),
    ("yxpq", [("attention", 0), ("attention", 1), ("attention", 2), ("merge", 0), ("merge", 1), ("merge", 2)]),
]
SLAB_ROWS = {"merge": 16, "vector": 16, "small": 16}


def part_rows(items):
    return sum(SLAB_ROWS.get(name, 48) for name, _ in items)


def layout(parts):
    out = {}
    for p, (_, items) in enumerate(parts):
        at = 0
        for item in items:
            out[item] = p, at
            at += SLAB_ROWS.get(item[0], 48)
    return out


def sizes(parts):
    return [(part_rows(items), order) for order, items in parts]


def put_matrix(scrs, mes, where, name, tile, value):
    value = value.astype(bf)
    for k in range(3):
        p, at = where[name, k]
        for i in range(8):
            scrs[p][(8 * tile + i) ^ mes[p], at:at + 48, :] = value[48 * i:48 * i + 48, 128 * k:128 * k + 128]


def ship(sources, keep, send):
    at = 0
    for v, first, rows in sources:
        n = v.shape[0] // 2
        keep[:, at:at + rows] = v[:n, first:first + rows]
        send[:, at:at + rows] = v[n:, first:first + rows]
        at += rows


def index_bits(index, count):
    return [(index // (1 << (count - 1 - k))) % 2 for k in range(count)]


def rows_of(tmp, row, v):
    for j in range(0, v.shape[1], 128):
        tmp[row:row + 1, :] = v[:, j:j + 128]
        row += 1
    return row


def columns_kernel(count, masks, *refs):
    states, hidh, sigma = refs[:3]
    cots, refs = refs[3:3 + count], refs[3 + count:]
    groups = max(count // 2, 1)
    outs, (tmp, *scrs) = refs[:2 * groups], refs[2 * groups:]
    me = me_of(masks, count)
    st = states[...]
    width = hidh.shape[1]
    cols = tmp.shape[0]
    for r in range(count):
        turned = (cots[r][...].astype(f32) * sigma[...]).astype(bf)
        scr = scrs[r // 2]

        def put(c, v):
            core, *others = index_bits(c ^ me, 4)
            at = core
            for axis in HEAD_ORDER:
                at = at * 2 + (r % 2 if axis == "x" else others.pop(0))
            scr[at] = v

        for j in range(0, width, TILE):
            v = dot(turned, hidh[:, j:j + TILE]).astype(bf)
            for i in range(TILE // 128):
                put(j // 128 + i, v[:, 128 * i:128 * i + 128])
        v = dot(turned, st).astype(bf)
        for i in range(st.shape[1] // 128):
            put(width // 128 + i, v[:, 128 * i:128 * i + 128])
        tmp[...] = jnp.zeros_like(tmp)
        bias = dot_nt(jnp.ones((8, turned.shape[1]), bf), turned)
        for row, j in enumerate(range(0, cols, 128)):
            n = min(128, cols - j)
            tmp[row:row + 1, 0:n] = bias[0:1, j:j + n]
        put(15, tmp[...].astype(bf))
    for i in range(groups):
        ship([(scrs[i], 0, cols)], *outs[2 * i:2 * i + 2])


def head_kernel(count, *refs):
    dh, sigma, wri = refs[:3]
    refs = refs[3:]
    cots, refs = refs[:count], refs[count:]
    whz, refs = refs[0], refs[1:]
    far, refs = refs[:2 * (count - 1)], refs[2 * (count - 1):]
    short, refs = refs[0], refs[1:]
    gstates, gpre, sums = refs[:3]
    mats, shorts = refs[3:2 + count], refs[2 + count:1 + 2 * count]
    width = wri.shape[1]
    dim = wri.shape[0]
    half, part = width // 2, (dim + 128) // 2
    core = lax.axis_index("wide") % 2
    for r in range(count - 1):
        for k, c in enumerate((core, 1 - core)):
            mats[r][:, pl.ds(pl.multiple_of(c * half, 128), half)] = far[2 * r + k][:, :half]
            shorts[r][:, pl.ds(pl.multiple_of(c * part, 128), part)] = far[2 * r + k][:, half:]
    mats = [whz] + list(mats)
    shorts = [short] + list(shorts)
    grads = [(c[...].astype(f32) * sigma[...]).astype(bf).T for c in cots]
    for j in range(0, width, TILE):
        t = slice(j, j + TILE)
        acc = dot(grads[0], mats[0][:, t])
        for r in range(1, count):
            acc = acc + dot(grads[r], mats[r][:, t])
        gp = (acc * dh[:, t].astype(f32)).astype(bf)
        gpre[:, t] = gp
        sums[:, t] = jnp.sum(gp.astype(f32), axis=0, keepdims=True)
    acc = dot_nt(gpre[...], wri[...])
    for r in range(count):
        acc = acc + dot(grads[r], shorts[r][:, :dim])
    gstates[...] = acc.astype(bf)


def ffn_back_kernel(count, masks, gstates, states, gpre, sums, hid, dhid, normed, middle, wc, we, gain,
                    gmiddle, keep, send, *scrs):
    *scrs, tmp = scrs
    mes = [me_of(m, count) for m in masks]
    where = layout(FFN_PARTS)
    g = gstates[...]
    nt = normed[...].T
    acc = None
    for j in range(4):
        t = slice(TILE * j, TILE * j + TILE)
        gp = (dot_nt(g, wc[t, :]) * dhid[:, t].astype(f32)).astype(bf)
        part = dot_nt(gp, we[:, t])
        acc = part if acc is None else acc + part
        put_matrix(scrs, mes, where, "up", j, dot(nt, gp))
        put_matrix(scrs, mes, where, "down", j, dot_tn(hid[:, t], g))
    back, gg = norm_back(acc, middle[...], gain[...][None, :])
    gmiddle[...] = (g.astype(f32) + back).astype(bf)
    st = states[...].T
    for j in range(4):
        put_matrix(scrs, mes, where, "inner", j, dot(st, gpre[:, TILE * j:TILE * j + TILE]))
    p, at = where["vector", 0]
    scrs[p][:, at:at + 16, :] = jnp.zeros((32, 16, 128), bf)
    tmp[...] = jnp.zeros_like(tmp)
    row = rows_of(tmp, 0, sums[...])
    rows_of(tmp, row, gg)
    scrs[p][mes[p], at:at + 16, :] = tmp[...].astype(bf)
    ship([(v, 0, v.shape[1]) for v in scrs], keep, send)


def attend_back_kernel(gmiddle, wm, qkv, probs, gqkv, gmix, gprobs, low):
    keep = block_mask()
    inner = HEADS * HEAD_DIM
    rows = qkv.shape[0]
    gmix[...] = dot_nt(gmiddle[...], wm[...]).astype(bf)
    for i, s, c in pairs(rows):
        g = spread_heads(gmix[s, c:c + 256], keep)
        gprobs[i] = dot_nt(qkv[s, 2 * inner + c:2 * inner + c + 256], g)
        gqkv[s, 2 * inner + c:2 * inner + c + 256] = dot(probs[i].astype(bf), g).astype(bf)
    for i in range(0, rows // 16, 4):
        p, g = probs[i:i + 4], gprobs[i:i + 4]
        low[i:i + 4] = (p * (g - jnp.sum(g * p, axis=1, keepdims=True))).astype(bf)
    for i, s, c in pairs(rows):
        ds = low[i]
        q = spread_heads(qkv[s, c:c + 256], keep)
        k = qkv[s, inner + c:inner + c + 256]
        gqkv[s, c:c + 256] = (pick_heads(dot_tn(ds, k)) * SCALE).astype(bf)
        gqkv[s, inner + c:inner + c + 256] = (dot(ds, q) * SCALE).astype(bf)


def project_back_kernel(count, masks, gqkv, gmiddle, mixed, normed, embed, wq, wk, wv, gain, gembed, ggain,
                        *scrs):
    mes = [me_of(m, count) for m in masks]
    where = layout(TOKEN_PARTS)
    inner = wq.shape[1]
    acc = dot_nt(gqkv[:, :inner], wq[...])
    acc = acc + dot_nt(gqkv[:, inner:2 * inner], wk[...])
    acc = acc + dot_nt(gqkv[:, 2 * inner:], wv[...])
    back, gg = norm_back(acc, embed[...], gain[...][None, :])
    ggain[...] = gg
    gm = gmiddle[...]
    gembed[...] = (gm.astype(f32) + back).astype(bf)
    nt = normed[...].T
    for j in range(4):
        put_matrix(scrs, mes, where, "attention", j, dot(nt, gqkv[:, TILE * j:TILE * j + TILE]))
    v = dot_tn(mixed[...], gm).astype(bf)
    for k in range(3):
        p, at = where["merge", k]
        for i in range(32):
            scrs[p][i ^ mes[p], at:at + 16, :] = v[16 * i:16 * i + 16, 128 * k:128 * k + 128]


def tokens_back_kernel(count, masks, patch, gembed, hid, dhid, patches, wfin, wskip, wi, gain_one, *refs):
    n = len(masks)
    earlier, (gscaled, keep, send), scrs, tmp = refs[:n], refs[n:n + 3], refs[n + 3:2 * n + 3], refs[-1]
    mes = [me_of(m, count) for m in masks]
    where = layout(TOKEN_PARTS)
    g = gembed[...]
    p = patches[...]
    pt = p.T
    tmp[...] = jnp.zeros_like(tmp)
    gpat = dot_nt(g, wskip[...])
    row = 480
    for j in range(4):
        t = slice(TILE * j, TILE * j + TILE)
        gp = (dot_nt(g, wfin[t, :]) * dhid[:, t].astype(f32)).astype(bf)
        gpat = gpat + dot_nt(gp, wi[:, t])
        v = dot(pt, gp)
        for i in range(3):
            c = 3 * j + i
            tmp[32 * c:32 * c + 32, :] = v[:, 128 * i:128 * i + 128]
        row = rows_of(tmp, row, jnp.sum(gp.astype(f32), axis=0, keepdims=True))
        put_matrix(scrs, mes, where, "final", j, dot_tn(hid[:, t], g))
    v = dot(pt, g)
    for i in range(3):
        tmp[384 + 32 * i:416 + 32 * i, :] = v[:, 128 * i:128 * i + 128]
    row = rows_of(tmp, row, jnp.sum(g.astype(f32), axis=0, keepdims=True))
    rows_of(tmp, row, gain_one[...])
    p, at = where["small", 0]
    for b in range(32):
        scrs[p][b ^ mes[p], at:at + 16, :] = tmp[16 * b:16 * b + 16].astype(bf)
    ship([((earlier if item[0] in ("attention", "merge") else scrs)[where[item][0]], where[item][1],
           SLAB_ROWS.get(item[0], 48)) for _, items in TOKEN_PARTS for item in items], keep, send)
    series, points = gscaled.shape
    tokens = points // patch
    rows = series * tokens
    lane = iota((2 * patch, points), 1) % patch
    fold = (iota((2 * patch, points), 0) == lane).astype(f32).astype(bf)
    own = (iota((rows, points), 1) // patch == iota((rows, points), 0) % tokens).astype(f32)
    high = gpat.astype(bf)
    low = (gpat - high.astype(f32)).astype(bf)
    full = (dot(high, fold) + dot(low, fold)) * own
    gscaled[...] = jnp.sum(full.reshape(series, tokens, points), axis=1)


def forecast_kernel(count, patch, *refs):
    samples, mask, gscaled, hid, states, sigma_row, center_row = refs[:7]
    refs = refs[7:]
    mats, refs = refs[:count], refs[count:]
    short, refs = refs[:count], refs[count:]
    cots, refs = refs[:count], refs[count:]
    preds, series_grad = refs[:count], refs[count]
    sg = sigma_row[...]
    ct = center_row[...]
    st = states[...]
    dim = st.shape[1]
    row_c, row_s = 0.0, 0.0
    for r in range(count):
        raw = dot_nt(mats[r][...], hid[...]) + dot_nt(short[r][:, :dim], st) + short[r][:, dim:dim + 1].astype(f32)
        preds[r][...] = (raw * sg + ct).astype(preds[r].dtype)
        c = cots[r][...].astype(f32)
        row_c = row_c + jnp.sum(c, axis=0, keepdims=True)
        row_s = row_s + jnp.sum(c * raw, axis=0, keepdims=True)
    observed = mask[...].astype(f32)
    series = samples.shape[0]
    first, cnt, center, offset, spread, sigma = series_stats(samples[...], observed, patch)
    out_c = series_column(row_c, series)
    out_s = series_column(row_s, series)
    og = observed * gscaled[...]
    g_center = out_c - jnp.sum(og, axis=1, keepdims=True) / sigma
    g_sigma = out_s - jnp.sum(og * offset, axis=1, keepdims=True) / (sigma * sigma)
    g_spread = jnp.where(spread > 1.0, g_sigma * 0.5 / sigma, 0.0)
    g_center = g_center - g_spread * 2.0 * jnp.sum(first * offset, axis=1, keepdims=True) / cnt
    series_grad[...] = og / sigma + g_spread * 2.0 * first * offset / cnt + g_center * first / cnt


def place_kernel(count, *refs):
    preds, out = refs[:count], refs[count]
    rows = preds[0].shape[1]
    narrow = lax.axis_index("narrow")
    for r in range(count):
        out[:, pl.ds(pl.multiple_of((narrow ^ r) * rows, 128), rows)] = preds[r][...].astype(f32)


def xor_send(v, mask, total):
    return lax.ppermute(v, AXES, [(i, i ^ mask) for i in range(total)])


def grouped(parts, level):
    groups = {}
    for p, (_, order) in enumerate(parts):
        groups.setdefault(order[level:], []).append(p)
    return list(groups.values())


def places(parts, groups):
    out = {}
    for g, members in enumerate(groups):
        at = 0
        for p in members:
            out[p] = g, at
            at += parts[p][0]
    return out


def add_kernel(parts, before, after, split, *refs):
    n_in = 2 * (max(g for g, _ in before.values()) + 1)
    ins, outs = refs[:n_in], refs[n_in:]
    n = ins[0].shape[0]
    half = n // split
    for p, (rows, _) in enumerate(parts):
        (g, a), (o, b) = before[p], after[p]
        for k in range(n):
            v = ins[2 * g][k, a:a + rows].astype(f32) + ins[2 * g + 1][k, a:a + rows].astype(f32)
            outs[split * o + k // half][k % half, b:b + rows] = v.astype(bf)


def join_kernel(parts, before, after, *refs):
    n_in = 2 * (max(g for g, _ in before.values()) + 1)
    ins, outs = refs[:n_in], refs[n_in:]
    n = ins[0].shape[0]
    for p, (rows, _) in enumerate(parts):
        (g, a), (o, b) = before[p], after[p]
        for k in range(2):
            outs[o][n * k:n * k + n, b:b + rows] = ins[2 * g + k][:, a:a + rows]


class Flow:
    def __init__(self, chain, total, bits, rest, parts, keep, send, name, head=False):
        self.chain, self.total, self.bits, self.rest, self.parts = chain, total, bits, rest, parts
        self.name, self.head = name, head
        self.whole = {p: (0, sum(r for r, _ in parts[:p])) for p in range(len(parts))}
        self.level, self.down, self.at = 0, True, self.whole
        self.held = [keep, self.to(send, bits["c"])]

    def to(self, v, mask):
        with jax.named_scope(self.name + str(mask)):
            return xor_send(v, mask, self.total)

    def shapes(self, groups, n):
        return [((n, sum(self.parts[p][0] for p in g), 128), bf) for g in groups]

    def axis(self, group, level):
        return self.parts[group[0]][1][level]

    def step(self):
        (self.add if self.down else self.join)()

    def add(self):
        n = self.held[0].shape[0]
        last = self.level == 4
        groups = grouped(self.parts, 3 if last else self.level)
        at = places(self.parts, groups)
        shapes = self.shapes(groups, n if last else n // 2)
        outs = self.chain(functools.partial(add_kernel, self.parts, self.at, at, 1 if last else 2),
                          shapes if last else [s for s in shapes for _ in range(2)], self.held, limit=4)
        self.at = at
        if not last:
            self.held = [v for g, (a, b) in zip(groups, zip(outs[::2], outs[1::2]))
                         for v in (a, self.to(b, self.bits[self.axis(g, self.level)]))]
            self.level += 1
            return
        for m in self.rest:
            outs = [v + self.to(v, m) for v in outs]
        self.down = False
        self.level = 3
        self.spread(groups, outs)

    def spread(self, groups, arrays):
        if self.head and self.axis(groups[0], self.level) == "x":
            self.level -= 1
        if self.level < 0:
            self.held = [v for a in arrays for v in (a, self.to(a, self.bits["c"]))]
            return
        self.held = [v for g, a in zip(groups, arrays) for v in (a, self.to(a, self.bits[self.axis(g, self.level)]))]

    def join(self):
        n = self.held[0].shape[0]
        self.level -= 1
        groups = grouped(self.parts, self.level) if self.level >= 0 else [list(range(len(self.parts)))]
        at = places(self.parts, groups)
        outs = self.chain(functools.partial(join_kernel, self.parts, self.at, at), self.shapes(groups, 2 * n),
                          self.held, limit=4)
        self.at = at
        self.spread(groups, outs)


def assemble(refs, scr):
    k = 0
    for a in refs:
        scr[k:k + a.shape[0]] = a[...]
        k += a.shape[0]


def finder(scr, parts, masks, count):
    where, mes = layout(parts), [me_of(m, count) for m in masks]
    base = [sum(part_rows(items) for _, items in parts[:p]) for p in range(len(parts))]

    def find(name, k, b):
        p, at = where[name, k]
        at += base[p]
        return scr[b ^ mes[p], at:at + SLAB_ROWS.get(name, 48), :].astype(f32)

    return find


def vectors(tmp, row, outs):
    for o in outs:
        n = o.shape[0]
        for j in range(0, n, 128):
            o[pl.ds(j, 128)] = tmp[row]
            row += 1


def unpack_columns(count, masks, here, there, w, skip, bias, scr, tmp):
    me = me_of(masks, count)
    assemble((here, there), scr)
    cols, width = w.shape
    for b in range(width // 128):
        w[:, 128 * b:128 * b + 128] = scr[b ^ me].astype(f32)
    for i in range(skip.shape[1] // 128):
        skip[:, 128 * i:128 * i + 128] = scr[(width // 128 + i) ^ me].astype(f32)
    tmp[...] = scr[15 ^ me].astype(f32)
    bias[...] = jnp.concatenate([tmp[i:i + 1, :] for i in range(-(-cols // 128))], axis=1)[0, :cols]


def unpack_ffn(count, masks, here, there, inner, up, down, bias, gain, scr, tmp):
    assemble((here, there), scr)
    find = finder(scr, FFN_PARTS, masks, count)
    for b in range(32):
        j, i = b // 8, b % 8
        rows = slice(48 * i, 48 * i + 48)
        for k in range(3):
            cols = slice(TILE * j + 128 * k, TILE * j + 128 * k + 128)
            inner[rows, cols] = find("inner", k, b)
            up[rows, cols] = find("up", k, b)
            down[48 * b:48 * b + 48, 128 * k:128 * k + 128] = find("down", k, b)
    tmp[...] = find("vector", 0, 0)
    vectors(tmp, 0, (bias, gain))


def unpack_tokens(count, masks, here, there, gq, gk, gv, wo, out, tin, skip, bin_, bout, gain, scr, tmp):
    assemble((here, there), scr)
    find = finder(scr, TOKEN_PARTS, masks, count)
    for b in range(32):
        j, i = b // 8, b % 8
        tmp[16 * b:16 * b + 16, :] = find("small", 0, b)
        for k in range(3):
            c = TILE * j + 128 * k
            (gq, gk, gv)[c // 512][48 * i:48 * i + 48, c % 512:c % 512 + 128] = find("attention", k, b)
            out[48 * b:48 * b + 48, 128 * k:128 * k + 128] = find("final", k, b)
            wo[16 * b:16 * b + 16, 128 * k:128 * k + 128] = find("merge", k, b)
    for c in range(12):
        tin[:, 128 * c:128 * c + 128] = tmp[32 * c:32 * c + 32, :]
    for i in range(3):
        skip[:, 128 * i:128 * i + 128] = tmp[384 + 32 * i:416 + 32 * i, :]
    vectors(tmp, 480, (bin_, bout, gain))


def per_device(wide, count, signal_samples, present_mask, wi, bi, wfin, wskip, bfin, gain_one, wq, wk, wv, wm,
               gain_two, we, wc, wri, bri, whz, wrs, bro, cotangent):
    series, points = signal_samples.shape
    patch = wi.shape[0] // 2
    rows = series * (points // patch)
    dim, width = wri.shape
    cols = whz.shape[1]
    inner = wq.shape[1]
    total = wide * count
    X, CORE, Y, Z0, Z1 = 1, count, 2 * count, 4 * count, 8 * count
    bits = {"c": CORE, "x": X, "y": Y, "p": Z0, "q": Z1}
    narrow_rest = [1 << i for i in range(1, count.bit_length() - 1)]
    wide_rest = [count << i for i in range(4, wide.bit_length() - 1)]
    ffn_masks, token_masks = ([[CORE] + [bits[a] for a in order] for order, _ in parts]
                              for parts in (FFN_PARTS, TOKEN_PARTS))
    column_masks = [CORE] + [bits[a] for a in HEAD_ORDER if a != "x"]
    ffn_rows, token_rows = ([r for r, _ in sizes(parts)] for parts in (FFN_PARTS, TOKEN_PARTS))
    chain = Chain()
    vmem = pltpu.VMEM

    whz_t, wrs_t, cot_t = whz.T, wrs.T, cotangent.T
    packed = (width + dim + 128) // 2
    prepared = chain(
        functools.partial(prepare_kernel, count, rows),
        [((cols, rows), bf)] * (count - 1) + [((cols, rows), f32), ((cols, packed), bf), ((cols, dim + 128), bf)],
        [bro], raw=[cot_t, whz_t, wrs_t],
        scratch=[vmem((max(count - 1, 1), cols, rows), f32), vmem((cols, width // 2), bf), vmem((cols, dim), bf),
                 pltpu.SemaphoreType.DMA((count + 2,))], limit=24)
    own_cot, mine, short = prepared[count - 1:]
    cots = [own_cot] + [xor_send(prepared[r - 1], r, total) for r in range(1, count)]
    far = [xor_send(mine, r, total) for r in range(1, count)]

    weights = [wi, wfin, wskip, wq, wk, wv, wm, we, wc, wri, whz_t]
    out = chain(
        functools.partial(tokens_kernel, patch),
        [((rows, 2 * patch), bf), ((rows, width), bf), ((rows, width), bf), ((rows, dim), f32), ((rows, dim), bf),
         ((rows, 3 * inner), bf), ((1, rows), f32), ((1, rows), f32)] + [(w.shape, bf) for w in weights],
        [signal_samples, present_mask, bi, bfin, gain_one], raw=weights,
        scratch=[pltpu.SemaphoreType.DMA((len(weights),))])
    patches, hid1, d1, embed, normed1, qkv, sigma, center = out[:8]
    wi, wfin, wskip, wq, wk, wv, wm, we, wc, wri, whz_t = out[8:]

    probs, mixed = chain(attend_kernel, [((2 * series, 32, 128), f32), ((rows, inner), bf)], [qkv])
    middle, normed2, hid2, d2, states, hidh, dh = chain(
        ffn_kernel,
        [((rows, dim), f32), ((rows, dim), bf), ((rows, width), bf), ((rows, width), bf), ((rows, dim), bf),
         ((rows, width), bf), ((rows, width), bf)],
        [embed, mixed, wm, gain_two, we, wc, wri, bri])

    groups = max(count // 2, 1)

    def columns():
        out = chain(
            functools.partial(columns_kernel, count, column_masks), [((16, cols, 128), bf)] * (2 * groups),
            [states, hidh, sigma] + cots,
            scratch=[vmem((cols, 128), f32)] + [vmem((32, cols, 128), bf)] * groups, limit=24)
        first = list(out[:2])
        for i in range(1, groups):
            for k in range(2):
                first[k] = first[k] + xor_send(out[2 * i + k], 2 * i, total)
        return Flow(chain, total, bits, wide_rest, [(cols, HEAD_ORDER)], *first, "columns", head=True)

    def gate():
        out = []
        for v in far:
            (v,) = chain(gate_kernel, [(v.shape, bf)], [v], limit=4)
            out += [v, xor_send(v, CORE, total)]
        return out

    def head():
        out = chain(
            functools.partial(head_kernel, count),
            [((rows, dim), bf), ((rows, width), bf), ((1, width), f32)] + [((cols, width), bf)] * (count - 1)
            + [((cols, dim + 128), bf)] * (count - 1),
            [dh, sigma, wri] + cots + [whz_t] + far_both + [short])
        return out[0], out[1], out[2], [whz_t] + out[3:2 + count], [short] + out[2 + count:]

    def ffn_back():
        gmiddle, keep, send = chain(
            functools.partial(ffn_back_kernel, count, ffn_masks),
            [((rows, dim), bf)] + [((16, sum(ffn_rows), 128), bf)] * 2,
            [gstates, states, gpre, sums, hid2, d2, normed2, middle, wc, we, gain_two],
            scratch=[vmem((32, n, 128), bf) for n in ffn_rows] + [vmem((16, 128), f32)])
        return gmiddle, Flow(chain, total, bits, narrow_rest + wide_rest, sizes(FFN_PARTS), keep, send, "ffn")

    def attend_back():
        return chain(attend_back_kernel, [((rows, 3 * inner), bf)], [gmiddle, wm, qkv, probs],
                     scratch=[vmem((rows, inner), bf), vmem(probs.shape, f32), vmem(probs.shape, bf)])[0]

    def project_back():
        return chain(
            functools.partial(project_back_kernel, count, token_masks),
            [((rows, dim), bf), ((1, dim), f32)] + [((32, n, 128), bf) for n in token_rows],
            [gqkv, gmiddle, mixed, normed1, embed, wq, wk, wv, gain_one])

    def tokens_back():
        gscaled, keep, send = chain(
            functools.partial(tokens_back_kernel, count, token_masks, patch),
            [((series, points), f32)] + [((16, sum(token_rows), 128), bf)] * 2,
            [gembed, hid1, d1, patches, wfin, wskip, wi, gg1] + earlier,
            scratch=[vmem((32, n, 128), bf) for n in token_rows] + [vmem((512, 128), f32)])
        return gscaled, Flow(chain, total, bits, narrow_rest + wide_rest, sizes(TOKEN_PARTS), keep, send, "tokens")

    def forecast():
        out = chain(
            functools.partial(forecast_kernel, count, patch),
            [((cols, rows), f32)] + [((cols, rows), bf)] * (count - 1) + [((series, points), f32)],
            [signal_samples, present_mask, gscaled, hidh, states, sigma, center] + mats + shorts + cots)
        return [out[0]] + [xor_send(out[r], r, total) for r in range(1, count)], out[count]

    def place():
        return chain(functools.partial(place_kernel, count), [((cols, count * rows), f32)], preds)[0]

    def finish_columns():
        return chain(functools.partial(unpack_columns, count, column_masks),
                     [((cols, width), f32), ((cols, dim), f32), ((cols,), f32)],
                     one.held, scratch=[vmem((16, cols, 128), bf), vmem((cols, 128), f32)], limit=24)

    def finish_ffn():
        return chain(functools.partial(unpack_ffn, count, ffn_masks),
                     [((dim, width), f32)] * 2 + [((width, dim), f32), ((width,), f32), ((dim,), f32)], two.held,
                     scratch=[vmem((32, sum(ffn_rows), 128), bf), vmem((16, 128), f32)], limit=24)

    def finish_tokens():
        return chain(
            functools.partial(unpack_tokens, count, token_masks),
            [((dim, inner), f32)] * 3 + [((inner, dim), f32), ((width, dim), f32), ((2 * patch, width), f32),
                                         ((2 * patch, dim), f32), ((width,), f32), ((dim,), f32), ((dim,), f32)],
            three.held, scratch=[vmem((32, sum(token_rows), 128), bf), vmem((512, 128), f32)], limit=24)

    far_both = gate()
    one = columns()
    gstates, gpre, sums, mats, shorts = head()
    gmiddle, two = ffn_back()
    gqkv = attend_back()
    gembed, gg1, *earlier = project_back()
    two.step()
    gscaled, three = tokens_back()
    one.step()
    preds, g_series = forecast()
    three.step()
    two.step()
    prediction = place()
    one.step()
    three.step()
    two.step()
    three.step()
    two.step()
    one.step()
    three.step()
    one.step()
    two.step()
    three.step()
    two.step()
    one.step()
    three.step()
    one.step()
    two.step()
    three.step()
    three.step()
    two.step()
    one.step()
    two.step()
    ffn_out = finish_ffn()
    one.step()
    three.step()
    tokens_out = finish_tokens()
    columns_out = finish_columns()
    g_hw, g_hs, g_hb = columns_out
    g_hiw, g_up, g_down, g_hib, g_g2 = ffn_out
    g_q, g_k, g_v, g_wo, g_to, g_ti, g_ts, g_tib, g_tob, g_g1 = tokens_out
    return (prediction.T, g_series, g_ti, g_tib, g_to, g_ts, g_tob, g_g1, g_q, g_k, g_v, g_wo, g_g2, g_up, g_down,
            g_hiw, g_hib, g_hw.T, g_hs.T, g_hb)


def solution(mesh):
    wide, count = mesh.shape["wide"], mesh.shape["narrow"]
    both = P(("wide", "narrow"), None)
    return jax.shard_map(
        functools.partial(per_device, wide, count),
        mesh=mesh,
        in_specs=(both, both) + (P(),) * 15 + (P(None, "narrow"), P(None, "narrow"), P("narrow"), P("wide", "narrow")),
        out_specs=(P("wide", "narrow"), both) + (P(),) * 15
        + (P(None, "narrow"), P(None, "narrow"), P("narrow")),
        check_vma=False,
    )
```

```python
import functools

import jax
import jax.numpy as jnp
from jax import lax
from jax.experimental import pallas as pl
from jax.experimental.pallas import tpu as pltpu
from jax.sharding import PartitionSpec as P

HEADS = 8
HEAD_DIM = 64
EPS = 1e-06
SCALE = HEAD_DIM ** (-0.5)
bf = jnp.bfloat16
f32 = jnp.float32
TILE = 384
WIDE = 256
AXES = ("wide", "narrow")
MIB = 1 << 20
COSTS = {31: 20000000000, 20: 6000000000, 12: 30000000000, 19: 30000000000, 35: 20000000000, 27: 30000000000, 5: 10000000000, 16: 3000000000, 21: 10000000000, 28: 6000000000, 23: 30000000000, 29: 6000000000, 32: 30000000000, 26: 10000000000, 10: 3000000000, 8: 20000000000, 38: 10000000000}


def dot(a, b):
    return lax.dot_general(a, b, (((1,), (0,)), ((), ())), preferred_element_type=f32)


def dot_nt(a, b):
    return lax.dot_general(a, b, (((1,), (1,)), ((), ())), preferred_element_type=f32)


def dot_tn(a, b):
    return lax.dot_general(a, b, (((0,), (0,)), ((), ())), preferred_element_type=f32)


class Chain:
    def __init__(self):
        self.last = None
        self.calls = 0

    def __call__(self, kernel, outs, args, scratch=(), limit=16, raw=()):
        vmem = pl.BlockSpec(memory_space=pltpu.VMEM)
        hbm = pl.BlockSpec(memory_space=pl.ANY)
        args, raw = list(args), [pltpu.with_memory_space_constraint(v, pltpu.HBM) for v in raw]
        deps = [] if self.last is None or any(a is self.last for a in args) else [self.last]
        n, d = len(args) + len(raw), len(deps)
        cost = COSTS.get(self.calls, 1000)
        self.calls += 1

        def body(*refs):
            kernel(*refs[:n], *refs[n + d:])

        name = getattr(kernel, "__name__", None) or kernel.func.__name__
        res = list(pl.pallas_call(
            body,
            name=name,
            out_shape=[jax.ShapeDtypeStruct(s, d) for s, d in outs],
            in_specs=[vmem] * len(args) + [pl.BlockSpec(memory_space=pltpu.HBM)] * len(raw) + [hbm] * d,
            out_specs=[vmem] * len(outs),
            scratch_shapes=list(scratch),
            cost_estimate=pl.CostEstimate(flops=cost, bytes_accessed=1000, transcendentals=0),
            compiler_params=pltpu.CompilerParams(vmem_limit_bytes=limit * MIB),
        )(*args, *raw, *deps))
        self.last = min(res, key=lambda r: r.size)
        return res


def silu_parts(v):
    s = 0.5 * jnp.tanh(0.5 * v) + 0.5
    h = v * s
    return h, s + h * (1.0 - s)


def iota(shape, dim):
    return lax.broadcasted_iota(jnp.int32, shape, dim)


def series_stats(samples, observed, patch):
    first = jnp.where(iota(samples.shape, 1) < patch, observed, 0.0)
    count = jnp.maximum(jnp.sum(first, axis=1, keepdims=True), 1.0)
    center = jnp.sum(first * samples, axis=1, keepdims=True) / count
    offset = samples - center
    spread = jnp.sum(first * offset * offset, axis=1, keepdims=True) / count
    sigma = jnp.sqrt(jnp.maximum(spread, 1.0))
    return first, count, center, offset, spread, sigma


def rms(v):
    return lax.rsqrt(jnp.mean(v * v, axis=-1, keepdims=True) + EPS)


def norm_back(g, v, gain):
    r = rms(v)
    u = v * r
    w = g * gain
    grad_gain = jnp.sum(g * u, axis=0, keepdims=True)
    return r * (w - u * jnp.mean(w * u, axis=-1, keepdims=True)), grad_gain


def token_row(v, rows):
    series = v.shape[0]
    own = iota((series, rows), 1) // (rows // series) == iota((series, rows), 0)
    return jnp.sum(jnp.where(own, v, 0.0), axis=0, keepdims=True)


def series_column(v, series):
    rows = v.shape[1]
    own = iota((series, rows), 1) // (rows // series) == iota((series, rows), 0)
    return jnp.sum(jnp.where(own, v, 0.0), axis=1, keepdims=True)


def me_of(masks, count):
    index = lax.axis_index("wide") * count + lax.axis_index("narrow")
    out = jnp.int32(0)
    for m in masks:
        out = out * 2 + ((index // m) % 2 if m else 0)
    return out


def prepare_kernel(count, rows, bias, cot, whz, wrs, *refs):
    cots, (own, mine, short) = refs[:count - 1], refs[count - 1:count + 2]
    wide_cots, shortcut, offsets, sems = refs[count + 2:]
    narrow = lax.axis_index("narrow")
    core = lax.axis_index("wide") % 2
    width, dim = mine.shape[1], shortcut.shape[1]

    def tokens(r):
        return cot.at[:, pl.ds(pl.multiple_of((narrow ^ r) * rows, 128), rows)]

    copies = [
        pltpu.make_async_copy(bias, offsets, sems.at[0]),
        pltpu.make_async_copy(wrs, shortcut, sems.at[1]),
        pltpu.make_async_copy(whz.at[:, pl.ds(pl.multiple_of(core * width, 128), width)], mine, sems.at[2]),
        pltpu.make_async_copy(tokens(0), own, sems.at[3]),
    ] + [pltpu.make_async_copy(tokens(r), wide_cots.at[r - 1], sems.at[3 + r]) for r in range(1, count)]
    for c in copies:
        c.start()
    for c in copies[:2]:
        c.wait()
    short[:, :dim] = shortcut[...]
    short[:, dim:] = dot_tn(offsets[...].astype(f32)[None, :].astype(bf), jnp.ones((1, 128), bf)).astype(bf)
    for c in copies[2:]:
        c.wait()
    for r in range(1, count):
        cots[r - 1][...] = wide_cots[r - 1].astype(bf)


def gate_kernel(v, out):
    out[...] = v[...]


def tokens_kernel(patch, *refs):
    samples, mask, bi, bfin, gain = refs[:5]
    hbm = refs[5:16]
    patches, hid, dhid, embed, normed, qkv, sigma_row, center_row = refs[16:24]
    vmem, sems = refs[24:35], refs[35]
    copies = [pltpu.make_async_copy(h, v, sems.at[i]) for i, (h, v) in enumerate(zip(hbm, vmem))]
    for c in copies:
        c.start()
    wi, wfin, wskip, wq, wk, wv = vmem[:6]
    series, points = samples.shape
    tokens = points // patch
    rows = series * tokens
    observed = mask[...].astype(f32)
    _, _, center, offset, _, sigma = series_stats(samples[...], observed, patch)
    sigma_row[...] = token_row(sigma, rows)
    center_row[...] = token_row(center, rows)
    scaled = (observed * offset / sigma).astype(bf)
    spread_rows = (iota((rows, series), 0) // tokens == iota((rows, series), 1)).astype(f32).astype(bf)
    own = (iota((rows, points), 1) // patch == iota((rows, points), 0) % tokens).astype(f32)
    col = iota((points, 2 * patch), 0) % patch
    lane = iota((points, 2 * patch), 1)
    fold_s = (col == lane).astype(f32).astype(bf)
    fold_o = (col + patch == lane).astype(f32).astype(bf)
    es = (dot(spread_rows, scaled) * own).astype(bf)
    eo = (dot(spread_rows, observed.astype(bf)) * own).astype(bf)
    p = (dot(es, fold_s) + dot(eo, fold_o)).astype(bf)
    patches[...] = p
    for c in copies[:3]:
        c.wait()
    acc = dot(p, wskip[...]) + bfin[...][None, :]
    for j in range(0, wi.shape[1], WIDE):
        t = slice(j, j + WIDE)
        h, d = silu_parts(dot(p, wi[:, t]) + bi[t][None, :])
        h = h.astype(bf)
        hid[:, t] = h
        dhid[:, t] = d.astype(bf)
        acc = acc + dot(h, wfin[t, :])
    embed[...] = acc
    n = (acc * rms(acc) * gain[...][None, :]).astype(bf)
    normed[...] = n
    inner = wq.shape[1]
    for i, w in enumerate((wq, wk, wv)):
        copies[3 + i].wait()
        qkv[:, i * inner:(i + 1) * inner] = dot(n, w[...]).astype(bf)
    for c in copies[6:]:
        c.wait()


def block_mask():
    return (iota((128, 256), 0) // 32 == iota((128, 256), 1) // 64).astype(f32).astype(bf)


def spread_heads(v, keep):
    return jnp.concatenate([v] * 4, axis=0) * keep


def pick_heads(v):
    head = iota((32, 256), 1) // 64
    out = v[0:32]
    for h in range(1, 4):
        out = jnp.where(head == h, v[32 * h:32 * h + 32], out)
    return out


def pairs(rows):
    for i in range(rows // 16):
        yield i, slice(32 * (i // 2), 32 * (i // 2) + 32), 256 * (i % 2)


def attend_kernel(qkv, probs, mixed):
    keep = block_mask()
    inner = HEADS * HEAD_DIM
    rows = qkv.shape[0]
    for i, s, c in pairs(rows):
        q = spread_heads(qkv[s, c:c + 256], keep)
        probs[i] = dot_nt(qkv[s, inner + c:inner + c + 256], q)
    for i in range(0, rows // 16, 4):
        v = probs[i:i + 4] * SCALE
        e = jnp.exp(v - jnp.max(v, axis=1, keepdims=True))
        probs[i:i + 4] = e / jnp.sum(e, axis=1, keepdims=True)
    for i, s, c in pairs(rows):
        v = qkv[s, 2 * inner + c:2 * inner + c + 256]
        mixed[s, c:c + 256] = pick_heads(dot_tn(probs[i].astype(bf), v)).astype(bf)


def ffn_kernel(embed, mixed, wm, gain, we, wc, wri, bri, middle, normed, hid, dhid, states, hidh, dh):
    mid = embed[...] + dot(mixed[...], wm[...])
    middle[...] = mid
    n = (mid * rms(mid) * gain[...][None, :]).astype(bf)
    normed[...] = n
    acc = mid
    for j in range(0, we.shape[1], WIDE):
        t = slice(j, j + WIDE)
        h, d = silu_parts(dot(n, we[:, t]))
        h = h.astype(bf)
        hid[:, t] = h
        dhid[:, t] = d.astype(bf)
        acc = acc + dot(h, wc[t, :])
    st = acc.astype(bf)
    states[...] = st
    for j in range(0, wri.shape[1], WIDE):
        t = slice(j, j + WIDE)
        h, d = silu_parts(dot(st, wri[:, t]) + bri[t][None, :])
        hidh[:, t] = h.astype(bf)
        dh[:, t] = d.astype(bf)


HEAD_ORDER = "pqxy"
FFN_PARTS = [
    ("xypq", [("down", 0), ("down", 1), ("down", 2), ("up", 0), ("up", 1)]),
    ("yqxp", [("inner", 0), ("inner", 1), ("inner", 2), ("up", 2), ("vector", 0)]),
]
TOKEN_PARTS = [
    ("xpyq", [("final", 0), ("final", 1), ("final", 2), ("small", 0)]),
    ("yxpq", [("attention", 0), ("attention", 1), ("attention", 2), ("merge", 0), ("merge", 1), ("merge", 2)]),
]
SLAB_ROWS = {"merge": 16, "vector": 16, "small": 16}


def part_rows(items):
    return sum(SLAB_ROWS.get(name, 48) for name, _ in items)


def layout(parts):
    out = {}
    for p, (_, items) in enumerate(parts):
        at = 0
        for item in items:
            out[item] = p, at
            at += SLAB_ROWS.get(item[0], 48)
    return out


def sizes(parts):
    return [(part_rows(items), order) for order, items in parts]


def put_matrix(scrs, mes, where, name, tile, value):
    value = value.astype(bf)
    for k in range(3):
        p, at = where[name, k]
        for i in range(8):
            scrs[p][(8 * tile + i) ^ mes[p], at:at + 48, :] = value[48 * i:48 * i + 48, 128 * k:128 * k + 128]


def ship(sources, keep, send):
    at = 0
    for v, first, rows in sources:
        n = v.shape[0] // 2
        keep[:, at:at + rows] = v[:n, first:first + rows]
        send[:, at:at + rows] = v[n:, first:first + rows]
        at += rows


def index_bits(index, count):
    return [(index // (1 << (count - 1 - k))) % 2 for k in range(count)]


def rows_of(tmp, row, v):
    for j in range(0, v.shape[1], 128):
        tmp[row:row + 1, :] = v[:, j:j + 128]
        row += 1
    return row


def columns_kernel(count, masks, *refs):
    states, hidh, sigma = refs[:3]
    cots, refs = refs[3:3 + count], refs[3 + count:]
    groups = max(count // 2, 1)
    outs, (tmp, *scrs) = refs[:2 * groups], refs[2 * groups:]
    me = me_of(masks, count)
    st = states[...]
    width = hidh.shape[1]
    cols = tmp.shape[0]
    for r in range(count):
        turned = (cots[r][...].astype(f32) * sigma[...]).astype(bf)
        scr = scrs[r // 2]

        def put(c, v):
            core, *others = index_bits(c ^ me, 4)
            at = core
            for axis in HEAD_ORDER.replace("d", "yx").replace("z", "qp"):
                at = at * 2 + (r % 2 if axis == "x" else others.pop(0))
            scr[at] = v

        for j in range(0, width, TILE):
            v = dot(turned, hidh[:, j:j + TILE]).astype(bf)
            for i in range(TILE // 128):
                put(j // 128 + i, v[:, 128 * i:128 * i + 128])
        v = dot(turned, st).astype(bf)
        for i in range(st.shape[1] // 128):
            put(width // 128 + i, v[:, 128 * i:128 * i + 128])
        tmp[...] = jnp.zeros_like(tmp)
        bias = dot_nt(jnp.ones((8, turned.shape[1]), bf), turned)
        for row, j in enumerate(range(0, cols, 128)):
            n = min(128, cols - j)
            tmp[row:row + 1, 0:n] = bias[0:1, j:j + n]
        put(15, tmp[...].astype(bf))
    for i in range(groups):
        ship([(scrs[i], 0, cols)], *outs[2 * i:2 * i + 2])


def head_kernel(count, *refs):
    dh, sigma = refs[:2]
    refs = refs[2:]
    cots, refs = refs[:count], refs[count:]
    whz, refs = refs[0], refs[1:]
    far, refs = refs[:2 * (count - 1)], refs[2 * (count - 1):]
    gpre, sums = refs[:2]
    gs, mats = refs[2:2 + count], refs[2 + count:]
    width = dh.shape[1]
    half = width // 2
    core = lax.axis_index("wide") % 2
    for r in range(count - 1):
        for k, c in enumerate((core, 1 - core)):
            mats[r][:, pl.ds(pl.multiple_of(c * half, 128), half)] = far[2 * r + k][...]
    mats = [whz] + list(mats)
    grads = [(c[...].astype(f32) * sigma[...]).astype(bf).T for c in cots]
    for o, g in zip(gs, grads):
        o[...] = g
    for j in range(0, width, WIDE):
        t = slice(j, j + WIDE)
        acc = dot(grads[0], mats[0][:, t])
        for r in range(1, count):
            acc = acc + dot(grads[r], mats[r][:, t])
        gp = (acc * dh[:, t].astype(f32)).astype(bf)
        gpre[:, t] = gp
        sums[:, t] = jnp.sum(gp.astype(f32), axis=0, keepdims=True)


def ffn_back_kernel(count, masks, states, gpre, sums, wri, hid, dhid, normed, middle, wc, we, gain, *refs):
    gs, shorts, refs = refs[:count], refs[count:2 * count], refs[2 * count:]
    gmiddle, keep, send, *scrs, tmp = refs
    mes = [me_of(m, count) for m in masks]
    where = layout(FFN_PARTS)
    acc = dot_nt(gpre[...], wri[...])
    for r in range(count):
        acc = acc + dot(gs[r][...], shorts[r][:, :wri.shape[0]])
    g = acc.astype(bf)
    nt = normed[...].T
    acc = None
    for j in range(4):
        t = slice(TILE * j, TILE * j + TILE)
        gp = (dot_nt(g, wc[t, :]) * dhid[:, t].astype(f32)).astype(bf)
        part = dot_nt(gp, we[:, t])
        acc = part if acc is None else acc + part
        put_matrix(scrs, mes, where, "up", j, dot(nt, gp))
        put_matrix(scrs, mes, where, "down", j, dot_tn(hid[:, t], g))
    back, gg = norm_back(acc, middle[...], gain[...][None, :])
    gmiddle[...] = (g.astype(f32) + back).astype(bf)
    st = states[...].T
    for j in range(4):
        put_matrix(scrs, mes, where, "inner", j, dot(st, gpre[:, TILE * j:TILE * j + TILE]))
    p, at = where["vector", 0]
    scrs[p][:, at:at + 16, :] = jnp.zeros((32, 16, 128), bf)
    tmp[...] = jnp.zeros_like(tmp)
    row = rows_of(tmp, 0, sums[...])
    rows_of(tmp, row, gg)
    scrs[p][mes[p], at:at + 16, :] = tmp[...].astype(bf)
    ship([(v, 0, v.shape[1]) for v in scrs], keep, send)


def attend_back_kernel(gmiddle, wm, qkv, probs, gqkv, gmix, gprobs, low):
    keep = block_mask()
    inner = HEADS * HEAD_DIM
    rows = qkv.shape[0]
    gmix[...] = dot_nt(gmiddle[...], wm[...]).astype(bf)
    for i, s, c in pairs(rows):
        g = spread_heads(gmix[s, c:c + 256], keep)
        gprobs[i] = dot_nt(qkv[s, 2 * inner + c:2 * inner + c + 256], g)
        gqkv[s, 2 * inner + c:2 * inner + c + 256] = dot(probs[i].astype(bf), g).astype(bf)
    for i in range(0, rows // 16, 4):
        p, g = probs[i:i + 4], gprobs[i:i + 4]
        low[i:i + 4] = (p * (g - jnp.sum(g * p, axis=1, keepdims=True))).astype(bf)
    for i, s, c in pairs(rows):
        ds = low[i]
        q = spread_heads(qkv[s, c:c + 256], keep)
        k = qkv[s, inner + c:inner + c + 256]
        gqkv[s, c:c + 256] = (pick_heads(dot_tn(ds, k)) * SCALE).astype(bf)
        gqkv[s, inner + c:inner + c + 256] = (dot(ds, q) * SCALE).astype(bf)


def project_back_kernel(count, masks, gqkv, gmiddle, mixed, normed, embed, wq, wk, wv, gain, gembed, ggain,
                        *scrs):
    mes = [me_of(m, count) for m in masks]
    where = layout(TOKEN_PARTS)
    inner = wq.shape[1]
    acc = dot_nt(gqkv[:, :inner], wq[...])
    acc = acc + dot_nt(gqkv[:, inner:2 * inner], wk[...])
    acc = acc + dot_nt(gqkv[:, 2 * inner:], wv[...])
    back, gg = norm_back(acc, embed[...], gain[...][None, :])
    ggain[...] = gg
    gm = gmiddle[...]
    gembed[...] = (gm.astype(f32) + back).astype(bf)
    nt = normed[...].T
    for j in range(4):
        put_matrix(scrs, mes, where, "attention", j, dot(nt, gqkv[:, TILE * j:TILE * j + TILE]))
    v = dot_tn(mixed[...], gm).astype(bf)
    for k in range(3):
        p, at = where["merge", k]
        for i in range(32):
            scrs[p][i ^ mes[p], at:at + 16, :] = v[16 * i:16 * i + 16, 128 * k:128 * k + 128]


def tokens_back_kernel(count, masks, patch, gembed, hid, dhid, patches, wfin, wskip, wi, gain_one, *refs):
    n = len(masks)
    earlier, (gpatches, keep, send), scrs, tmp = refs[:n], refs[n:n + 3], refs[n + 3:2 * n + 3], refs[-1]
    mes = [me_of(m, count) for m in masks]
    where = layout(TOKEN_PARTS)
    g = gembed[...]
    p = patches[...]
    pt = p.T
    tmp[...] = jnp.zeros_like(tmp)
    gpat = dot_nt(g, wskip[...])
    row = 480
    for j in range(4):
        t = slice(TILE * j, TILE * j + TILE)
        gp = (dot_nt(g, wfin[t, :]) * dhid[:, t].astype(f32)).astype(bf)
        gpat = gpat + dot_nt(gp, wi[:, t])
        v = dot(pt, gp)
        for i in range(3):
            c = 3 * j + i
            tmp[32 * c:32 * c + 32, :] = v[:, 128 * i:128 * i + 128]
        row = rows_of(tmp, row, jnp.sum(gp.astype(f32), axis=0, keepdims=True))
        put_matrix(scrs, mes, where, "final", j, dot_tn(hid[:, t], g))
    v = dot(pt, g)
    for i in range(3):
        tmp[384 + 32 * i:416 + 32 * i, :] = v[:, 128 * i:128 * i + 128]
    row = rows_of(tmp, row, jnp.sum(g.astype(f32), axis=0, keepdims=True))
    rows_of(tmp, row, gain_one[...])
    p, at = where["small", 0]
    for b in range(32):
        scrs[p][b ^ mes[p], at:at + 16, :] = tmp[16 * b:16 * b + 16].astype(bf)
    ship([((earlier if item[0] in ("attention", "merge") else scrs)[where[item][0]], where[item][1],
           SLAB_ROWS.get(item[0], 48)) for _, items in TOKEN_PARTS for item in items], keep, send)
    gpatches[...] = gpat


def forecast_kernel(count, patch, *refs):
    samples, mask, gpatches, hid, states, sigma_row, center_row = refs[:7]
    refs = refs[7:]
    mats, refs = refs[:count], refs[count:]
    short, refs = refs[:count], refs[count:]
    cots, refs = refs[:count], refs[count:]
    preds, series_grad = refs[:count], refs[count]
    sg = sigma_row[...]
    ct = center_row[...]
    st = states[...]
    dim = st.shape[1]
    row_c, row_s = 0.0, 0.0
    for r in range(count):
        raw = dot_nt(mats[r][...], hid[...]) + dot_nt(short[r][:, :dim], st) + short[r][:, dim:dim + 1].astype(f32)
        preds[r][...] = (raw * sg + ct).astype(preds[r].dtype)
        c = cots[r][...].astype(f32)
        row_c = row_c + jnp.sum(c, axis=0, keepdims=True)
        row_s = row_s + jnp.sum(c * raw, axis=0, keepdims=True)
    observed = mask[...].astype(f32)
    series = samples.shape[0]
    first, cnt, center, offset, spread, sigma = series_stats(samples[...], observed, patch)
    out_c = series_column(row_c, series)
    out_s = series_column(row_s, series)
    points = samples.shape[1]
    per_series = points // patch
    rows = series * per_series
    lane = iota((2 * patch, points), 1) % patch
    fold = (iota((2 * patch, points), 0) == lane).astype(f32).astype(bf)
    own = (iota((rows, points), 1) // patch == iota((rows, points), 0) % per_series).astype(f32)
    gpat = gpatches[...]
    high = gpat.astype(bf)
    low = (gpat - high.astype(f32)).astype(bf)
    full = (dot(high, fold) + dot(low, fold)) * own
    og = observed * jnp.sum(full.reshape(series, per_series, points), axis=1)
    g_center = out_c - jnp.sum(og, axis=1, keepdims=True) / sigma
    g_sigma = out_s - jnp.sum(og * offset, axis=1, keepdims=True) / (sigma * sigma)
    g_spread = jnp.where(spread > 1.0, g_sigma * 0.5 / sigma, 0.0)
    g_center = g_center - g_spread * 2.0 * jnp.sum(first * offset, axis=1, keepdims=True) / cnt
    series_grad[...] = og / sigma + g_spread * 2.0 * first * offset / cnt + g_center * first / cnt


def place_kernel(count, *refs):
    preds, out = refs[:count], refs[count]
    rows = preds[0].shape[1]
    narrow = lax.axis_index("narrow")
    for r in range(count):
        out[:, pl.ds(pl.multiple_of((narrow ^ r) * rows, 128), rows)] = preds[r][...].astype(f32)


def xor_send(v, mask, total):
    return lax.ppermute(v, AXES, [(i, i ^ mask) for i in range(total)])


def grouped(parts, level):
    groups = {}
    for p, (_, order) in enumerate(parts):
        groups.setdefault(order[level:], []).append(p)
    return list(groups.values())


def places(parts, groups):
    out = {}
    for g, members in enumerate(groups):
        at = 0
        for p in members:
            out[p] = g, at
            at += parts[p][0]
    return out


def combos(bits):
    out = [0]
    for b in bits:
        out = [o + s for o in out for s in (0, b)]
    return out


def starts(counts):
    return [sum(counts[:k]) for k in range(len(counts))]


def swaps(parts, head=False):
    return all(order[-1] in "xypq" for _, order in parts) and not (head and parts[0][1][-1] == "x")


def add_kernel(parts, before, came, after, split, *refs):
    ins, outs = refs[:sum(came)], refs[sum(came):]
    first, to = starts(came), starts(split)
    n = ins[0].shape[0]
    for p, (rows, _) in enumerate(parts):
        (g, a), (o, b) = before[p], after[p]
        step = n // split[o]
        for k in range(n):
            v = ins[first[g]][k, a:a + rows].astype(f32)
            for c in range(1, came[g]):
                v = v + ins[first[g] + c][k, a:a + rows].astype(f32)
            outs[to[o] + k // step][k % step, b:b + rows] = v.astype(bf)


def join_kernel(parts, before, came, after, *refs):
    ins, outs = refs[:sum(came)], refs[sum(came):]
    first = starts(came)
    for p, (rows, _) in enumerate(parts):
        (g, a), (o, b) = before[p], after[p]
        n = ins[first[g]].shape[0]
        for k in range(came[g]):
            outs[o][n * k:n * k + n, b:b + rows] = ins[first[g] + k][:, a:a + rows]


class Flow:
    def __init__(self, chain, total, bits, rest, parts, keep, send, name, head=False):
        self.chain, self.total, self.bits, self.rest, self.parts = chain, total, bits, rest, parts
        self.name, self.head = name, head
        self.swap = swaps(parts, head)
        self.level, self.down = 0, True
        self.groups = [list(range(len(parts)))]
        self.held = [[keep, self.to(send, bits["c"][0])]]

    def to(self, v, mask):
        with jax.named_scope(self.name + str(mask)):
            return xor_send(v, mask, self.total)

    def rows(self, group):
        return sum(self.parts[p][0] for p in group)

    def levels(self, group):
        return len(self.parts[group[0]][1])

    def masks(self, group, gather=False):
        bits = self.bits[self.parts[group[0]][1][self.level]]
        return combos([b for b in bits if not (gather and self.head and b == self.bits["x"][0])])[1:]

    def step(self):
        (self.add if self.down else self.join)()

    def add(self):
        before, came = places(self.parts, self.groups), [len(h) for h in self.held]
        n = self.held[0][0].shape[0]
        last = self.level == self.levels([0])
        if not last:
            self.groups = grouped(self.parts, self.level)
            whole = self.swap and self.level + 1 == self.levels([0])
            split = [1 if whole else 1 + len(self.masks(g)) for g in self.groups]
        else:
            if self.swap:
                self.groups = grouped(self.parts, self.level - 2)
            split = [1] * len(self.groups)
        shapes = [((n // c, self.rows(g), 128), bf) for g, c in zip(self.groups, split) for _ in range(c)]
        outs = self.chain(
            functools.partial(add_kernel, self.parts, before, came, places(self.parts, self.groups), split),
            shapes, [v for h in self.held for v in h], limit=4)
        at = starts(split)
        if not last:
            self.held = [[outs[k]] + [self.to(outs[k if whole else k + 1 + i], m) for i, m in enumerate(self.masks(g))]
                         for g, k in zip(self.groups, at)]
            self.level += 1
            return
        for m in self.rest:
            outs = [v + self.to(v, m) for v in outs]
        self.down = False
        if self.swap:
            self.level -= 1
        self.spread(outs)

    def spread(self, arrays):
        self.level -= 1
        if self.level >= 0 and not self.masks(self.groups[0], True):
            self.level -= 1
        if self.level < 0:
            self.held = [[a, self.to(a, self.bits["c"][0])] for a in arrays]
            return
        self.held = [[a] + [self.to(a, m) for m in self.masks(g, True)] for g, a in zip(self.groups, arrays)]

    def join(self):
        before, came = places(self.parts, self.groups), [len(h) for h in self.held]
        ns = {p: self.held[g][0].shape[0] * came[g] for p, (g, _) in before.items()}
        up = self.level - 1
        self.groups = grouped(self.parts, up) if up >= 0 else [list(range(len(self.parts)))]
        outs = self.chain(
            functools.partial(join_kernel, self.parts, before, came, places(self.parts, self.groups)),
            [((ns[g[0]], self.rows(g), 128), bf) for g in self.groups], [v for h in self.held for v in h], limit=4)
        self.spread(outs)


def assemble(refs, scr):
    k = 0
    for a in refs:
        scr[k:k + a.shape[0]] = a[...]
        k += a.shape[0]


def finder(scr, parts, masks, count):
    where, mes = layout(parts), [me_of(m, count) for m in masks]
    base = [sum(part_rows(items) for _, items in parts[:p]) for p in range(len(parts))]

    def find(name, k, b):
        p, at = where[name, k]
        at += base[p]
        return scr[b ^ mes[p], at:at + SLAB_ROWS.get(name, 48), :].astype(f32)

    return find


def vectors(tmp, row, outs):
    for o in outs:
        n = o.shape[0]
        for j in range(0, n, 128):
            o[pl.ds(j, 128)] = tmp[row]
            row += 1


def unpack_columns(count, masks, here, there, w, skip, bias, scr, tmp):
    me = me_of(masks, count)
    assemble((here, there), scr)
    cols, width = w.shape
    for b in range(width // 128):
        w[:, 128 * b:128 * b + 128] = scr[b ^ me].astype(f32)
    for i in range(skip.shape[1] // 128):
        skip[:, 128 * i:128 * i + 128] = scr[(width // 128 + i) ^ me].astype(f32)
    tmp[...] = scr[15 ^ me].astype(f32)
    bias[...] = jnp.concatenate([tmp[i:i + 1, :] for i in range(-(-cols // 128))], axis=1)[0, :cols]


def unpack_ffn(count, masks, here, there, inner, up, down, bias, gain, scr, tmp):
    assemble((here, there), scr)
    find = finder(scr, FFN_PARTS, masks, count)
    for b in range(32):
        j, i = b // 8, b % 8
        rows = slice(48 * i, 48 * i + 48)
        for k in range(3):
            cols = slice(TILE * j + 128 * k, TILE * j + 128 * k + 128)
            inner[rows, cols] = find("inner", k, b)
            up[rows, cols] = find("up", k, b)
            down[48 * b:48 * b + 48, 128 * k:128 * k + 128] = find("down", k, b)
    tmp[...] = find("vector", 0, 0)
    vectors(tmp, 0, (bias, gain))


def unpack_tokens(count, masks, here, there, gq, gk, gv, wo, out, tin, skip, bin_, bout, gain, scr, tmp):
    assemble((here, there), scr)
    find = finder(scr, TOKEN_PARTS, masks, count)
    for b in range(32):
        j, i = b // 8, b % 8
        tmp[16 * b:16 * b + 16, :] = find("small", 0, b)
        for k in range(3):
            c = TILE * j + 128 * k
            (gq, gk, gv)[c // 512][48 * i:48 * i + 48, c % 512:c % 512 + 128] = find("attention", k, b)
            out[48 * b:48 * b + 48, 128 * k:128 * k + 128] = find("final", k, b)
            wo[16 * b:16 * b + 16, 128 * k:128 * k + 128] = find("merge", k, b)
    for c in range(12):
        tin[:, 128 * c:128 * c + 128] = tmp[32 * c:32 * c + 32, :]
    for i in range(3):
        skip[:, 128 * i:128 * i + 128] = tmp[384 + 32 * i:416 + 32 * i, :]
    vectors(tmp, 480, (bin_, bout, gain))


def per_device(wide, count, signal_samples, present_mask, wi, bi, wfin, wskip, bfin, gain_one, wq, wk, wv, wm,
               gain_two, we, wc, wri, bri, whz, wrs, bro, cotangent):
    series, points = signal_samples.shape
    patch = wi.shape[0] // 2
    rows = series * (points // patch)
    dim, width = wri.shape
    cols = whz.shape[1]
    inner = wq.shape[1]
    total = wide * count
    X, CORE, Y, Z0, Z1 = 1, count, 2 * count, 4 * count, 8 * count
    bits = {"c": [CORE], "x": [X], "y": [Y], "p": [Z0], "q": [Z1], "d": [Y, X], "z": [Z1, Z0]}
    narrow_rest = [1 << i for i in range(1, count.bit_length() - 1)]
    wide_rest = [count << i for i in range(4, wide.bit_length() - 1)]
    def block_bits(parts, head=False):
        out = []
        for _, order in parts:
            own = [CORE] + [b for a in order for b in bits[a] if not (head and b == X)]
            out.append(own[:-1] + [0] if swaps(parts, head) else own)
        return out

    ffn_masks, token_masks = block_bits(sizes(FFN_PARTS)), block_bits(sizes(TOKEN_PARTS))
    (column_masks,) = block_bits([(cols, HEAD_ORDER)], True)
    ffn_rows, token_rows = ([r for r, _ in sizes(parts)] for parts in (FFN_PARTS, TOKEN_PARTS))
    chain = Chain()
    vmem = pltpu.VMEM

    whz_t, wrs_t, cot_t = whz.T, wrs.T, cotangent.T
    prepared = chain(
        functools.partial(prepare_kernel, count, rows),
        [((cols, rows), bf)] * (count - 1)
        + [((cols, rows), f32), ((cols, width // 2), bf), ((cols, dim + 128), bf)],
        [], raw=[bro, cot_t, whz_t, wrs_t],
        scratch=[vmem((max(count - 1, 1), cols, rows), f32), vmem((cols, dim), bf), vmem((cols,), bf),
                 pltpu.SemaphoreType.DMA((count + 3,))], limit=24)
    own_cot, mine, short = prepared[count - 1:]
    cots = [own_cot] + [xor_send(prepared[r - 1], r, total) for r in range(1, count)]
    far = [xor_send(mine, r, total) for r in range(1, count)]
    shorts = [short] + [xor_send(short, r, total) for r in range(1, count)]

    weights = [wi, wfin, wskip, wq, wk, wv, wm, we, wc, wri, whz_t]
    out = chain(
        functools.partial(tokens_kernel, patch),
        [((rows, 2 * patch), bf), ((rows, width), bf), ((rows, width), bf), ((rows, dim), f32), ((rows, dim), bf),
         ((rows, 3 * inner), bf), ((1, rows), f32), ((1, rows), f32)] + [(w.shape, bf) for w in weights],
        [signal_samples, present_mask, bi, bfin, gain_one], raw=weights,
        scratch=[pltpu.SemaphoreType.DMA((len(weights),))])
    patches, hid1, d1, embed, normed1, qkv, sigma, center = out[:8]
    wi, wfin, wskip, wq, wk, wv, wm, we, wc, wri, whz_t = out[8:]

    probs, mixed = chain(attend_kernel, [((2 * series, 32, 128), f32), ((rows, inner), bf)], [qkv])
    middle, normed2, hid2, d2, states, hidh, dh = chain(
        ffn_kernel,
        [((rows, dim), f32), ((rows, dim), bf), ((rows, width), bf), ((rows, width), bf), ((rows, dim), bf),
         ((rows, width), bf), ((rows, width), bf)],
        [embed, mixed, wm, gain_two, we, wc, wri, bri])

    groups = max(count // 2, 1)

    def columns():
        out = chain(
            functools.partial(columns_kernel, count, column_masks), [((16, cols, 128), bf)] * (2 * groups),
            [states, hidh, sigma] + cots,
            scratch=[vmem((cols, 128), f32)] + [vmem((32, cols, 128), bf)] * groups, limit=24)
        first = list(out[:2])
        for i in range(1, groups):
            for k in range(2):
                first[k] = first[k] + xor_send(out[2 * i + k], 2 * i, total)
        return Flow(chain, total, bits, wide_rest, [(cols, HEAD_ORDER)], *first, "columns", head=True)

    def gate():
        out = []
        for v in far:
            (v,) = chain(gate_kernel, [(v.shape, bf)], [v], limit=4)
            out += [v, xor_send(v, CORE, total)]
        return out

    def head():
        out = chain(
            functools.partial(head_kernel, count),
            [((rows, width), bf), ((1, width), f32)] + [((rows, cols), bf)] * count
            + [((cols, width), bf)] * (count - 1),
            [dh, sigma] + cots + [whz_t] + far_both)
        return out[0], out[1], out[2:2 + count], [whz_t] + out[2 + count:]

    def ffn_back():
        gmiddle, keep, send = chain(
            functools.partial(ffn_back_kernel, count, ffn_masks),
            [((rows, dim), bf)] + [((16, sum(ffn_rows), 128), bf)] * 2,
            [states, gpre, sums, wri, hid2, d2, normed2, middle, wc, we, gain_two] + gs + shorts,
            scratch=[vmem((32, n, 128), bf) for n in ffn_rows] + [vmem((16, 128), f32)])
        return gmiddle, Flow(chain, total, bits, narrow_rest + wide_rest, sizes(FFN_PARTS), keep, send, "ffn")

    def attend_back():
        return chain(attend_back_kernel, [((rows, 3 * inner), bf)], [gmiddle, wm, qkv, probs],
                     scratch=[vmem((rows, inner), bf), vmem(probs.shape, f32), vmem(probs.shape, bf)])[0]

    def project_back():
        return chain(
            functools.partial(project_back_kernel, count, token_masks),
            [((rows, dim), bf), ((1, dim), f32)] + [((32, n, 128), bf) for n in token_rows],
            [gqkv, gmiddle, mixed, normed1, embed, wq, wk, wv, gain_one])

    def tokens_back():
        gpatches, keep, send = chain(
            functools.partial(tokens_back_kernel, count, token_masks, patch),
            [((rows, 2 * patch), f32)] + [((16, sum(token_rows), 128), bf)] * 2,
            [gembed, hid1, d1, patches, wfin, wskip, wi, gg1] + earlier,
            scratch=[vmem((32, n, 128), bf) for n in token_rows] + [vmem((512, 128), f32)])
        return gpatches, Flow(chain, total, bits, narrow_rest + wide_rest, sizes(TOKEN_PARTS), keep, send, "tokens")

    def forecast():
        out = chain(
            functools.partial(forecast_kernel, count, patch),
            [((cols, rows), f32)] + [((cols, rows), bf)] * (count - 1) + [((series, points), f32)],
            [signal_samples, present_mask, gpatches, hidh, states, sigma, center] + mats + shorts + cots)
        return [out[0]] + [xor_send(out[r], r, total) for r in range(1, count)], out[count]

    def place():
        return chain(functools.partial(place_kernel, count), [((cols, count * rows), f32)], preds)[0]

    def finish_columns():
        return chain(functools.partial(unpack_columns, count, column_masks),
                     [((cols, width), f32), ((cols, dim), f32), ((cols,), f32)],
                     one.held[0], scratch=[vmem((16, cols, 128), bf), vmem((cols, 128), f32)], limit=24)

    def finish_ffn():
        return chain(functools.partial(unpack_ffn, count, ffn_masks),
                     [((dim, width), f32)] * 2 + [((width, dim), f32), ((width,), f32), ((dim,), f32)], two.held[0],
                     scratch=[vmem((32, sum(ffn_rows), 128), bf), vmem((16, 128), f32)], limit=24)

    def finish_tokens():
        return chain(
            functools.partial(unpack_tokens, count, token_masks),
            [((dim, inner), f32)] * 3 + [((inner, dim), f32), ((width, dim), f32), ((2 * patch, width), f32),
                                         ((2 * patch, dim), f32), ((width,), f32), ((dim,), f32), ((dim,), f32)],
            three.held[0], scratch=[vmem((32, sum(token_rows), 128), bf), vmem((512, 128), f32)], limit=24)

    far_both = gate()
    one = columns()
    gpre, sums, gs, mats = head()
    gmiddle, two = ffn_back()
    gqkv = attend_back()
    gembed, gg1, *earlier = project_back()
    two.step()
    gpatches, three = tokens_back()
    one.step()
    three.step()
    two.step()
    preds, g_series = forecast()
    three.step()
    one.step()
    three.step()
    two.step()
    three.step()
    prediction = place()
    one.step()
    two.step()
    three.step()
    two.step()
    three.step()
    one.step()
    two.step()
    one.step()
    three.step()
    two.step()
    one.step()
    three.step()
    two.step()
    one.step()
    tokens_out = finish_tokens()
    ffn_out = finish_ffn()
    columns_out = finish_columns()
    g_hw, g_hs, g_hb = columns_out
    g_hiw, g_up, g_down, g_hib, g_g2 = ffn_out
    g_q, g_k, g_v, g_wo, g_to, g_ti, g_ts, g_tib, g_tob, g_g1 = tokens_out
    return (prediction.T, g_series, g_ti, g_tib, g_to, g_ts, g_tob, g_g1, g_q, g_k, g_v, g_wo, g_g2, g_up, g_down,
            g_hiw, g_hib, g_hw.T, g_hs.T, g_hb)


def solution(mesh):
    wide, count = mesh.shape["wide"], mesh.shape["narrow"]
    both = P(("wide", "narrow"), None)
    return jax.shard_map(
        functools.partial(per_device, wide, count),
        mesh=mesh,
        in_specs=(both, both) + (P(),) * 15 + (P(None, "narrow"), P(None, "narrow"), P("narrow"), P("wide", "narrow")),
        out_specs=(P("wide", "narrow"), both) + (P(),) * 15
        + (P(None, "narrow"), P(None, "narrow"), P("narrow")),
        check_vma=False,
    )
```

```python
import functools

import jax
import jax.numpy as jnp
from jax import lax
from jax.experimental import pallas as pl
from jax.experimental.pallas import tpu as pltpu
from jax.sharding import PartitionSpec as P

HEADS = 8
HEAD_DIM = 64
EPS = 1e-06
SCALE = HEAD_DIM ** (-0.5)
bf = jnp.bfloat16
f32 = jnp.float32
TILE = 384
WIDE = 256
AXES = ("wide", "narrow")
MIB = 1 << 20
COSTS = {31: 15000000000, 20: 6000000000, 12: 30000000000, 19: 30000000000, 35: 20000000000, 27: 30000000000, 5: 10000000000, 21: 10000000000, 28: 6000000000, 23: 30000000000, 29: 6000000000, 32: 30000000000, 26: 10000000000, 10: 3000000000, 8: 20000000000, 38: 10000000000}


def dot(a, b):
    return lax.dot_general(a, b, (((1,), (0,)), ((), ())), preferred_element_type=f32)


def dot_nt(a, b):
    return lax.dot_general(a, b, (((1,), (1,)), ((), ())), preferred_element_type=f32)


def dot_tn(a, b):
    return lax.dot_general(a, b, (((0,), (0,)), ((), ())), preferred_element_type=f32)


class Chain:
    def __init__(self):
        self.last = None
        self.calls = 0

    def __call__(self, kernel, outs, args, scratch=(), limit=16, raw=()):
        vmem = pl.BlockSpec(memory_space=pltpu.VMEM)
        hbm = pl.BlockSpec(memory_space=pl.ANY)
        args, raw = list(args), [pltpu.with_memory_space_constraint(v, pltpu.HBM) for v in raw]
        deps = [] if self.last is None or any(a is self.last for a in args) else [self.last]
        n, d = len(args) + len(raw), len(deps)
        cost = COSTS.get(self.calls, 1000)
        self.calls += 1

        def body(*refs):
            kernel(*refs[:n], *refs[n + d:])

        name = getattr(kernel, "__name__", None) or kernel.func.__name__
        res = list(pl.pallas_call(
            body,
            name=name,
            out_shape=[jax.ShapeDtypeStruct(s, d) for s, d in outs],
            in_specs=[vmem] * len(args) + [pl.BlockSpec(memory_space=pltpu.HBM)] * len(raw) + [hbm] * d,
            out_specs=[vmem] * len(outs),
            scratch_shapes=list(scratch),
            cost_estimate=pl.CostEstimate(flops=cost, bytes_accessed=1000, transcendentals=0),
            compiler_params=pltpu.CompilerParams(vmem_limit_bytes=limit * MIB),
        )(*args, *raw, *deps))
        self.last = min(res, key=lambda r: r.size)
        return res


def silu_parts(v):
    s = 0.5 * jnp.tanh(0.5 * v) + 0.5
    h = v * s
    return h, s + h * (1.0 - s)


def iota(shape, dim):
    return lax.broadcasted_iota(jnp.int32, shape, dim)


def series_stats(samples, observed, patch):
    first = jnp.where(iota(samples.shape, 1) < patch, observed, 0.0)
    count = jnp.maximum(jnp.sum(first, axis=1, keepdims=True), 1.0)
    center = jnp.sum(first * samples, axis=1, keepdims=True) / count
    offset = samples - center
    spread = jnp.sum(first * offset * offset, axis=1, keepdims=True) / count
    sigma = jnp.sqrt(jnp.maximum(spread, 1.0))
    return first, count, center, offset, spread, sigma


def rms(v):
    return lax.rsqrt(jnp.mean(v * v, axis=-1, keepdims=True) + EPS)


def norm_back(g, v, gain):
    r = rms(v)
    u = v * r
    w = g * gain
    grad_gain = jnp.sum(g * u, axis=0, keepdims=True)
    return r * (w - u * jnp.mean(w * u, axis=-1, keepdims=True)), grad_gain


def token_row(v, rows):
    series = v.shape[0]
    own = iota((series, rows), 1) // (rows // series) == iota((series, rows), 0)
    return jnp.sum(jnp.where(own, v, 0.0), axis=0, keepdims=True)


def series_column(v, series):
    rows = v.shape[1]
    own = iota((series, rows), 1) // (rows // series) == iota((series, rows), 0)
    return jnp.sum(jnp.where(own, v, 0.0), axis=1, keepdims=True)


def me_of(masks, count):
    index = lax.axis_index("wide") * count + lax.axis_index("narrow")
    out = jnp.int32(0)
    for m in masks:
        out = out * 2 + ((index // m) % 2 if m else 0)
    return out


def prepare_kernel(count, rows, cot, whz, *refs):
    cots, (own, mine) = refs[:count - 1], refs[count - 1:count + 1]
    wide_cots, sems = refs[count + 1:]
    narrow = lax.axis_index("narrow")
    core = lax.axis_index("wide") % 2
    width = mine.shape[1]

    def tokens(r):
        return cot.at[:, pl.ds(pl.multiple_of((narrow ^ r) * rows, 128), rows)]

    copies = [
        pltpu.make_async_copy(whz.at[:, pl.ds(pl.multiple_of(core * width, 128), width)], mine, sems.at[0]),
        pltpu.make_async_copy(tokens(0), own, sems.at[1]),
    ] + [pltpu.make_async_copy(tokens(r), wide_cots.at[r - 1], sems.at[1 + r]) for r in range(1, count)]
    for c in copies:
        c.start()
    for c in copies:
        c.wait()
    for r in range(1, count):
        cots[r - 1][...] = wide_cots[r - 1].astype(bf)


def gate_kernel(v, out):
    out[...] = v[...]


def tokens_kernel(patch, *refs):
    samples, mask, bi, bfin, gain = refs[:5]
    hbm = refs[5:16]
    patches, hid, dhid, embed, normed, qkv, sigma_row, center_row = refs[16:24]
    vmem, sems = refs[24:35], refs[35]
    copies = [pltpu.make_async_copy(h, v, sems.at[i]) for i, (h, v) in enumerate(zip(hbm, vmem))]
    for c in copies:
        c.start()
    wi, wfin, wskip, wq, wk, wv = vmem[:6]
    series, points = samples.shape
    tokens = points // patch
    rows = series * tokens
    observed = mask[...].astype(f32)
    _, _, center, offset, _, sigma = series_stats(samples[...], observed, patch)
    sigma_row[...] = token_row(sigma, rows)
    center_row[...] = token_row(center, rows)
    scaled = (observed * offset / sigma).astype(bf)
    spread_rows = (iota((rows, series), 0) // tokens == iota((rows, series), 1)).astype(f32).astype(bf)
    own = (iota((rows, points), 1) // patch == iota((rows, points), 0) % tokens).astype(f32)
    col = iota((points, 2 * patch), 0) % patch
    lane = iota((points, 2 * patch), 1)
    fold_s = (col == lane).astype(f32).astype(bf)
    fold_o = (col + patch == lane).astype(f32).astype(bf)
    es = (dot(spread_rows, scaled) * own).astype(bf)
    eo = (dot(spread_rows, observed.astype(bf)) * own).astype(bf)
    p = (dot(es, fold_s) + dot(eo, fold_o)).astype(bf)
    patches[...] = p
    for c in copies[:3]:
        c.wait()
    acc = dot(p, wskip[...]) + bfin[...][None, :]
    for j in range(0, wi.shape[1], WIDE):
        t = slice(j, j + WIDE)
        h, d = silu_parts(dot(p, wi[:, t]) + bi[t][None, :])
        h = h.astype(bf)
        hid[:, t] = h
        dhid[:, t] = d.astype(bf)
        acc = acc + dot(h, wfin[t, :])
    embed[...] = acc
    n = (acc * rms(acc) * gain[...][None, :]).astype(bf)
    normed[...] = n
    inner = wq.shape[1]
    for i, w in enumerate((wq, wk, wv)):
        copies[3 + i].wait()
        qkv[:, i * inner:(i + 1) * inner] = dot(n, w[...]).astype(bf)
    for c in copies[6:]:
        c.wait()


def block_mask():
    return (iota((128, 256), 0) // 32 == iota((128, 256), 1) // 64).astype(f32).astype(bf)


def spread_heads(v, keep):
    return jnp.concatenate([v] * 4, axis=0) * keep


def pick_heads(v):
    head = iota((32, 256), 1) // 64
    out = v[0:32]
    for h in range(1, 4):
        out = jnp.where(head == h, v[32 * h:32 * h + 32], out)
    return out


def pairs(rows):
    for i in range(rows // 16):
        yield i, slice(32 * (i // 2), 32 * (i // 2) + 32), 256 * (i % 2)


def attend_kernel(qkv, probs, mixed):
    keep = block_mask()
    inner = HEADS * HEAD_DIM
    rows = qkv.shape[0]
    for i, s, c in pairs(rows):
        q = spread_heads(qkv[s, c:c + 256], keep)
        probs[i] = dot_nt(qkv[s, inner + c:inner + c + 256], q)
    for i in range(0, rows // 16, 4):
        v = probs[i:i + 4] * SCALE
        e = jnp.exp(v - jnp.max(v, axis=1, keepdims=True))
        probs[i:i + 4] = e / jnp.sum(e, axis=1, keepdims=True)
    for i, s, c in pairs(rows):
        v = qkv[s, 2 * inner + c:2 * inner + c + 256]
        mixed[s, c:c + 256] = pick_heads(dot_tn(probs[i].astype(bf), v)).astype(bf)


def ffn_kernel(embed, mixed, wm, gain, we, wc, wri, bri, middle, normed, hid, dhid, states, hidh, dh):
    mid = embed[...] + dot(mixed[...], wm[...])
    middle[...] = mid
    n = (mid * rms(mid) * gain[...][None, :]).astype(bf)
    normed[...] = n
    acc = mid
    for j in range(0, we.shape[1], WIDE):
        t = slice(j, j + WIDE)
        h, d = silu_parts(dot(n, we[:, t]))
        h = h.astype(bf)
        hid[:, t] = h
        dhid[:, t] = d.astype(bf)
        acc = acc + dot(h, wc[t, :])
    st = acc.astype(bf)
    states[...] = st
    for j in range(0, wri.shape[1], WIDE):
        t = slice(j, j + WIDE)
        h, d = silu_parts(dot(st, wri[:, t]) + bri[t][None, :])
        hidh[:, t] = h.astype(bf)
        dh[:, t] = d.astype(bf)


HEAD_ORDER = "pqxy"
FFN_PARTS = [
    ("xypq", [("down", 0), ("down", 1), ("down", 2), ("up", 0), ("up", 1)]),
    ("yqxp", [("inner", 0), ("inner", 1), ("inner", 2), ("up", 2), ("vector", 0)]),
]
TOKEN_PARTS = [
    ("xpyq", [("final", 0), ("final", 1), ("final", 2), ("small", 0)]),
    ("yxpq", [("attention", 0), ("attention", 1), ("attention", 2), ("merge", 0), ("merge", 1), ("merge", 2)]),
]
SLAB_ROWS = {"merge": 16, "vector": 16, "small": 16}


def part_rows(items):
    return sum(SLAB_ROWS.get(name, 48) for name, _ in items)


def layout(parts):
    out = {}
    for p, (_, items) in enumerate(parts):
        at = 0
        for item in items:
            out[item] = p, at
            at += SLAB_ROWS.get(item[0], 48)
    return out


def sizes(parts):
    return [(part_rows(items), order) for order, items in parts]


def put_matrix(scrs, mes, where, name, tile, value):
    value = value.astype(bf)
    for k in range(3):
        p, at = where[name, k]
        for i in range(8):
            scrs[p][(8 * tile + i) ^ mes[p], at:at + 48, :] = value[48 * i:48 * i + 48, 128 * k:128 * k + 128]


def ship(sources, keep, send):
    at = 0
    for v, first, rows in sources:
        n = v.shape[0] // 2
        keep[:, at:at + rows] = v[:n, first:first + rows]
        send[:, at:at + rows] = v[n:, first:first + rows]
        at += rows


def index_bits(index, count):
    return [(index // (1 << (count - 1 - k))) % 2 for k in range(count)]


def rows_of(tmp, row, v):
    for j in range(0, v.shape[1], 128):
        tmp[row:row + 1, :] = v[:, j:j + 128]
        row += 1
    return row


def columns_kernel(count, masks, *refs):
    states, hidh, sigma = refs[:3]
    cots, refs = refs[3:3 + count], refs[3 + count:]
    groups = max(count // 2, 1)
    outs, (tmp, *scrs) = refs[:2 * groups], refs[2 * groups:]
    me = me_of(masks, count)
    st = states[...]
    width = hidh.shape[1]
    cols = tmp.shape[0]
    for r in range(count):
        turned = (cots[r][...].astype(f32) * sigma[...]).astype(bf)
        scr = scrs[r // 2]

        def put(c, v):
            core, *others = index_bits(c ^ me, 4)
            at = core
            for axis in HEAD_ORDER.replace("d", "yx").replace("z", "qp"):
                at = at * 2 + (r % 2 if axis == "x" else others.pop(0))
            scr[at] = v

        for j in range(0, width, TILE):
            v = dot(turned, hidh[:, j:j + TILE]).astype(bf)
            for i in range(TILE // 128):
                put(j // 128 + i, v[:, 128 * i:128 * i + 128])
        v = dot(turned, st).astype(bf)
        for i in range(st.shape[1] // 128):
            put(width // 128 + i, v[:, 128 * i:128 * i + 128])
        tmp[...] = jnp.zeros_like(tmp)
        bias = dot_nt(jnp.ones((8, turned.shape[1]), bf), turned)
        for row, j in enumerate(range(0, cols, 128)):
            n = min(128, cols - j)
            tmp[row:row + 1, 0:n] = bias[0:1, j:j + n]
        put(15, tmp[...].astype(bf))
    for i in range(groups):
        ship([(scrs[i], 0, cols)], *outs[2 * i:2 * i + 2])


def head_kernel(count, *refs):
    dh, sigma = refs[:2]
    refs = refs[2:]
    cots, refs = refs[:count], refs[count:]
    whz, refs = refs[0], refs[1:]
    far, refs = refs[:2 * (count - 1)], refs[2 * (count - 1):]
    gpre, sums = refs[:2]
    gs, mats = refs[2:2 + count], refs[2 + count:]
    width = dh.shape[1]
    half = width // 2
    core = lax.axis_index("wide") % 2
    for r in range(count - 1):
        for k, c in enumerate((core, 1 - core)):
            mats[r][:, pl.ds(pl.multiple_of(c * half, 128), half)] = far[2 * r + k][...]
    mats = [whz] + list(mats)
    grads = [(c[...].astype(f32) * sigma[...]).astype(bf).T for c in cots]
    for o, g in zip(gs, grads):
        o[...] = g
    for j in range(0, width, WIDE):
        t = slice(j, j + WIDE)
        acc = dot(grads[0], mats[0][:, t])
        for r in range(1, count):
            acc = acc + dot(grads[r], mats[r][:, t])
        gp = (acc * dh[:, t].astype(f32)).astype(bf)
        gpre[:, t] = gp
        sums[:, t] = jnp.sum(gp.astype(f32), axis=0, keepdims=True)


def ffn_back_kernel(count, masks, states, gpre, sums, wri, hid, dhid, normed, middle, wc, we, gain, *refs):
    gs, shorts, refs = refs[:count], refs[count:2 * count], refs[2 * count:]
    gmiddle, keep, send, *scrs, tmp = refs
    mes = [me_of(m, count) for m in masks]
    where = layout(FFN_PARTS)
    acc = dot_nt(gpre[...], wri[...])
    for r in range(count):
        acc = acc + dot(gs[r][...], shorts[r][:, :wri.shape[0]])
    g = acc.astype(bf)
    nt = normed[...].T
    acc = None
    for j in range(4):
        t = slice(TILE * j, TILE * j + TILE)
        gp = (dot_nt(g, wc[t, :]) * dhid[:, t].astype(f32)).astype(bf)
        part = dot_nt(gp, we[:, t])
        acc = part if acc is None else acc + part
        put_matrix(scrs, mes, where, "up", j, dot(nt, gp))
        put_matrix(scrs, mes, where, "down", j, dot_tn(hid[:, t], g))
    back, gg = norm_back(acc, middle[...], gain[...][None, :])
    gmiddle[...] = (g.astype(f32) + back).astype(bf)
    st = states[...].T
    for j in range(4):
        put_matrix(scrs, mes, where, "inner", j, dot(st, gpre[:, TILE * j:TILE * j + TILE]))
    p, at = where["vector", 0]
    scrs[p][:, at:at + 16, :] = jnp.zeros((32, 16, 128), bf)
    tmp[...] = jnp.zeros_like(tmp)
    row = rows_of(tmp, 0, sums[...])
    rows_of(tmp, row, gg)
    scrs[p][mes[p], at:at + 16, :] = tmp[...].astype(bf)
    ship([(v, 0, v.shape[1]) for v in scrs], keep, send)


def attend_back_kernel(gmiddle, wm, qkv, probs, gqkv, gmix, gprobs, low):
    keep = block_mask()
    inner = HEADS * HEAD_DIM
    rows = qkv.shape[0]
    gmix[...] = dot_nt(gmiddle[...], wm[...]).astype(bf)
    for i, s, c in pairs(rows):
        g = spread_heads(gmix[s, c:c + 256], keep)
        gprobs[i] = dot_nt(qkv[s, 2 * inner + c:2 * inner + c + 256], g)
        gqkv[s, 2 * inner + c:2 * inner + c + 256] = dot(probs[i].astype(bf), g).astype(bf)
    for i in range(0, rows // 16, 4):
        p, g = probs[i:i + 4], gprobs[i:i + 4]
        low[i:i + 4] = (p * (g - jnp.sum(g * p, axis=1, keepdims=True))).astype(bf)
    for i, s, c in pairs(rows):
        ds = low[i]
        q = spread_heads(qkv[s, c:c + 256], keep)
        k = qkv[s, inner + c:inner + c + 256]
        gqkv[s, c:c + 256] = (pick_heads(dot_tn(ds, k)) * SCALE).astype(bf)
        gqkv[s, inner + c:inner + c + 256] = (dot(ds, q) * SCALE).astype(bf)


def project_back_kernel(count, masks, gqkv, gmiddle, mixed, normed, embed, wq, wk, wv, gain, gembed, ggain,
                        *scrs):
    mes = [me_of(m, count) for m in masks]
    where = layout(TOKEN_PARTS)
    inner = wq.shape[1]
    acc = dot_nt(gqkv[:, :inner], wq[...])
    acc = acc + dot_nt(gqkv[:, inner:2 * inner], wk[...])
    acc = acc + dot_nt(gqkv[:, 2 * inner:], wv[...])
    back, gg = norm_back(acc, embed[...], gain[...][None, :])
    ggain[...] = gg
    gm = gmiddle[...]
    gembed[...] = (gm.astype(f32) + back).astype(bf)
    nt = normed[...].T
    for j in range(4):
        put_matrix(scrs, mes, where, "attention", j, dot(nt, gqkv[:, TILE * j:TILE * j + TILE]))
    v = dot_tn(mixed[...], gm).astype(bf)
    for k in range(3):
        p, at = where["merge", k]
        for i in range(32):
            scrs[p][i ^ mes[p], at:at + 16, :] = v[16 * i:16 * i + 16, 128 * k:128 * k + 128]


def tokens_back_kernel(count, masks, patch, gembed, hid, dhid, patches, wfin, wskip, wi, gain_one, *refs):
    n = len(masks)
    earlier, (gpatches, keep, send), scrs, tmp = refs[:n], refs[n:n + 3], refs[n + 3:2 * n + 3], refs[-1]
    mes = [me_of(m, count) for m in masks]
    where = layout(TOKEN_PARTS)
    g = gembed[...]
    p = patches[...]
    pt = p.T
    tmp[...] = jnp.zeros_like(tmp)
    gpat = dot_nt(g, wskip[...])
    row = 480
    for j in range(4):
        t = slice(TILE * j, TILE * j + TILE)
        gp = (dot_nt(g, wfin[t, :]) * dhid[:, t].astype(f32)).astype(bf)
        gpat = gpat + dot_nt(gp, wi[:, t])
        v = dot(pt, gp)
        for i in range(3):
            c = 3 * j + i
            tmp[32 * c:32 * c + 32, :] = v[:, 128 * i:128 * i + 128]
        row = rows_of(tmp, row, jnp.sum(gp.astype(f32), axis=0, keepdims=True))
        put_matrix(scrs, mes, where, "final", j, dot_tn(hid[:, t], g))
    v = dot(pt, g)
    for i in range(3):
        tmp[384 + 32 * i:416 + 32 * i, :] = v[:, 128 * i:128 * i + 128]
    row = rows_of(tmp, row, jnp.sum(g.astype(f32), axis=0, keepdims=True))
    rows_of(tmp, row, gain_one[...])
    p, at = where["small", 0]
    for b in range(32):
        scrs[p][b ^ mes[p], at:at + 16, :] = tmp[16 * b:16 * b + 16].astype(bf)
    ship([((earlier if item[0] in ("attention", "merge") else scrs)[where[item][0]], where[item][1],
           SLAB_ROWS.get(item[0], 48)) for _, items in TOKEN_PARTS for item in items], keep, send)
    gpatches[...] = gpat


def forecast_kernel(count, patch, *refs):
    samples, mask, gpatches, hid, states, sigma_row, center_row = refs[:7]
    refs = refs[7:]
    mats, refs = refs[:count], refs[count:]
    short, refs = refs[:count], refs[count:]
    offsets, refs = refs[:count], refs[count:]
    cots, refs = refs[:count], refs[count:]
    preds, series_grad = refs[:count], refs[count]
    sg = sigma_row[...]
    ct = center_row[...]
    st = states[...]
    ones = jnp.ones((1, 128), bf)
    row_c, row_s = 0.0, 0.0
    for r in range(count):
        added_bias = dot_tn(offsets[r][...].astype(f32)[None, :].astype(bf), ones)[:, :1]
        raw = dot_nt(mats[r][...], hid[...]) + dot_nt(short[r][...], st) + added_bias
        preds[r][...] = (raw * sg + ct).astype(preds[r].dtype)
        c = cots[r][...].astype(f32)
        row_c = row_c + jnp.sum(c, axis=0, keepdims=True)
        row_s = row_s + jnp.sum(c * raw, axis=0, keepdims=True)
    observed = mask[...].astype(f32)
    series = samples.shape[0]
    first, cnt, center, offset, spread, sigma = series_stats(samples[...], observed, patch)
    out_c = series_column(row_c, series)
    out_s = series_column(row_s, series)
    points = samples.shape[1]
    per_series = points // patch
    rows = series * per_series
    lane = iota((2 * patch, points), 1) % patch
    fold = (iota((2 * patch, points), 0) == lane).astype(f32).astype(bf)
    own = (iota((rows, points), 1) // patch == iota((rows, points), 0) % per_series).astype(f32)
    gpat = gpatches[...]
    high = gpat.astype(bf)
    low = (gpat - high.astype(f32)).astype(bf)
    full = (dot(high, fold) + dot(low, fold)) * own
    og = observed * jnp.sum(full.reshape(series, per_series, points), axis=1)
    g_center = out_c - jnp.sum(og, axis=1, keepdims=True) / sigma
    g_sigma = out_s - jnp.sum(og * offset, axis=1, keepdims=True) / (sigma * sigma)
    g_spread = jnp.where(spread > 1.0, g_sigma * 0.5 / sigma, 0.0)
    g_center = g_center - g_spread * 2.0 * jnp.sum(first * offset, axis=1, keepdims=True) / cnt
    series_grad[...] = og / sigma + g_spread * 2.0 * first * offset / cnt + g_center * first / cnt


def place_kernel(count, *refs):
    preds, out = refs[:count], refs[count]
    rows = preds[0].shape[1]
    narrow = lax.axis_index("narrow")
    for r in range(count):
        out[:, pl.ds(pl.multiple_of((narrow ^ r) * rows, 128), rows)] = preds[r][...].astype(f32)


def xor_send(v, mask, total):
    return lax.ppermute(v, AXES, [(i, i ^ mask) for i in range(total)])


def grouped(parts, level):
    groups = {}
    for p, (_, order) in enumerate(parts):
        groups.setdefault(order[level:], []).append(p)
    return list(groups.values())


def places(parts, groups):
    out = {}
    for g, members in enumerate(groups):
        at = 0
        for p in members:
            out[p] = g, at
            at += parts[p][0]
    return out


def combos(bits):
    out = [0]
    for b in bits:
        out = [o + s for o in out for s in (0, b)]
    return out


def starts(counts):
    return [sum(counts[:k]) for k in range(len(counts))]


def swaps(parts, head=False):
    return all(order[-1] in "xypq" for _, order in parts) and not (head and parts[0][1][-1] == "x")


def add_kernel(parts, before, came, after, split, *refs):
    ins, outs = refs[:sum(came)], refs[sum(came):]
    first, to = starts(came), starts(split)
    n = ins[0].shape[0]
    for p, (rows, _) in enumerate(parts):
        (g, a), (o, b) = before[p], after[p]
        step = n // split[o]
        for k in range(n):
            v = ins[first[g]][k, a:a + rows].astype(f32)
            for c in range(1, came[g]):
                v = v + ins[first[g] + c][k, a:a + rows].astype(f32)
            outs[to[o] + k // step][k % step, b:b + rows] = v.astype(bf)


def join_kernel(parts, before, came, after, *refs):
    ins, outs = refs[:sum(came)], refs[sum(came):]
    first = starts(came)
    for p, (rows, _) in enumerate(parts):
        (g, a), (o, b) = before[p], after[p]
        n = ins[first[g]].shape[0]
        for k in range(came[g]):
            outs[o][n * k:n * k + n, b:b + rows] = ins[first[g] + k][:, a:a + rows]


class Flow:
    def __init__(self, chain, total, bits, rest, parts, keep, send, name, head=False):
        self.chain, self.total, self.bits, self.rest, self.parts = chain, total, bits, rest, parts
        self.name, self.head = name, head
        self.swap = swaps(parts, head)
        self.level, self.down = 0, True
        self.groups = [list(range(len(parts)))]
        self.held = [[keep, self.to(send, bits["c"][0])]]

    def to(self, v, mask):
        with jax.named_scope(self.name + str(mask)):
            return xor_send(v, mask, self.total)

    def rows(self, group):
        return sum(self.parts[p][0] for p in group)

    def levels(self, group):
        return len(self.parts[group[0]][1])

    def masks(self, group, gather=False):
        bits = self.bits[self.parts[group[0]][1][self.level]]
        return combos([b for b in bits if not (gather and self.head and b == self.bits["x"][0])])[1:]

    def step(self):
        (self.add if self.down else self.join)()

    def add(self):
        before, came = places(self.parts, self.groups), [len(h) for h in self.held]
        n = self.held[0][0].shape[0]
        last = self.level == self.levels([0])
        if not last:
            self.groups = grouped(self.parts, self.level)
            whole = self.swap and self.level + 1 == self.levels([0])
            split = [1 if whole else 1 + len(self.masks(g)) for g in self.groups]
        else:
            if self.swap:
                self.groups = grouped(self.parts, self.level - 2)
            split = [1] * len(self.groups)
        shapes = [((n // c, self.rows(g), 128), bf) for g, c in zip(self.groups, split) for _ in range(c)]
        outs = self.chain(
            functools.partial(add_kernel, self.parts, before, came, places(self.parts, self.groups), split),
            shapes, [v for h in self.held for v in h], limit=4)
        at = starts(split)
        if not last:
            self.held = [[outs[k]] + [self.to(outs[k if whole else k + 1 + i], m) for i, m in enumerate(self.masks(g))]
                         for g, k in zip(self.groups, at)]
            self.level += 1
            return
        for m in self.rest:
            outs = [v + self.to(v, m) for v in outs]
        self.down = False
        if self.swap:
            self.level -= 1
        self.spread(outs)

    def spread(self, arrays):
        self.level -= 1
        if self.level >= 0 and not self.masks(self.groups[0], True):
            self.level -= 1
        if self.level < 0:
            self.held = [[a, self.to(a, self.bits["c"][0])] for a in arrays]
            return
        self.held = [[a] + [self.to(a, m) for m in self.masks(g, True)] for g, a in zip(self.groups, arrays)]

    def join(self):
        before, came = places(self.parts, self.groups), [len(h) for h in self.held]
        ns = {p: self.held[g][0].shape[0] * came[g] for p, (g, _) in before.items()}
        up = self.level - 1
        self.groups = grouped(self.parts, up) if up >= 0 else [list(range(len(self.parts)))]
        outs = self.chain(
            functools.partial(join_kernel, self.parts, before, came, places(self.parts, self.groups)),
            [((ns[g[0]], self.rows(g), 128), bf) for g in self.groups], [v for h in self.held for v in h], limit=4)
        self.spread(outs)


def assemble(refs, scr):
    k = 0
    for a in refs:
        scr[k:k + a.shape[0]] = a[...]
        k += a.shape[0]


def finder(scr, parts, masks, count):
    where, mes = layout(parts), [me_of(m, count) for m in masks]
    base = [sum(part_rows(items) for _, items in parts[:p]) for p in range(len(parts))]

    def find(name, k, b):
        p, at = where[name, k]
        at += base[p]
        return scr[b ^ mes[p], at:at + SLAB_ROWS.get(name, 48), :].astype(f32)

    return find


def vectors(tmp, row, outs):
    for o in outs:
        n = o.shape[0]
        for j in range(0, n, 128):
            o[pl.ds(j, 128)] = tmp[row]
            row += 1


def unpack_columns(count, masks, here, there, w, skip, bias, scr, tmp):
    me = me_of(masks, count)
    assemble((here, there), scr)
    cols, width = w.shape
    for b in range(width // 128):
        w[:, 128 * b:128 * b + 128] = scr[b ^ me].astype(f32)
    for i in range(skip.shape[1] // 128):
        skip[:, 128 * i:128 * i + 128] = scr[(width // 128 + i) ^ me].astype(f32)
    tmp[...] = scr[15 ^ me].astype(f32)
    bias[...] = jnp.concatenate([tmp[i:i + 1, :] for i in range(-(-cols // 128))], axis=1)[0, :cols]


def unpack_ffn(count, masks, here, there, inner, up, down, bias, gain, scr, tmp):
    assemble((here, there), scr)
    find = finder(scr, FFN_PARTS, masks, count)
    for b in range(32):
        j, i = b // 8, b % 8
        rows = slice(48 * i, 48 * i + 48)
        for k in range(3):
            cols = slice(TILE * j + 128 * k, TILE * j + 128 * k + 128)
            inner[rows, cols] = find("inner", k, b)
            up[rows, cols] = find("up", k, b)
            down[48 * b:48 * b + 48, 128 * k:128 * k + 128] = find("down", k, b)
    tmp[...] = find("vector", 0, 0)
    vectors(tmp, 0, (bias, gain))


def unpack_tokens(count, masks, here, there, gq, gk, gv, wo, out, tin, skip, bin_, bout, gain, scr, tmp):
    assemble((here, there), scr)
    find = finder(scr, TOKEN_PARTS, masks, count)
    for b in range(32):
        j, i = b // 8, b % 8
        tmp[16 * b:16 * b + 16, :] = find("small", 0, b)
        for k in range(3):
            c = TILE * j + 128 * k
            (gq, gk, gv)[c // 512][48 * i:48 * i + 48, c % 512:c % 512 + 128] = find("attention", k, b)
            out[48 * b:48 * b + 48, 128 * k:128 * k + 128] = find("final", k, b)
            wo[16 * b:16 * b + 16, 128 * k:128 * k + 128] = find("merge", k, b)
    for c in range(12):
        tin[:, 128 * c:128 * c + 128] = tmp[32 * c:32 * c + 32, :]
    for i in range(3):
        skip[:, 128 * i:128 * i + 128] = tmp[384 + 32 * i:416 + 32 * i, :]
    vectors(tmp, 480, (bin_, bout, gain))


def per_device(wide, count, signal_samples, present_mask, wi, bi, wfin, wskip, bfin, gain_one, wq, wk, wv, wm,
               gain_two, we, wc, wri, bri, whz, wrs, bro, cotangent):
    series, points = signal_samples.shape
    patch = wi.shape[0] // 2
    rows = series * (points // patch)
    dim, width = wri.shape
    cols = whz.shape[1]
    inner = wq.shape[1]
    total = wide * count
    X, CORE, Y, Z0, Z1 = 1, count, 2 * count, 4 * count, 8 * count
    bits = {"c": [CORE], "x": [X], "y": [Y], "p": [Z0], "q": [Z1], "d": [Y, X], "z": [Z1, Z0]}
    narrow_rest = [1 << i for i in range(1, count.bit_length() - 1)]
    wide_rest = [count << i for i in range(4, wide.bit_length() - 1)]
    def block_bits(parts, head=False):
        out = []
        for _, order in parts:
            own = [CORE] + [b for a in order for b in bits[a] if not (head and b == X)]
            out.append(own[:-1] + [0] if swaps(parts, head) else own)
        return out

    ffn_masks, token_masks = block_bits(sizes(FFN_PARTS)), block_bits(sizes(TOKEN_PARTS))
    (column_masks,) = block_bits([(cols, HEAD_ORDER)], True)
    ffn_rows, token_rows = ([r for r, _ in sizes(parts)] for parts in (FFN_PARTS, TOKEN_PARTS))
    chain = Chain()
    vmem = pltpu.VMEM

    whz_t, wrs_t, cot_t = whz.T, wrs.T, cotangent.T
    prepared = chain(
        functools.partial(prepare_kernel, count, rows),
        [((cols, rows), bf)] * (count - 1)
        + [((cols, rows), f32), ((cols, width // 2), bf)],
        [], raw=[cot_t, whz_t],
        scratch=[vmem((max(count - 1, 1), cols, rows), f32), pltpu.SemaphoreType.DMA((count + 1,))], limit=24)
    own_cot, mine = prepared[count - 1:]
    cots = [own_cot] + [xor_send(prepared[r - 1], r, total) for r in range(1, count)]
    far = [xor_send(mine, r, total) for r in range(1, count)]
    shorts = [wrs_t] + [xor_send(wrs_t, r, total) for r in range(1, count)]
    offsets = [bro] + [xor_send(bro, r, total) for r in range(1, count)]

    weights = [wi, wfin, wskip, wq, wk, wv, wm, we, wc, wri, whz_t]
    out = chain(
        functools.partial(tokens_kernel, patch),
        [((rows, 2 * patch), bf), ((rows, width), bf), ((rows, width), bf), ((rows, dim), f32), ((rows, dim), bf),
         ((rows, 3 * inner), bf), ((1, rows), f32), ((1, rows), f32)] + [(w.shape, bf) for w in weights],
        [signal_samples, present_mask, bi, bfin, gain_one], raw=weights,
        scratch=[pltpu.SemaphoreType.DMA((len(weights),))])
    patches, hid1, d1, embed, normed1, qkv, sigma, center = out[:8]
    wi, wfin, wskip, wq, wk, wv, wm, we, wc, wri, whz_t = out[8:]

    probs, mixed = chain(attend_kernel, [((2 * series, 32, 128), f32), ((rows, inner), bf)], [qkv])
    middle, normed2, hid2, d2, states, hidh, dh = chain(
        ffn_kernel,
        [((rows, dim), f32), ((rows, dim), bf), ((rows, width), bf), ((rows, width), bf), ((rows, dim), bf),
         ((rows, width), bf), ((rows, width), bf)],
        [embed, mixed, wm, gain_two, we, wc, wri, bri])

    groups = max(count // 2, 1)

    def columns():
        out = chain(
            functools.partial(columns_kernel, count, column_masks), [((16, cols, 128), bf)] * (2 * groups),
            [states, hidh, sigma] + cots,
            scratch=[vmem((cols, 128), f32)] + [vmem((32, cols, 128), bf)] * groups, limit=24)
        first = list(out[:2])
        for i in range(1, groups):
            for k in range(2):
                first[k] = first[k] + xor_send(out[2 * i + k], 2 * i, total)
        return Flow(chain, total, bits, wide_rest, [(cols, HEAD_ORDER)], *first, "columns", head=True)

    def gate():
        out = []
        for v in far:
            (v,) = chain(gate_kernel, [(v.shape, bf)], [v], limit=4)
            out += [v, xor_send(v, CORE, total)]
        return out

    def head():
        out = chain(
            functools.partial(head_kernel, count),
            [((rows, width), bf), ((1, width), f32)] + [((rows, cols), bf)] * count
            + [((cols, width), bf)] * (count - 1),
            [dh, sigma] + cots + [whz_t] + far_both)
        return out[0], out[1], out[2:2 + count], [whz_t] + out[2 + count:]

    def ffn_back():
        gmiddle, keep, send = chain(
            functools.partial(ffn_back_kernel, count, ffn_masks),
            [((rows, dim), bf)] + [((16, sum(ffn_rows), 128), bf)] * 2,
            [states, gpre, sums, wri, hid2, d2, normed2, middle, wc, we, gain_two] + gs + shorts,
            scratch=[vmem((32, n, 128), bf) for n in ffn_rows] + [vmem((16, 128), f32)])
        return gmiddle, Flow(chain, total, bits, narrow_rest + wide_rest, sizes(FFN_PARTS), keep, send, "ffn")

    def attend_back():
        return chain(attend_back_kernel, [((rows, 3 * inner), bf)], [gmiddle, wm, qkv, probs],
                     scratch=[vmem((rows, inner), bf), vmem(probs.shape, f32), vmem(probs.shape, bf)])[0]

    def project_back():
        return chain(
            functools.partial(project_back_kernel, count, token_masks),
            [((rows, dim), bf), ((1, dim), f32)] + [((32, n, 128), bf) for n in token_rows],
            [gqkv, gmiddle, mixed, normed1, embed, wq, wk, wv, gain_one])

    def tokens_back():
        gpatches, keep, send = chain(
            functools.partial(tokens_back_kernel, count, token_masks, patch),
            [((rows, 2 * patch), f32)] + [((16, sum(token_rows), 128), bf)] * 2,
            [gembed, hid1, d1, patches, wfin, wskip, wi, gg1] + earlier,
            scratch=[vmem((32, n, 128), bf) for n in token_rows] + [vmem((512, 128), f32)])
        return gpatches, Flow(chain, total, bits, narrow_rest + wide_rest, sizes(TOKEN_PARTS), keep, send, "tokens")

    def forecast():
        out = chain(
            functools.partial(forecast_kernel, count, patch),
            [((cols, rows), f32)] + [((cols, rows), bf)] * (count - 1) + [((series, points), f32)],
            [signal_samples, present_mask, gpatches, hidh, states, sigma, center] + mats + shorts + offsets + cots)
        return [out[0]] + [xor_send(out[r], r, total) for r in range(1, count)], out[count]

    def place():
        return chain(functools.partial(place_kernel, count), [((cols, count * rows), f32)], preds)[0]

    def finish_columns():
        return chain(functools.partial(unpack_columns, count, column_masks),
                     [((cols, width), f32), ((cols, dim), f32), ((cols,), f32)],
                     one.held[0], scratch=[vmem((16, cols, 128), bf), vmem((cols, 128), f32)], limit=24)

    def finish_ffn():
        return chain(functools.partial(unpack_ffn, count, ffn_masks),
                     [((dim, width), f32)] * 2 + [((width, dim), f32), ((width,), f32), ((dim,), f32)], two.held[0],
                     scratch=[vmem((32, sum(ffn_rows), 128), bf), vmem((16, 128), f32)], limit=24)

    def finish_tokens():
        return chain(
            functools.partial(unpack_tokens, count, token_masks),
            [((dim, inner), f32)] * 3 + [((inner, dim), f32), ((width, dim), f32), ((2 * patch, width), f32),
                                         ((2 * patch, dim), f32), ((width,), f32), ((dim,), f32), ((dim,), f32)],
            three.held[0], scratch=[vmem((32, sum(token_rows), 128), bf), vmem((512, 128), f32)], limit=24)

    far_both = gate()
    one = columns()
    gpre, sums, gs, mats = head()
    gmiddle, two = ffn_back()
    gqkv = attend_back()
    gembed, gg1, *earlier = project_back()
    two.step()
    gpatches, three = tokens_back()
    one.step()
    three.step()
    two.step()
    three.step()
    one.step()
    three.step()
    preds, g_series = forecast()
    two.step()
    three.step()
    one.step()
    two.step()
    prediction = place()
    three.step()
    one.step()
    two.step()
    three.step()
    two.step()
    one.step()
    three.step()
    two.step()
    one.step()
    three.step()
    two.step()
    one.step()
    tokens_out = finish_tokens()
    ffn_out = finish_ffn()
    columns_out = finish_columns()
    g_hw, g_hs, g_hb = columns_out
    g_hiw, g_up, g_down, g_hib, g_g2 = ffn_out
    g_q, g_k, g_v, g_wo, g_to, g_ti, g_ts, g_tib, g_tob, g_g1 = tokens_out
    return (prediction.T, g_series, g_ti, g_tib, g_to, g_ts, g_tob, g_g1, g_q, g_k, g_v, g_wo, g_g2, g_up, g_down,
            g_hiw, g_hib, g_hw.T, g_hs.T, g_hb)


def solution(mesh):
    wide, count = mesh.shape["wide"], mesh.shape["narrow"]
    both = P(("wide", "narrow"), None)
    return jax.shard_map(
        functools.partial(per_device, wide, count),
        mesh=mesh,
        in_specs=(both, both) + (P(),) * 15 + (P(None, "narrow"), P(None, "narrow"), P("narrow"), P("wide", "narrow")),
        out_specs=(P("wide", "narrow"), both) + (P(),) * 15
        + (P(None, "narrow"), P(None, "narrow"), P("narrow")),
        check_vma=False,
    )
```

```python
import functools

import jax
import jax.numpy as jnp
from jax import lax
from jax.experimental import pallas as pl
from jax.experimental.pallas import tpu as pltpu
from jax.sharding import PartitionSpec as P

HEADS = 8
HEAD_DIM = 64
EPS = 1e-06
SCALE = HEAD_DIM ** (-0.5)
bf = jnp.bfloat16
f32 = jnp.float32
TILE = 384
WIDE = 256
AXES = ("wide", "narrow")
MIB = 1 << 20
COSTS = {31: 15000000000, 20: 6000000000, 12: 30000000000, 19: 30000000000, 35: 20000000000, 27: 30000000000, 5: 10000000000, 21: 10000000000, 28: 6000000000, 23: 30000000000, 29: 6000000000, 32: 30000000000, 26: 10000000000, 10: 3000000000, 8: 20000000000, 38: 10000000000}


def dot(a, b):
    return lax.dot_general(a, b, (((1,), (0,)), ((), ())), preferred_element_type=f32)


def dot_nt(a, b):
    return lax.dot_general(a, b, (((1,), (1,)), ((), ())), preferred_element_type=f32)


def dot_tn(a, b):
    return lax.dot_general(a, b, (((0,), (0,)), ((), ())), preferred_element_type=f32)


class Chain:
    def __init__(self):
        self.last = None
        self.calls = 0

    def __call__(self, kernel, outs, args, scratch=(), limit=16, raw=()):
        vmem = pl.BlockSpec(memory_space=pltpu.VMEM)
        hbm = pl.BlockSpec(memory_space=pl.ANY)
        args, raw = list(args), [pltpu.with_memory_space_constraint(v, pltpu.HBM) for v in raw]
        deps = [] if self.last is None or any(a is self.last for a in args) else [self.last]
        n, d = len(args) + len(raw), len(deps)
        cost = COSTS.get(self.calls, 1000)
        self.calls += 1

        def body(*refs):
            kernel(*refs[:n], *refs[n + d:])

        name = getattr(kernel, "__name__", None) or kernel.func.__name__
        res = list(pl.pallas_call(
            body,
            name=name,
            out_shape=[jax.ShapeDtypeStruct(s, d) for s, d in outs],
            in_specs=[vmem] * len(args) + [pl.BlockSpec(memory_space=pltpu.HBM)] * len(raw) + [hbm] * d,
            out_specs=[vmem] * len(outs),
            scratch_shapes=list(scratch),
            cost_estimate=pl.CostEstimate(flops=cost, bytes_accessed=1000, transcendentals=0),
            compiler_params=pltpu.CompilerParams(vmem_limit_bytes=limit * MIB),
        )(*args, *raw, *deps))
        self.last = min(res, key=lambda r: r.size)
        return res


def silu_parts(v):
    s = 0.5 * jnp.tanh(0.5 * v) + 0.5
    h = v * s
    return h, s + h * (1.0 - s)


def iota(shape, dim):
    return lax.broadcasted_iota(jnp.int32, shape, dim)


def series_stats(samples, observed, patch):
    first = jnp.where(iota(samples.shape, 1) < patch, observed, 0.0)
    count = jnp.maximum(jnp.sum(first, axis=1, keepdims=True), 1.0)
    center = jnp.sum(first * samples, axis=1, keepdims=True) / count
    offset = samples - center
    spread = jnp.sum(first * offset * offset, axis=1, keepdims=True) / count
    sigma = jnp.sqrt(jnp.maximum(spread, 1.0))
    return first, count, center, offset, spread, sigma


def rms(v):
    return lax.rsqrt(jnp.mean(v * v, axis=-1, keepdims=True) + EPS)


def norm_back(g, v, gain):
    r = rms(v)
    u = v * r
    w = g * gain
    grad_gain = jnp.sum(g * u, axis=0, keepdims=True)
    return r * (w - u * jnp.mean(w * u, axis=-1, keepdims=True)), grad_gain


def token_row(v, rows):
    series = v.shape[0]
    own = iota((series, rows), 1) // (rows // series) == iota((series, rows), 0)
    return jnp.sum(jnp.where(own, v, 0.0), axis=0, keepdims=True)


def series_column(v, series):
    rows = v.shape[1]
    own = iota((series, rows), 1) // (rows // series) == iota((series, rows), 0)
    return jnp.sum(jnp.where(own, v, 0.0), axis=1, keepdims=True)


def me_of(masks, count):
    index = lax.axis_index("wide") * count + lax.axis_index("narrow")
    out = jnp.int32(0)
    for m in masks:
        out = out * 2 + ((index // m) % 2 if m else 0)
    return out


def prepare_kernel(count, rows, cot, whz, *refs):
    cots, (own, mine) = refs[:count - 1], refs[count - 1:count + 1]
    wide_cots, sems = refs[count + 1:]
    narrow = lax.axis_index("narrow")
    core = lax.axis_index("wide") % 2
    width = mine.shape[1]

    def tokens(r):
        return cot.at[:, pl.ds(pl.multiple_of((narrow ^ r) * rows, 128), rows)]

    copies = [
        pltpu.make_async_copy(whz.at[:, pl.ds(pl.multiple_of(core * width, 128), width)], mine, sems.at[0]),
        pltpu.make_async_copy(tokens(0), own, sems.at[1]),
    ] + [pltpu.make_async_copy(tokens(r), wide_cots.at[r - 1], sems.at[1 + r]) for r in range(1, count)]
    for c in copies:
        c.start()
    for c in copies:
        c.wait()
    for r in range(1, count):
        cots[r - 1][...] = wide_cots[r - 1].astype(bf)


def gate_kernel(v, out):
    out[...] = v[...]


def tokens_kernel(patch, *refs):
    samples, mask, bi, bfin, gain = refs[:5]
    hbm = refs[5:16]
    patches, hid, dhid, embed, normed, qkv, sigma_row, center_row = refs[16:24]
    vmem, sems = refs[24:35], refs[35]
    copies = [pltpu.make_async_copy(h, v, sems.at[i]) for i, (h, v) in enumerate(zip(hbm, vmem))]
    for c in copies:
        c.start()
    wi, wfin, wskip, wq, wk, wv = vmem[:6]
    series, points = samples.shape
    tokens = points // patch
    rows = series * tokens
    observed = mask[...].astype(f32)
    _, _, center, offset, _, sigma = series_stats(samples[...], observed, patch)
    sigma_row[...] = token_row(sigma, rows)
    center_row[...] = token_row(center, rows)
    scaled = (observed * offset / sigma).astype(bf)
    spread_rows = (iota((rows, series), 0) // tokens == iota((rows, series), 1)).astype(f32).astype(bf)
    own = (iota((rows, points), 1) // patch == iota((rows, points), 0) % tokens).astype(f32)
    col = iota((points, 2 * patch), 0) % patch
    lane = iota((points, 2 * patch), 1)
    fold_s = (col == lane).astype(f32).astype(bf)
    fold_o = (col + patch == lane).astype(f32).astype(bf)
    es = (dot(spread_rows, scaled) * own).astype(bf)
    eo = (dot(spread_rows, observed.astype(bf)) * own).astype(bf)
    p = (dot(es, fold_s) + dot(eo, fold_o)).astype(bf)
    patches[...] = p
    for c in copies[:3]:
        c.wait()
    acc = dot(p, wskip[...]) + bfin[...][None, :]
    for j in range(0, wi.shape[1], WIDE):
        t = slice(j, j + WIDE)
        h, d = silu_parts(dot(p, wi[:, t]) + bi[t][None, :])
        h = h.astype(bf)
        hid[:, t] = h
        dhid[:, t] = d.astype(bf)
        acc = acc + dot(h, wfin[t, :])
    embed[...] = acc
    n = (acc * rms(acc) * gain[...][None, :]).astype(bf)
    normed[...] = n
    inner = wq.shape[1]
    for i, w in enumerate((wq, wk, wv)):
        copies[3 + i].wait()
        qkv[:, i * inner:(i + 1) * inner] = dot(n, w[...]).astype(bf)
    for c in copies[6:]:
        c.wait()


def block_mask():
    return (iota((128, 256), 0) // 32 == iota((128, 256), 1) // 64).astype(f32).astype(bf)


def spread_heads(v, keep):
    return jnp.concatenate([v] * 4, axis=0) * keep


def pick_heads(v):
    head = iota((32, 256), 1) // 64
    out = v[0:32]
    for h in range(1, 4):
        out = jnp.where(head == h, v[32 * h:32 * h + 32], out)
    return out


def pairs(rows):
    for i in range(rows // 16):
        yield i, slice(32 * (i // 2), 32 * (i // 2) + 32), 256 * (i % 2)


def attend_kernel(qkv, probs, mixed):
    keep = block_mask()
    inner = HEADS * HEAD_DIM
    rows = qkv.shape[0]
    for i, s, c in pairs(rows):
        q = spread_heads(qkv[s, c:c + 256], keep)
        probs[i] = dot_nt(qkv[s, inner + c:inner + c + 256], q)
    for i in range(0, rows // 16, 4):
        v = probs[i:i + 4] * SCALE
        e = jnp.exp(v - jnp.max(v, axis=1, keepdims=True))
        probs[i:i + 4] = e / jnp.sum(e, axis=1, keepdims=True)
    for i, s, c in pairs(rows):
        v = qkv[s, 2 * inner + c:2 * inner + c + 256]
        mixed[s, c:c + 256] = pick_heads(dot_tn(probs[i].astype(bf), v)).astype(bf)


def ffn_kernel(embed, mixed, wm, gain, we, wc, wri, bri, middle, normed, hid, dhid, states, hidh, dh):
    mid = embed[...] + dot(mixed[...], wm[...])
    middle[...] = mid
    n = (mid * rms(mid) * gain[...][None, :]).astype(bf)
    normed[...] = n
    acc = mid
    for j in range(0, we.shape[1], WIDE):
        t = slice(j, j + WIDE)
        h, d = silu_parts(dot(n, we[:, t]))
        h = h.astype(bf)
        hid[:, t] = h
        dhid[:, t] = d.astype(bf)
        acc = acc + dot(h, wc[t, :])
    st = acc.astype(bf)
    states[...] = st
    for j in range(0, wri.shape[1], WIDE):
        t = slice(j, j + WIDE)
        h, d = silu_parts(dot(st, wri[:, t]) + bri[t][None, :])
        hidh[:, t] = h.astype(bf)
        dh[:, t] = d.astype(bf)


HEAD_ORDER = "pqxy"
FFN_PARTS = [
    ("xypq", [("down", 0), ("down", 1), ("down", 2), ("up", 0), ("up", 1)]),
    ("yqxp", [("inner", 0), ("inner", 1), ("inner", 2), ("up", 2), ("vector", 0)]),
]
TOKEN_PARTS = [
    ("xpyq", [("final", 0), ("final", 1), ("final", 2), ("small", 0)]),
    ("yxpq", [("attention", 0), ("attention", 1), ("attention", 2), ("merge", 0), ("merge", 1), ("merge", 2)]),
]
SLAB_ROWS = {"merge": 16, "vector": 16, "small": 16}


def part_rows(items):
    return sum(SLAB_ROWS.get(name, 48) for name, _ in items)


def layout(parts):
    out = {}
    for p, (_, items) in enumerate(parts):
        at = 0
        for item in items:
            out[item] = p, at
            at += SLAB_ROWS.get(item[0], 48)
    return out


def sizes(parts):
    return [(part_rows(items), order) for order, items in parts]


def put_matrix(scrs, mes, where, name, tile, value):
    value = value.astype(bf)
    for k in range(3):
        p, at = where[name, k]
        for i in range(8):
            scrs[p][(8 * tile + i) ^ mes[p], at:at + 48, :] = value[48 * i:48 * i + 48, 128 * k:128 * k + 128]


def ship(sources, keep, send):
    at = 0
    for v, first, rows in sources:
        n = v.shape[0] // 2
        keep[:, at:at + rows] = v[:n, first:first + rows]
        send[:, at:at + rows] = v[n:, first:first + rows]
        at += rows


def index_bits(index, count):
    return [(index // (1 << (count - 1 - k))) % 2 for k in range(count)]


def rows_of(tmp, row, v):
    for j in range(0, v.shape[1], 128):
        tmp[row:row + 1, :] = v[:, j:j + 128]
        row += 1
    return row


def columns_kernel(count, masks, *refs):
    states, hidh, sigma = refs[:3]
    cots, refs = refs[3:3 + count], refs[3 + count:]
    groups = max(count // 2, 1)
    outs, (tmp, *scrs) = refs[:2 * groups], refs[2 * groups:]
    me = me_of(masks, count)
    st = states[...]
    width = hidh.shape[1]
    cols = tmp.shape[0]
    for r in range(count):
        turned = (cots[r][...].astype(f32) * sigma[...]).astype(bf)
        scr = scrs[r // 2]

        def put(c, v):
            core, *others = index_bits(c ^ me, 4)
            at = core
            for axis in HEAD_ORDER.replace("d", "yx").replace("z", "qp"):
                at = at * 2 + (r % 2 if axis == "x" else others.pop(0))
            scr[at] = v

        for j in range(0, width, 2 * WIDE):
            v = dot(turned, hidh[:, j:j + 2 * WIDE]).astype(bf)
            for i in range(2 * WIDE // 128):
                put(j // 128 + i, v[:, 128 * i:128 * i + 128])
        v = dot(turned, st).astype(bf)
        for i in range(st.shape[1] // 128):
            put(width // 128 + i, v[:, 128 * i:128 * i + 128])
        tmp[...] = jnp.zeros_like(tmp)
        bias = dot_nt(jnp.ones((8, turned.shape[1]), bf), turned)
        for row, j in enumerate(range(0, cols, 128)):
            n = min(128, cols - j)
            tmp[row:row + 1, 0:n] = bias[0:1, j:j + n]
        put(15, tmp[...].astype(bf))
    for i in range(groups):
        ship([(scrs[i], 0, cols)], *outs[2 * i:2 * i + 2])


def head_kernel(count, *refs):
    dh, sigma = refs[:2]
    refs = refs[2:]
    cots, refs = refs[:count], refs[count:]
    whz, refs = refs[0], refs[1:]
    far, refs = refs[:2 * (count - 1)], refs[2 * (count - 1):]
    gpre, sums = refs[:2]
    gs, mats = refs[2:2 + count], refs[2 + count:]
    width = dh.shape[1]
    half = width // 2
    core = lax.axis_index("wide") % 2
    for r in range(count - 1):
        for k, c in enumerate((core, 1 - core)):
            mats[r][:, pl.ds(pl.multiple_of(c * half, 128), half)] = far[2 * r + k][...]
    mats = [whz] + list(mats)
    grads = [(c[...].astype(f32) * sigma[...]).astype(bf).T for c in cots]
    for o, g in zip(gs, grads):
        o[...] = g
    for j in range(0, width, WIDE):
        t = slice(j, j + WIDE)
        acc = dot(grads[0], mats[0][:, t])
        for r in range(1, count):
            acc = acc + dot(grads[r], mats[r][:, t])
        gp = (acc * dh[:, t].astype(f32)).astype(bf)
        gpre[:, t] = gp
        sums[:, t] = jnp.sum(gp.astype(f32), axis=0, keepdims=True)


def ffn_back_kernel(count, masks, states, gpre, sums, wri, hid, dhid, normed, middle, wc, we, gain, *refs):
    gs, shorts, refs = refs[:count], refs[count:2 * count], refs[2 * count:]
    gmiddle, keep, send, *scrs, tmp = refs
    mes = [me_of(m, count) for m in masks]
    where = layout(FFN_PARTS)
    acc = dot_nt(gpre[...], wri[...])
    for r in range(count):
        acc = acc + dot(gs[r][...], shorts[r][:, :wri.shape[0]])
    g = acc.astype(bf)
    nt = normed[...].T
    acc = None
    for j in range(4):
        t = slice(TILE * j, TILE * j + TILE)
        gp = (dot_nt(g, wc[t, :]) * dhid[:, t].astype(f32)).astype(bf)
        part = dot_nt(gp, we[:, t])
        acc = part if acc is None else acc + part
        put_matrix(scrs, mes, where, "up", j, dot(nt, gp))
        put_matrix(scrs, mes, where, "down", j, dot_tn(hid[:, t], g))
    back, gg = norm_back(acc, middle[...], gain[...][None, :])
    gmiddle[...] = (g.astype(f32) + back).astype(bf)
    st = states[...].T
    for j in range(4):
        put_matrix(scrs, mes, where, "inner", j, dot(st, gpre[:, TILE * j:TILE * j + TILE]))
    p, at = where["vector", 0]
    scrs[p][:, at:at + 16, :] = jnp.zeros((32, 16, 128), bf)
    tmp[...] = jnp.zeros_like(tmp)
    row = rows_of(tmp, 0, sums[...])
    rows_of(tmp, row, gg)
    scrs[p][mes[p], at:at + 16, :] = tmp[...].astype(bf)
    ship([(v, 0, v.shape[1]) for v in scrs], keep, send)


def attend_back_kernel(gmiddle, wm, qkv, probs, gqkv, gmix, gprobs, low):
    keep = block_mask()
    inner = HEADS * HEAD_DIM
    rows = qkv.shape[0]
    gmix[...] = dot_nt(gmiddle[...], wm[...]).astype(bf)
    for i, s, c in pairs(rows):
        g = spread_heads(gmix[s, c:c + 256], keep)
        gprobs[i] = dot_nt(qkv[s, 2 * inner + c:2 * inner + c + 256], g)
        gqkv[s, 2 * inner + c:2 * inner + c + 256] = dot(probs[i].astype(bf), g).astype(bf)
    for i in range(0, rows // 16, 4):
        p, g = probs[i:i + 4], gprobs[i:i + 4]
        low[i:i + 4] = (p * (g - jnp.sum(g * p, axis=1, keepdims=True))).astype(bf)
    for i, s, c in pairs(rows):
        ds = low[i]
        q = spread_heads(qkv[s, c:c + 256], keep)
        k = qkv[s, inner + c:inner + c + 256]
        gqkv[s, c:c + 256] = (pick_heads(dot_tn(ds, k)) * SCALE).astype(bf)
        gqkv[s, inner + c:inner + c + 256] = (dot(ds, q) * SCALE).astype(bf)


def project_back_kernel(count, masks, gqkv, gmiddle, mixed, normed, embed, wq, wk, wv, gain, gembed, ggain,
                        *scrs):
    mes = [me_of(m, count) for m in masks]
    where = layout(TOKEN_PARTS)
    inner = wq.shape[1]
    acc = dot_nt(gqkv[:, :inner], wq[...])
    acc = acc + dot_nt(gqkv[:, inner:2 * inner], wk[...])
    acc = acc + dot_nt(gqkv[:, 2 * inner:], wv[...])
    back, gg = norm_back(acc, embed[...], gain[...][None, :])
    ggain[...] = gg
    gm = gmiddle[...]
    gembed[...] = (gm.astype(f32) + back).astype(bf)
    nt = normed[...].T
    for j in range(4):
        put_matrix(scrs, mes, where, "attention", j, dot(nt, gqkv[:, TILE * j:TILE * j + TILE]))
    v = dot_tn(mixed[...], gm).astype(bf)
    for k in range(3):
        p, at = where["merge", k]
        for i in range(32):
            scrs[p][i ^ mes[p], at:at + 16, :] = v[16 * i:16 * i + 16, 128 * k:128 * k + 128]


def tokens_back_kernel(count, masks, patch, gembed, hid, dhid, patches, wfin, wskip, wi, gain_one, *refs):
    n = len(masks)
    earlier, (gpatches, keep, send), scrs, tmp = refs[:n], refs[n:n + 3], refs[n + 3:2 * n + 3], refs[-1]
    mes = [me_of(m, count) for m in masks]
    where = layout(TOKEN_PARTS)
    g = gembed[...]
    p = patches[...]
    pt = p.T
    tmp[...] = jnp.zeros_like(tmp)
    gpat = dot_nt(g, wskip[...])
    row = 480
    for j in range(4):
        t = slice(TILE * j, TILE * j + TILE)
        gp = (dot_nt(g, wfin[t, :]) * dhid[:, t].astype(f32)).astype(bf)
        gpat = gpat + dot_nt(gp, wi[:, t])
        v = dot(pt, gp)
        for i in range(3):
            c = 3 * j + i
            tmp[32 * c:32 * c + 32, :] = v[:, 128 * i:128 * i + 128]
        row = rows_of(tmp, row, jnp.sum(gp.astype(f32), axis=0, keepdims=True))
        put_matrix(scrs, mes, where, "final", j, dot_tn(hid[:, t], g))
    v = dot(pt, g)
    for i in range(3):
        tmp[384 + 32 * i:416 + 32 * i, :] = v[:, 128 * i:128 * i + 128]
    row = rows_of(tmp, row, jnp.sum(g.astype(f32), axis=0, keepdims=True))
    rows_of(tmp, row, gain_one[...])
    p, at = where["small", 0]
    for b in range(32):
        scrs[p][b ^ mes[p], at:at + 16, :] = tmp[16 * b:16 * b + 16].astype(bf)
    ship([((earlier if item[0] in ("attention", "merge") else scrs)[where[item][0]], where[item][1],
           SLAB_ROWS.get(item[0], 48)) for _, items in TOKEN_PARTS for item in items], keep, send)
    gpatches[...] = gpat


def forecast_kernel(count, patch, *refs):
    samples, mask, gpatches, hid, states, sigma_row, center_row = refs[:7]
    refs = refs[7:]
    mats, refs = refs[:count], refs[count:]
    short, refs = refs[:count], refs[count:]
    offsets, refs = refs[:count], refs[count:]
    cots, refs = refs[:count], refs[count:]
    preds, series_grad = refs[:count], refs[count]
    sg = sigma_row[...]
    ct = center_row[...]
    st = states[...]
    ones = jnp.ones((1, 128), bf)
    row_c, row_s = 0.0, 0.0
    for r in range(count):
        added_bias = dot_tn(offsets[r][...].astype(f32)[None, :].astype(bf), ones)[:, :1]
        raw = dot_nt(mats[r][...], hid[...]) + dot_nt(short[r][...], st) + added_bias
        preds[r][...] = (raw * sg + ct).astype(preds[r].dtype)
        c = cots[r][...].astype(f32)
        row_c = row_c + jnp.sum(c, axis=0, keepdims=True)
        row_s = row_s + jnp.sum(c * raw, axis=0, keepdims=True)
    observed = mask[...].astype(f32)
    series = samples.shape[0]
    first, cnt, center, offset, spread, sigma = series_stats(samples[...], observed, patch)
    out_c = series_column(row_c, series)
    out_s = series_column(row_s, series)
    points = samples.shape[1]
    per_series = points // patch
    rows = series * per_series
    lane = iota((2 * patch, points), 1) % patch
    fold = (iota((2 * patch, points), 0) == lane).astype(f32).astype(bf)
    own = (iota((rows, points), 1) // patch == iota((rows, points), 0) % per_series).astype(f32)
    gpat = gpatches[...]
    high = gpat.astype(bf)
    low = (gpat - high.astype(f32)).astype(bf)
    full = (dot(high, fold) + dot(low, fold)) * own
    og = observed * jnp.sum(full.reshape(series, per_series, points), axis=1)
    g_center = out_c - jnp.sum(og, axis=1, keepdims=True) / sigma
    g_sigma = out_s - jnp.sum(og * offset, axis=1, keepdims=True) / (sigma * sigma)
    g_spread = jnp.where(spread > 1.0, g_sigma * 0.5 / sigma, 0.0)
    g_center = g_center - g_spread * 2.0 * jnp.sum(first * offset, axis=1, keepdims=True) / cnt
    series_grad[...] = og / sigma + g_spread * 2.0 * first * offset / cnt + g_center * first / cnt


def place_kernel(count, *refs):
    preds, out = refs[:count], refs[count]
    rows = preds[0].shape[1]
    narrow = lax.axis_index("narrow")
    for r in range(count):
        out[:, pl.ds(pl.multiple_of((narrow ^ r) * rows, 128), rows)] = preds[r][...].astype(f32)


def xor_send(v, mask, total):
    return lax.ppermute(v, AXES, [(i, i ^ mask) for i in range(total)])


def grouped(parts, level):
    groups = {}
    for p, (_, order) in enumerate(parts):
        groups.setdefault(order[level:], []).append(p)
    return list(groups.values())


def places(parts, groups):
    out = {}
    for g, members in enumerate(groups):
        at = 0
        for p in members:
            out[p] = g, at
            at += parts[p][0]
    return out


def combos(bits):
    out = [0]
    for b in bits:
        out = [o + s for o in out for s in (0, b)]
    return out


def starts(counts):
    return [sum(counts[:k]) for k in range(len(counts))]


def swaps(parts, head=False):
    return all(order[-1] in "xypq" for _, order in parts) and not (head and parts[0][1][-1] == "x")


def add_kernel(parts, before, came, after, split, *refs):
    ins, outs = refs[:sum(came)], refs[sum(came):]
    first, to = starts(came), starts(split)
    n = ins[0].shape[0]
    for p, (rows, _) in enumerate(parts):
        (g, a), (o, b) = before[p], after[p]
        step = n // split[o]
        for k in range(n):
            v = ins[first[g]][k, a:a + rows].astype(f32)
            for c in range(1, came[g]):
                v = v + ins[first[g] + c][k, a:a + rows].astype(f32)
            outs[to[o] + k // step][k % step, b:b + rows] = v.astype(bf)


def join_kernel(parts, before, came, after, *refs):
    ins, outs = refs[:sum(came)], refs[sum(came):]
    first = starts(came)
    for p, (rows, _) in enumerate(parts):
        (g, a), (o, b) = before[p], after[p]
        n = ins[first[g]].shape[0]
        for k in range(came[g]):
            outs[o][n * k:n * k + n, b:b + rows] = ins[first[g] + k][:, a:a + rows]


class Flow:
    def __init__(self, chain, total, bits, rest, parts, keep, send, name, head=False):
        self.chain, self.total, self.bits, self.rest, self.parts = chain, total, bits, rest, parts
        self.name, self.head = name, head
        self.swap = swaps(parts, head)
        self.level, self.down = 0, True
        self.groups = [list(range(len(parts)))]
        self.held = [[keep, self.to(send, bits["c"][0])]]

    def to(self, v, mask):
        with jax.named_scope(self.name + str(mask)):
            return xor_send(v, mask, self.total)

    def rows(self, group):
        return sum(self.parts[p][0] for p in group)

    def levels(self, group):
        return len(self.parts[group[0]][1])

    def masks(self, group, gather=False):
        bits = self.bits[self.parts[group[0]][1][self.level]]
        return combos([b for b in bits if not (gather and self.head and b == self.bits["x"][0])])[1:]

    def step(self):
        (self.add if self.down else self.join)()

    def add(self):
        before, came = places(self.parts, self.groups), [len(h) for h in self.held]
        n = self.held[0][0].shape[0]
        last = self.level == self.levels([0])
        if not last:
            self.groups = grouped(self.parts, self.level)
            whole = self.swap and self.level + 1 == self.levels([0])
            split = [1 if whole else 1 + len(self.masks(g)) for g in self.groups]
        else:
            if self.swap:
                self.groups = grouped(self.parts, self.level - 2)
            split = [1] * len(self.groups)
        shapes = [((n // c, self.rows(g), 128), bf) for g, c in zip(self.groups, split) for _ in range(c)]
        outs = self.chain(
            functools.partial(add_kernel, self.parts, before, came, places(self.parts, self.groups), split),
            shapes, [v for h in self.held for v in h], limit=4)
        at = starts(split)
        if not last:
            self.held = [[outs[k]] + [self.to(outs[k if whole else k + 1 + i], m) for i, m in enumerate(self.masks(g))]
                         for g, k in zip(self.groups, at)]
            self.level += 1
            return
        for m in self.rest:
            outs = [v + self.to(v, m) for v in outs]
        self.down = False
        if self.swap:
            self.level -= 1
        self.spread(outs)

    def spread(self, arrays):
        self.level -= 1
        if self.level >= 0 and not self.masks(self.groups[0], True):
            self.level -= 1
        if self.level < 0:
            self.held = [[a, self.to(a, self.bits["c"][0])] for a in arrays]
            return
        self.held = [[a] + [self.to(a, m) for m in self.masks(g, True)] for g, a in zip(self.groups, arrays)]

    def join(self):
        before, came = places(self.parts, self.groups), [len(h) for h in self.held]
        ns = {p: self.held[g][0].shape[0] * came[g] for p, (g, _) in before.items()}
        up = self.level - 1
        self.groups = grouped(self.parts, up) if up >= 0 else [list(range(len(self.parts)))]
        outs = self.chain(
            functools.partial(join_kernel, self.parts, before, came, places(self.parts, self.groups)),
            [((ns[g[0]], self.rows(g), 128), bf) for g in self.groups], [v for h in self.held for v in h], limit=4)
        self.spread(outs)


def assemble(refs, scr):
    k = 0
    for a in refs:
        scr[k:k + a.shape[0]] = a[...]
        k += a.shape[0]


def finder(scr, parts, masks, count):
    where, mes = layout(parts), [me_of(m, count) for m in masks]
    base = [sum(part_rows(items) for _, items in parts[:p]) for p in range(len(parts))]

    def find(name, k, b):
        p, at = where[name, k]
        at += base[p]
        return scr[b ^ mes[p], at:at + SLAB_ROWS.get(name, 48), :].astype(f32)

    return find


def vectors(tmp, row, outs):
    for o in outs:
        n = o.shape[0]
        for j in range(0, n, 128):
            o[pl.ds(j, 128)] = tmp[row]
            row += 1


def unpack_columns(count, masks, here, there, w, skip, bias, scr, tmp):
    me = me_of(masks, count)
    assemble((here, there), scr)
    cols, width = w.shape
    for b in range(width // 128):
        w[:, 128 * b:128 * b + 128] = scr[b ^ me].astype(f32)
    for i in range(skip.shape[1] // 128):
        skip[:, 128 * i:128 * i + 128] = scr[(width // 128 + i) ^ me].astype(f32)
    tmp[...] = scr[15 ^ me].astype(f32)
    bias[...] = jnp.concatenate([tmp[i:i + 1, :] for i in range(-(-cols // 128))], axis=1)[0, :cols]


def unpack_ffn(count, masks, here, there, inner, up, down, bias, gain, scr, tmp):
    assemble((here, there), scr)
    find = finder(scr, FFN_PARTS, masks, count)
    for b in range(32):
        j, i = b // 8, b % 8
        rows = slice(48 * i, 48 * i + 48)
        for k in range(3):
            cols = slice(TILE * j + 128 * k, TILE * j + 128 * k + 128)
            inner[rows, cols] = find("inner", k, b)
            up[rows, cols] = find("up", k, b)
            down[48 * b:48 * b + 48, 128 * k:128 * k + 128] = find("down", k, b)
    tmp[...] = find("vector", 0, 0)
    vectors(tmp, 0, (bias, gain))


def unpack_tokens(count, masks, here, there, gq, gk, gv, wo, out, tin, skip, bin_, bout, gain, scr, tmp):
    assemble((here, there), scr)
    find = finder(scr, TOKEN_PARTS, masks, count)
    for b in range(32):
        j, i = b // 8, b % 8
        tmp[16 * b:16 * b + 16, :] = find("small", 0, b)
        for k in range(3):
            c = TILE * j + 128 * k
            (gq, gk, gv)[c // 512][48 * i:48 * i + 48, c % 512:c % 512 + 128] = find("attention", k, b)
            out[48 * b:48 * b + 48, 128 * k:128 * k + 128] = find("final", k, b)
            wo[16 * b:16 * b + 16, 128 * k:128 * k + 128] = find("merge", k, b)
    for c in range(12):
        tin[:, 128 * c:128 * c + 128] = tmp[32 * c:32 * c + 32, :]
    for i in range(3):
        skip[:, 128 * i:128 * i + 128] = tmp[384 + 32 * i:416 + 32 * i, :]
    vectors(tmp, 480, (bin_, bout, gain))


def per_device(wide, count, signal_samples, present_mask, wi, bi, wfin, wskip, bfin, gain_one, wq, wk, wv, wm,
               gain_two, we, wc, wri, bri, whz, wrs, bro, cotangent):
    series, points = signal_samples.shape
    patch = wi.shape[0] // 2
    rows = series * (points // patch)
    dim, width = wri.shape
    cols = whz.shape[1]
    inner = wq.shape[1]
    total = wide * count
    X, CORE, Y, Z0, Z1 = 1, count, 2 * count, 4 * count, 8 * count
    bits = {"c": [CORE], "x": [X], "y": [Y], "p": [Z0], "q": [Z1], "d": [Y, X], "z": [Z1, Z0]}
    narrow_rest = [1 << i for i in range(1, count.bit_length() - 1)]
    wide_rest = [count << i for i in range(4, wide.bit_length() - 1)]
    def block_bits(parts, head=False):
        out = []
        for _, order in parts:
            own = [CORE] + [b for a in order for b in bits[a] if not (head and b == X)]
            out.append(own[:-1] + [0] if swaps(parts, head) else own)
        return out

    ffn_masks, token_masks = block_bits(sizes(FFN_PARTS)), block_bits(sizes(TOKEN_PARTS))
    (column_masks,) = block_bits([(cols, HEAD_ORDER)], True)
    ffn_rows, token_rows = ([r for r, _ in sizes(parts)] for parts in (FFN_PARTS, TOKEN_PARTS))
    chain = Chain()
    vmem = pltpu.VMEM

    whz_t, wrs_t, cot_t = whz.T, wrs.T, cotangent.T
    prepared = chain(
        functools.partial(prepare_kernel, count, rows),
        [((cols, rows), bf)] * (count - 1)
        + [((cols, rows), f32), ((cols, width // 2), bf)],
        [], raw=[cot_t, whz_t],
        scratch=[vmem((max(count - 1, 1), cols, rows), f32), pltpu.SemaphoreType.DMA((count + 1,))], limit=24)
    own_cot, mine = prepared[count - 1:]
    cots = [own_cot] + [xor_send(prepared[r - 1], r, total) for r in range(1, count)]
    far = [xor_send(mine, r, total) for r in range(1, count)]
    shorts = [wrs_t] + [xor_send(wrs_t, r, total) for r in range(1, count)]
    offsets = [bro] + [xor_send(bro, r, total) for r in range(1, count)]

    weights = [wi, wfin, wskip, wq, wk, wv, wm, we, wc, wri, whz_t]
    out = chain(
        functools.partial(tokens_kernel, patch),
        [((rows, 2 * patch), bf), ((rows, width), bf), ((rows, width), bf), ((rows, dim), f32), ((rows, dim), bf),
         ((rows, 3 * inner), bf), ((1, rows), f32), ((1, rows), f32)] + [(w.shape, bf) for w in weights],
        [signal_samples, present_mask, bi, bfin, gain_one], raw=weights,
        scratch=[pltpu.SemaphoreType.DMA((len(weights),))])
    patches, hid1, d1, embed, normed1, qkv, sigma, center = out[:8]
    wi, wfin, wskip, wq, wk, wv, wm, we, wc, wri, whz_t = out[8:]

    probs, mixed = chain(attend_kernel, [((2 * series, 32, 128), f32), ((rows, inner), bf)], [qkv])
    middle, normed2, hid2, d2, states, hidh, dh = chain(
        ffn_kernel,
        [((rows, dim), f32), ((rows, dim), bf), ((rows, width), bf), ((rows, width), bf), ((rows, dim), bf),
         ((rows, width), bf), ((rows, width), bf)],
        [embed, mixed, wm, gain_two, we, wc, wri, bri])

    groups = max(count // 2, 1)

    def columns():
        out = chain(
            functools.partial(columns_kernel, count, column_masks), [((16, cols, 128), bf)] * (2 * groups),
            [states, hidh, sigma] + cots,
            scratch=[vmem((cols, 128), f32)] + [vmem((32, cols, 128), bf)] * groups, limit=24)
        first = list(out[:2])
        for i in range(1, groups):
            for k in range(2):
                first[k] = first[k] + xor_send(out[2 * i + k], 2 * i, total)
        return Flow(chain, total, bits, wide_rest, [(cols, HEAD_ORDER)], *first, "columns", head=True)

    def gate():
        out = []
        for v in far:
            (v,) = chain(gate_kernel, [(v.shape, bf)], [v], limit=4)
            out += [v, xor_send(v, CORE, total)]
        return out

    def head():
        out = chain(
            functools.partial(head_kernel, count),
            [((rows, width), bf), ((1, width), f32)] + [((rows, cols), bf)] * count
            + [((cols, width), bf)] * (count - 1),
            [dh, sigma] + cots + [whz_t] + far_both)
        return out[0], out[1], out[2:2 + count], [whz_t] + out[2 + count:]

    def ffn_back():
        gmiddle, keep, send = chain(
            functools.partial(ffn_back_kernel, count, ffn_masks),
            [((rows, dim), bf)] + [((16, sum(ffn_rows), 128), bf)] * 2,
            [states, gpre, sums, wri, hid2, d2, normed2, middle, wc, we, gain_two] + gs + shorts,
            scratch=[vmem((32, n, 128), bf) for n in ffn_rows] + [vmem((16, 128), f32)])
        return gmiddle, Flow(chain, total, bits, narrow_rest + wide_rest, sizes(FFN_PARTS), keep, send, "ffn")

    def attend_back():
        return chain(attend_back_kernel, [((rows, 3 * inner), bf)], [gmiddle, wm, qkv, probs],
                     scratch=[vmem((rows, inner), bf), vmem(probs.shape, f32), vmem(probs.shape, bf)])[0]

    def project_back():
        return chain(
            functools.partial(project_back_kernel, count, token_masks),
            [((rows, dim), bf), ((1, dim), f32)] + [((32, n, 128), bf) for n in token_rows],
            [gqkv, gmiddle, mixed, normed1, embed, wq, wk, wv, gain_one])

    def tokens_back():
        gpatches, keep, send = chain(
            functools.partial(tokens_back_kernel, count, token_masks, patch),
            [((rows, 2 * patch), f32)] + [((16, sum(token_rows), 128), bf)] * 2,
            [gembed, hid1, d1, patches, wfin, wskip, wi, gg1] + earlier,
            scratch=[vmem((32, n, 128), bf) for n in token_rows] + [vmem((512, 128), f32)])
        return gpatches, Flow(chain, total, bits, narrow_rest + wide_rest, sizes(TOKEN_PARTS), keep, send, "tokens")

    def forecast():
        out = chain(
            functools.partial(forecast_kernel, count, patch),
            [((cols, rows), f32)] + [((cols, rows), bf)] * (count - 1) + [((series, points), f32)],
            [signal_samples, present_mask, gpatches, hidh, states, sigma, center] + mats + shorts + offsets + cots)
        return [out[0]] + [xor_send(out[r], r, total) for r in range(1, count)], out[count]

    def place():
        return chain(functools.partial(place_kernel, count), [((cols, count * rows), f32)], preds)[0]

    def finish_columns():
        return chain(functools.partial(unpack_columns, count, column_masks),
                     [((cols, width), f32), ((cols, dim), f32), ((cols,), f32)],
                     one.held[0], scratch=[vmem((16, cols, 128), bf), vmem((cols, 128), f32)], limit=24)

    def finish_ffn():
        return chain(functools.partial(unpack_ffn, count, ffn_masks),
                     [((dim, width), f32)] * 2 + [((width, dim), f32), ((width,), f32), ((dim,), f32)], two.held[0],
                     scratch=[vmem((32, sum(ffn_rows), 128), bf), vmem((16, 128), f32)], limit=24)

    def finish_tokens():
        return chain(
            functools.partial(unpack_tokens, count, token_masks),
            [((dim, inner), f32)] * 3 + [((inner, dim), f32), ((width, dim), f32), ((2 * patch, width), f32),
                                         ((2 * patch, dim), f32), ((width,), f32), ((dim,), f32), ((dim,), f32)],
            three.held[0], scratch=[vmem((32, sum(token_rows), 128), bf), vmem((512, 128), f32)], limit=24)

    far_both = gate()
    one = columns()
    gpre, sums, gs, mats = head()
    gmiddle, two = ffn_back()
    gqkv = attend_back()
    gembed, gg1, *earlier = project_back()
    two.step()
    gpatches, three = tokens_back()
    one.step()
    three.step()
    two.step()
    three.step()
    one.step()
    three.step()
    preds, g_series = forecast()
    two.step()
    three.step()
    one.step()
    two.step()
    prediction = place()
    three.step()
    one.step()
    two.step()
    three.step()
    two.step()
    one.step()
    three.step()
    two.step()
    one.step()
    three.step()
    two.step()
    one.step()
    tokens_out = finish_tokens()
    ffn_out = finish_ffn()
    columns_out = finish_columns()
    g_hw, g_hs, g_hb = columns_out
    g_hiw, g_up, g_down, g_hib, g_g2 = ffn_out
    g_q, g_k, g_v, g_wo, g_to, g_ti, g_ts, g_tib, g_tob, g_g1 = tokens_out
    return (prediction.T, g_series, g_ti, g_tib, g_to, g_ts, g_tob, g_g1, g_q, g_k, g_v, g_wo, g_g2, g_up, g_down,
            g_hiw, g_hib, g_hw.T, g_hs.T, g_hb)


def solution(mesh):
    wide, count = mesh.shape["wide"], mesh.shape["narrow"]
    both = P(("wide", "narrow"), None)
    return jax.shard_map(
        functools.partial(per_device, wide, count),
        mesh=mesh,
        in_specs=(both, both) + (P(),) * 15 + (P(None, "narrow"), P(None, "narrow"), P("narrow"), P("wide", "narrow")),
        out_specs=(P("wide", "narrow"), both) + (P(),) * 15
        + (P(None, "narrow"), P(None, "narrow"), P("narrow")),
        check_vma=False,
    )
```
